32 devices in a mesh: groups: 2 (over y), dp: 4 (over z), tensor: 4 (over x, core).
Axes of the slice: x: 2, y: 2, z: 4, core: 2. Of those that a mesh axis runs over, the one named last changes fastest.
Arguments:
- normed_input: bfloat16 [4096, 8192], P(('groups', 'dp'), 'tensor'), parts along dimension 0, may hold values from -6 to 6
- rotated_queries: bfloat16 [4096, 8192], P(('groups', 'dp'), 'tensor'), parts along dimension 0, may hold values from -6 to 6
- rotated_keys: bfloat16 [4096, 1024], P(('groups', 'dp'), 'tensor'), parts along dimension 0, may hold values from -6 to 6
- value_rows: bfloat16 [4096, 1024], P(('groups', 'dp'), 'tensor'), parts along dimension 0, may hold values from -6 to 6
- output_gradient: bfloat16 [4096, 8192], P(('groups', 'dp'), 'tensor'), parts along dimension 0, may hold values from -6 to 6
- document_length: int32 [8, 8], P(('groups', 'dp')), parts along dimension 0, may hold values from 1 to 256, 512 in all within a row
- document_adapter: int32 [8, 8], P(('groups', 'dp')), parts along dimension 0, may hold values from 0 to 3
- adapter_in_slot: int32 [4], replicated, may hold values from 0 to 3, each once
- down_weight: bfloat16 [8, 16, 8192], P(('groups', 'dp'), None, 'tensor'), parts along dimension 0, may hold values from -0.0625 to 0.0625
- up_weight: bfloat16 [8, 16, 8192], P(('groups', 'dp'), None, 'tensor'), parts along dimension 0, may hold values from -0.0625 to 0.0625
Outputs:
- input_gradient: bfloat16 [4096, 8192], P(('groups', 'dp'), 'tensor'), parts along dimension 0
- key_gradient: bfloat16 [4096, 1024], P(('groups', 'dp'), 'tensor'), parts along dimension 0
- value_gradient: bfloat16 [4096, 1024], P(('groups', 'dp'), 'tensor'), parts along dimension 0
- down_gradient: float32 [8, 16, 8192], P(('groups', 'dp'), None, 'tensor'), parts along dimension 0
- up_gradient: float32 [8, 16, 8192], P(('groups', 'dp'), None, 'tensor'), parts along dimension 0
The draws below stay inside these ranges and needn't reach their ends.
There are 2 independent parts, one for each index of `groups`. The reference program is written for one: setup_inputs(seed, part) draws one part's arguments, and reference() takes and returns one part's arrays. A program takes and returns all parts, laid end to end along the dimension named above; an argument that names none is the same for every part. Nothing has to cross between parts.
Inputs may be any that keep to these rules, and one draw needn't show every extreme that they name: `document_length`: each row sums to 512. `adapter_in_slot`: each adapter once.
All inputs are finite; a program needn't handle non-finite values.
Results may differ from the reference program's by a relative error of at most 0.012.
The reference program's roundings to bfloat16 on the way count: a program that leaves them out, or rounds other values in their place, can miss the bound.
Values may be sent and summed in bfloat16 or wider, within the bound.
No kernel may reach another device: no remote copies, remote signals or barrier semaphores. Data moves between devices by JAX's collectives and lax.ppermute only.
A program may use at most 64 MiB of HBM per device.

```python
import math
import jax
import jax.numpy as jnp
import numpy as np
from jax import lax

MODEL_WIDTH = 8192
QUERY_HEAD_COUNT = 64
KEY_VALUE_HEADS = 8
HEAD_SIZE = 128
ADAPTER_RANK = 16
SEGS = 8
SHARD_TOKENS = 512
ADAPTER_TOTAL = 4
TOKEN_TOTAL = 2048
N_DP = 4


def draw_rotated_queries(key, part):
    key = jax.random.fold_in(key, 11)
    base_offset = jax.random.truncated_normal(key, -6.0, 6.0, (TOKEN_TOTAL, QUERY_HEAD_COUNT * HEAD_SIZE), jnp.float32)
    return base_offset.astype(jnp.bfloat16)


def draw_rotated_keys(key, part):
    key = jax.random.fold_in(key, 13)
    base_offset = jax.random.truncated_normal(key, -6.0, 6.0, (TOKEN_TOTAL, KEY_VALUE_HEADS * HEAD_SIZE), jnp.float32)
    return base_offset.astype(jnp.bfloat16)


def set_ends(drawn, stream_key, smallest, high):
    longest = drawn.shape.index(max(drawn.shape))
    spots = []
    for shift in (0, 1):
        where = [jax.random.randint(jax.random.fold_in(stream_key, axis), (), 0, length) for axis, length in enumerate(drawn.shape)]
        where[longest] = (where[longest] + shift) % drawn.shape[longest]
        spots.append(tuple(where))
    return drawn.at[spots[0]].set(smallest).at[spots[1]].set(high)


def block_levels(rng, dims, pieces, low, high):
    gain, own = 1.0, jax.random.fold_in(rng, 6)
    for dim, parts in pieces:
        heights = jnp.exp(jax.random.uniform(jax.random.fold_in(own, dim), (parts,), jnp.float32, low / len(pieces), high / len(pieces)))
        gain = gain * jnp.repeat(heights, dims[dim] // parts).reshape([-1 if axis == dim else 1 for axis in range(len(dims))])
    return gain


def rank_bounds(count, lean):
    weights = [(1 << 20) // math.isqrt(standing ** lean) + 1 for standing in range(1, count + 1)]
    deviation = 1 + sum(weights) // (1 << 30)
    return np.cumsum(np.array([max(1, weight // deviation) for weight in weights]))


def skewed_ids(rng, extent, count, skew):
    table = rank_bounds(count, skew)
    ticket = jax.random.randint(jax.random.fold_in(rng, 1), extent, 0, int(table[count - 1]))
    standing = jnp.searchsorted(jnp.asarray(table, jnp.int32), ticket, side="right")
    return jax.random.permutation(jax.random.fold_in(rng, 2), count)[standing].astype(jnp.int32)


def length_profile(amount, total, most, slope):
    portions = [(1 << 20) // math.isqrt(grade ** slope) + 1 for grade in range(2, amount + 1)]
    surplus, counts = total - most - (amount - 1), [1] * (amount - 1)
    while surplus > 0:
        movable = [i for i in range(amount - 1) if counts[i] < most]
        pool, remaining = sum([portions[i] for i in movable]), surplus
        for i in movable:
            more = min(most - counts[i], max(1, remaining * portions[i] // pool), surplus)
            counts[i] = counts[i] + more
            surplus = surplus - more
    return np.array([most] + counts)


def ragged(key, amount, total, reach, skew):
    if amount == 2:
        one = jax.random.randint(key, (), max(1, total - reach), min(reach, total - 1) + 1)
        return jnp.stack([one, total - one])
    tallies = jnp.asarray(length_profile(amount, total, reach, skew), jnp.int32)
    pairs = (amount - 1) // 2
    donor, taker = tallies[1:1 + 2 * pairs:2], tallies[2:2 + 2 * pairs:2]
    slack = jnp.minimum(donor - 1, reach - taker)
    shifted = jax.random.randint(jax.random.fold_in(key, 1), (pairs,), 0, 1 << 20) % (slack + 1)
    tallies = tallies.at[1:1 + 2 * pairs:2].set(donor - shifted).at[2:2 + 2 * pairs:2].set(taker + shifted)
    return tallies[jax.random.permutation(jax.random.fold_in(key, 2), amount)]


def noise(rng, dims, deviation, reach, cuts=(), held_as=jnp.bfloat16):
    array = deviation * jax.random.normal(rng, dims, jnp.float32)
    if cuts:
        array = array * block_levels(rng, dims, cuts, -0.22, 0.18)
    return jnp.clip(array, -reach, reach).astype(held_as)


def setup_inputs(seed: int = 0, part: int = 0) -> dict:
    splits = jax.random.split(jax.random.key(seed), 11)
    part_keys = jax.random.split(jax.random.fold_in(splits[10], part), 11)
    normed_input = noise(part_keys[0], (TOKEN_TOTAL, MODEL_WIDTH), 1.0, 6.0, ((0, 4), (1, 4)))
    rotated_queries = draw_rotated_queries(jax.random.fold_in(jax.random.fold_in(splits[10], part), 71), part)
    rotated_keys = draw_rotated_keys(jax.random.fold_in(jax.random.fold_in(splits[10], part), 71), part)
    value_rows = noise(part_keys[3], (TOKEN_TOTAL, KEY_VALUE_HEADS * HEAD_SIZE), 1.0, 6.0, ((0, 4), (1, 4)))
    output_gradient = noise(part_keys[4], (TOKEN_TOTAL, QUERY_HEAD_COUNT * HEAD_SIZE), 1.0, 6.0, ((0, 4), (1, 4)))
    document_length = jax.vmap(lambda own: ragged(own, SEGS, SHARD_TOKENS, SHARD_TOKENS // 2, 2))(jax.random.split(part_keys[5], N_DP)).reshape((N_DP, SEGS)).astype(jnp.int32)
    document_adapter = set_ends(skewed_ids(part_keys[6], (N_DP, SEGS), ADAPTER_TOTAL, 2), jax.random.fold_in(part_keys[6], 3), 0, ADAPTER_TOTAL - 1).astype(jnp.int32)
    adapter_in_slot = jax.random.permutation(splits[7], ADAPTER_TOTAL).astype(jnp.int32)
    down_weight = noise(part_keys[8], (ADAPTER_TOTAL, ADAPTER_RANK, MODEL_WIDTH), MODEL_WIDTH ** -0.5, 0.0625, ((0, 4), (2, 4)))
    up_weight = noise(part_keys[9], (ADAPTER_TOTAL, ADAPTER_RANK, QUERY_HEAD_COUNT * HEAD_SIZE), MODEL_WIDTH ** -0.5, 0.0625, ((0, 4), (2, 4)))
    return dict(normed_input=normed_input, rotated_queries=rotated_queries, rotated_keys=rotated_keys, value_rows=value_rows, output_gradient=output_gradient, document_length=document_length, document_adapter=document_adapter, adapter_in_slot=adapter_in_slot, down_weight=down_weight, up_weight=up_weight)


MASKED = -1e+30
ADAPTER_SCALE = 2.0

def document_layout(lengths, adapters, row_count):
    position = jnp.arange(row_count, dtype=jnp.int32)
    ends = jnp.cumsum(lengths).astype(jnp.int32)
    starts = ends - lengths
    inside = ((position[:, None] >= starts[None, :]) & (position[:, None] < ends[None, :])).astype(jnp.int32)
    document = lax.optimization_barrier(jnp.sum(inside * jnp.arange(lengths.shape[0], dtype=jnp.int32)[None, :], axis=1))
    adapter = lax.optimization_barrier(jnp.sum(inside * adapters[None, :], axis=1))
    allowed = (document[:, None] == document[None, :]) & (position[None, :] <= position[:, None])
    return (allowed, adapter)

def head_backward(query_head, key_head, value_head, grad_head, allowed, score_scale):
    scores = lax.dot_general(query_head, key_head, (((1,), (1,)), ((), ())), preferred_element_type=jnp.float32) * score_scale
    scores = jnp.where(allowed, scores, MASKED)
    largest = lax.optimization_barrier(jnp.max(scores, axis=1, keepdims=True))
    numerator = jnp.where(allowed, jnp.exp(scores - largest), 0.0)
    weights = numerator / lax.optimization_barrier(jnp.sum(numerator, axis=1, keepdims=True))
    rounded = weights.astype(jnp.bfloat16)
    attended = jnp.dot(rounded, value_head, preferred_element_type=jnp.float32)
    row_delta = lax.optimization_barrier(jnp.sum(grad_head.astype(jnp.float32) * attended, axis=1, keepdims=True))
    grad_value = lax.dot_general(rounded, grad_head, (((0,), (0,)), ((), ())), preferred_element_type=jnp.float32)
    grad_weights = lax.dot_general(grad_head, value_head, (((1,), (1,)), ((), ())), preferred_element_type=jnp.float32)
    grad_scores = (weights * (grad_weights - row_delta)).astype(jnp.bfloat16)
    grad_query = (jnp.dot(grad_scores, key_head, preferred_element_type=jnp.float32) * score_scale).astype(jnp.bfloat16)
    grad_key = lax.dot_general(grad_scores, query_head, (((0,), (0,)), ((), ())), preferred_element_type=jnp.float32) * score_scale
    return (grad_query, grad_key, grad_value)

def attention_backward(rotated_queries, rotated_keys, value_rows, output_gradient, allowed):
    row_count = rotated_queries.shape[0]
    head_total = rotated_queries.shape[1] // HEAD_SIZE
    kv_total = rotated_keys.shape[1] // HEAD_SIZE
    group_share = QUERY_HEAD_COUNT // KEY_VALUE_HEADS
    score_scale = 1.0 / math.sqrt(HEAD_SIZE)
    query_heads = rotated_queries.reshape(row_count, head_total, HEAD_SIZE).transpose(1, 0, 2)
    grad_heads = output_gradient.reshape(row_count, head_total, HEAD_SIZE).transpose(1, 0, 2)
    key_heads = rotated_keys.reshape(row_count, kv_total, HEAD_SIZE).transpose(1, 0, 2)
    value_heads = value_rows.reshape(row_count, kv_total, HEAD_SIZE).transpose(1, 0, 2)
    kv_index = jnp.arange(head_total, dtype=jnp.int32) // group_share

    def one_head(items):
        query_head, grad_head, index = items
        return head_backward(query_head, key_heads[index], value_heads[index], grad_head, allowed, score_scale)
    grad_query, grad_key, grad_value = lax.map(one_head, (query_heads, grad_heads, kv_index))
    grad_query = grad_query.transpose(1, 0, 2).reshape(row_count, head_total * HEAD_SIZE)
    grad_key = lax.optimization_barrier(jnp.sum(grad_key.reshape(kv_total, group_share, row_count, HEAD_SIZE), axis=1)).astype(jnp.bfloat16)
    grad_value = lax.optimization_barrier(jnp.sum(grad_value.reshape(kv_total, group_share, row_count, HEAD_SIZE), axis=1)).astype(jnp.bfloat16)
    grad_key = grad_key.transpose(1, 0, 2).reshape(row_count, kv_total * HEAD_SIZE)
    grad_value = grad_value.transpose(1, 0, 2).reshape(row_count, kv_total * HEAD_SIZE)
    return (grad_query, grad_key, grad_value)

def reference(normed_input, rotated_queries, rotated_keys, value_rows, output_gradient, document_length, document_adapter, adapter_in_slot, down_weight, up_weight):

    def shard_effort(items):
        query_part, key_part, value_part, grad_part, lengths, adapters = items
        allowed, adapter = document_layout(lengths, adapters, SHARD_TOKENS)
        grad_query, grad_key, grad_value = attention_backward(query_part, key_part, value_part, grad_part, allowed)
        return (grad_query, grad_key, grad_value, adapter)
    query_gradient, key_gradient, value_gradient, adapter_of_token = lax.map(shard_effort, (rotated_queries.reshape(N_DP, SHARD_TOKENS, QUERY_HEAD_COUNT * HEAD_SIZE), rotated_keys.reshape(N_DP, SHARD_TOKENS, KEY_VALUE_HEADS * HEAD_SIZE), value_rows.reshape(N_DP, SHARD_TOKENS, KEY_VALUE_HEADS * HEAD_SIZE), output_gradient.reshape(N_DP, SHARD_TOKENS, QUERY_HEAD_COUNT * HEAD_SIZE), document_length, document_adapter))
    query_gradient = query_gradient.reshape(TOKEN_TOTAL, QUERY_HEAD_COUNT * HEAD_SIZE)
    key_gradient = key_gradient.reshape(TOKEN_TOTAL, KEY_VALUE_HEADS * HEAD_SIZE)
    value_gradient = value_gradient.reshape(TOKEN_TOTAL, KEY_VALUE_HEADS * HEAD_SIZE)
    adapter_of_token = adapter_of_token.reshape(TOKEN_TOTAL)
    onehot = (adapter_in_slot[None, :] == adapter_of_token[:, None]).astype(jnp.float32)
    down_matrix = down_weight.reshape(ADAPTER_TOTAL * ADAPTER_RANK, MODEL_WIDTH)
    up_matrix = up_weight.reshape(ADAPTER_TOTAL * ADAPTER_RANK, QUERY_HEAD_COUNT * HEAD_SIZE)
    input_all = lax.dot_general(normed_input, down_matrix, (((1,), (1,)), ((), ())), preferred_element_type=jnp.float32)
    low_inputs = lax.optimization_barrier(jnp.sum(input_all.reshape(TOKEN_TOTAL, ADAPTER_TOTAL, ADAPTER_RANK) * onehot[:, :, None], axis=1))
    grad_all = lax.dot_general(query_gradient, up_matrix, (((1,), (1,)), ((), ())), preferred_element_type=jnp.float32)
    low_grads = lax.optimization_barrier(jnp.sum(grad_all.reshape(TOKEN_TOTAL, ADAPTER_TOTAL, ADAPTER_RANK) * onehot[:, :, None], axis=1))
    input_wide_rows = (onehot[:, :, None] * low_inputs.astype(jnp.bfloat16).astype(jnp.float32)[:, None, :]).reshape(TOKEN_TOTAL, ADAPTER_TOTAL * ADAPTER_RANK).astype(jnp.bfloat16)
    gradient_wide_rows = (onehot[:, :, None] * low_grads.astype(jnp.bfloat16).astype(jnp.float32)[:, None, :]).reshape(TOKEN_TOTAL, ADAPTER_TOTAL * ADAPTER_RANK).astype(jnp.bfloat16)
    input_gradient = (ADAPTER_SCALE * jnp.dot(gradient_wide_rows, down_matrix, preferred_element_type=jnp.float32)).astype(jnp.bfloat16)
    down_gradient = ADAPTER_SCALE * lax.dot_general(gradient_wide_rows, normed_input, (((0,), (0,)), ((), ())), preferred_element_type=jnp.float32)
    up_gradient = ADAPTER_SCALE * lax.dot_general(input_wide_rows, query_gradient, (((0,), (0,)), ((), ())), preferred_element_type=jnp.float32)
    return (input_gradient, key_gradient, value_gradient, down_gradient.reshape(ADAPTER_TOTAL, ADAPTER_RANK, MODEL_WIDTH), up_gradient.reshape(ADAPTER_TOTAL, ADAPTER_RANK, QUERY_HEAD_COUNT * HEAD_SIZE))
```

```python
import functools
import math

import jax
import jax.numpy as jnp
from jax import lax
from jax.experimental import pallas as pl
from jax.experimental.pallas import tpu as pltpu
from jax.sharding import PartitionSpec as P

QUERY_HEAD_COUNT = 64
KEY_VALUE_HEADS = 8
HEAD_SIZE = 128
GROUP_SHARE = QUERY_HEAD_COUNT // KEY_VALUE_HEADS
DOCUMENT_REACH = 256
BLOCK = 128

MASKED = -1e30
ADAPTER_SCALE = 2.0
LOG2_E = 1.4426950408889634
VMEM_BYTES = 40 * 1024 * 1024

NN = (((1,), (0,)), ((), ()))
NT = (((1,), (1,)), ((), ()))
TN = (((0,), (0,)), ((), ()))


def mxu(a, b, dims):
    return lax.dot_general(a, b, dims, preferred_element_type=jnp.float32)


def query_spans(row_count):
    return [
        (at, max(0, (at - (DOCUMENT_REACH - 1)) // BLOCK * BLOCK), at + BLOCK)
        for at in range(0, row_count, BLOCK)
    ]


def attention_kernel(
    len_ref, q_ref, g_ref, k_ref, v_ref, gq_ref, gk_ref, gv_ref, bias_ref
):
    row_count = q_ref.shape[0]
    scale = 1.0 / math.sqrt(HEAD_SIZE)

    @pl.when(pl.program_id(0) == 0)
    def _():
        at = 0
        for first, low, high in query_spans(row_count):
            width = high - low
            query = lax.broadcasted_iota(jnp.int32, (1, BLOCK), 1) + first
            start = jnp.zeros((1, BLOCK), jnp.int32)
            end = jnp.int32(0)
            for index in range(len_ref.shape[1] - 1):
                end = end + len_ref[0, index]
                start = jnp.where(query >= end, end, start)
            key = lax.broadcasted_iota(jnp.int32, (width, BLOCK), 0) + low
            bias_ref[at : at + width, :] = jnp.where((key >= start) & (key <= query), 0.0, MASKED)
            at += width

    heads = [slice(h * HEAD_SIZE, (h + 1) * HEAD_SIZE) for h in range(GROUP_SHARE)]
    key_t = k_ref[...].T
    grad_key = [None] * (row_count // BLOCK)
    grad_value = [None] * (row_count // BLOCK)
    at = 0
    for first, low, high in query_spans(row_count):
        width = high - low
        rows = slice(first, first + BLOCK)
        query = jnp.concatenate([q_ref[rows, head] for head in heads], axis=0)
        grad = jnp.concatenate([g_ref[rows, head] for head in heads], axis=0)
        scores = mxu(k_ref[low:high, :], query, NT)
        grad_weights = mxu(v_ref[low:high, :], grad, NT)
        bias = bias_ref[at : at + width, :]
        at += width
        scores = scores * (scale * LOG2_E) + jnp.concatenate([bias] * GROUP_SHARE, axis=1)
        largest = jnp.max(scores, axis=0, keepdims=True)
        numerator = jnp.exp2(scores - largest)
        weights = numerator * (1.0 / jnp.sum(numerator, axis=0, keepdims=True))
        rounded = weights.astype(jnp.bfloat16)
        delta = jnp.sum(rounded.astype(jnp.float32) * grad_weights, axis=0, keepdims=True)
        grad_scores = (weights * (grad_weights - delta)).astype(jnp.bfloat16)
        value_terms = mxu(rounded, grad, NN)
        key_terms = mxu(grad_scores, query, NN)
        for block in range(low // BLOCK, high // BLOCK):
            part = slice(block * BLOCK - low, (block + 1) * BLOCK - low)
            for total, terms in ((grad_value, value_terms), (grad_key, key_terms)):
                total[block] = (
                    terms[part] if total[block] is None else total[block] + terms[part]
                )
        grad_query = (mxu(key_t[:, low:high], grad_scores, NN) * scale).astype(jnp.bfloat16)
        for h, head in enumerate(heads):
            gq_ref[head, rows] = grad_query[:, h * BLOCK : (h + 1) * BLOCK]
    for block in range(row_count // BLOCK):
        rows = slice(block * BLOCK, (block + 1) * BLOCK)
        gk_ref[rows, :] = (grad_key[block] * scale).astype(jnp.bfloat16)
        gv_ref[rows, :] = grad_value[block].astype(jnp.bfloat16)


def attention_backward(queries, keys, values, output_gradient, lengths):
    row_count = queries.shape[0]
    wide = GROUP_SHARE * HEAD_SIZE
    pair_rows = sum(high - low for _, low, high in query_spans(row_count))
    by_columns = lambda width: pl.BlockSpec((row_count, width), lambda j: (0, j))
    return pl.pallas_call(
        attention_kernel,
        grid=(keys.shape[1] // HEAD_SIZE,),
        in_specs=[
            pl.BlockSpec(memory_space=pltpu.SMEM),
            by_columns(wide),
            by_columns(wide),
            by_columns(HEAD_SIZE),
            by_columns(HEAD_SIZE),
        ],
        out_specs=[
            pl.BlockSpec((wide, row_count), lambda j: (j, 0)),
            by_columns(HEAD_SIZE),
            by_columns(HEAD_SIZE),
        ],
        out_shape=[
            jax.ShapeDtypeStruct((queries.shape[1], row_count), jnp.bfloat16),
            jax.ShapeDtypeStruct(keys.shape, jnp.bfloat16),
            jax.ShapeDtypeStruct(values.shape, jnp.bfloat16),
        ],
        scratch_shapes=[pltpu.VMEM((pair_rows, BLOCK), jnp.float32)],
        compiler_params=pltpu.CompilerParams(vmem_limit_bytes=VMEM_BYTES),
        cost_estimate=pl.CostEstimate(
            flops=16 * 10**9, bytes_accessed=8 * 2**20, transcendentals=0
        ),
        name="attention_backward",
    )(lengths, queries, output_gradient, keys, values)


def slot_masks(len_ref, adapter_ref, slot_ref, row_count, slots):
    token = lax.broadcasted_iota(jnp.int32, (1, row_count), 1)
    adapter = jnp.full((1, row_count), adapter_ref[0, 0], jnp.int32)
    end = jnp.int32(0)
    for index in range(len_ref.shape[1] - 1):
        end = end + len_ref[0, index]
        adapter = jnp.where(token >= end, adapter_ref[0, index + 1], adapter)
    return [adapter == slot_ref[slot] for slot in slots]


def peer_slots(me, peers, local_slots, sign):
    return [
        lax.rem(me + sign * shift + peers, peers) * local_slots + own
        for shift in range(peers)
        for own in range(local_slots)
    ]


def select(wide, masks, rank):
    total = None
    for index, mask in enumerate(masks):
        part = jnp.where(mask, wide[index * rank : (index + 1) * rank], 0.0)
        total = part if total is None else total + part
    return total


def low_kernel(peers, local_slots, len_ref, adapter_ref, slot_ref, me_ref, x_ref, gq_ref, *refs):
    factors, out_ref = refs[:peers], refs[peers]
    rank = factors[0].shape[0] // (2 * local_slots)
    share = rank * local_slots
    row_count = x_ref.shape[0]
    masks = slot_masks(
        len_ref, adapter_ref, slot_ref, row_count, peer_slots(me_ref[0], peers, local_slots, -1)
    )
    down = jnp.concatenate([ref[:share] for ref in factors], axis=0)
    up = jnp.concatenate([ref[share:] for ref in factors], axis=0)
    out_ref[:rank] = select(mxu(down, x_ref[...], NT), masks, rank)
    out_ref[rank:] = select(mxu(up, gq_ref[...], NN), masks, rank)


def spread(low, masks):
    zero = jnp.zeros_like(low)
    return jnp.concatenate([jnp.where(mask, low, zero) for mask in masks], axis=0).astype(
        jnp.bfloat16
    )


def product_kernel(peers, local_slots, parts, len_ref, adapter_ref, slot_ref, me_ref, *refs):
    lows, (x_ref, gq_ref), outs = refs[:parts], refs[parts : parts + 2], refs[parts + 2 :]
    low = lows[0][...]
    for ref in lows[1:]:
        low = low + ref[...]
    rank = low.shape[0] // 2
    share = rank * local_slots
    low = low.astype(jnp.bfloat16).astype(jnp.float32)
    masks = slot_masks(
        len_ref,
        adapter_ref,
        slot_ref,
        x_ref.shape[0],
        peer_slots(me_ref[0], peers, local_slots, 1),
    )
    wide_in, wide_grad = spread(low[:rank], masks), spread(low[rank:], masks)
    down = mxu(wide_grad, x_ref[...], NN) * ADAPTER_SCALE
    up = mxu(wide_in, gq_ref[...], NT) * ADAPTER_SCALE
    for shift, ref in enumerate(outs[:peers]):
        rows = slice(shift * share, (shift + 1) * share)
        ref[:share] = down[rows].astype(ref.dtype)
        ref[share:] = up[rows].astype(ref.dtype)
    outs[peers][...] = low[rank:].astype(jnp.bfloat16)


def input_kernel(peers, local_slots, len_ref, adapter_ref, slot_ref, me_ref, low_ref, *refs):
    factors, out_ref = refs[:peers], refs[peers]
    rank = low_ref.shape[0]
    masks = slot_masks(
        len_ref,
        adapter_ref,
        slot_ref,
        low_ref.shape[1],
        peer_slots(me_ref[0], peers, local_slots, -1),
    )
    wide = spread(low_ref[...].astype(jnp.float32), masks)
    down = jnp.concatenate([ref[: rank * local_slots] for ref in factors], axis=0)
    out_ref[...] = (mxu(wide, down, TN) * ADAPTER_SCALE).astype(jnp.bfloat16)


def call(kernel, scalars, arrays, out_shape, flops, name):
    return pl.pallas_call(
        kernel,
        in_specs=[pl.BlockSpec(memory_space=pltpu.SMEM)] * len(scalars)
        + [pl.BlockSpec(memory_space=pltpu.VMEM)] * len(arrays),
        out_specs=jax.tree.map(lambda _: pl.BlockSpec(memory_space=pltpu.VMEM), out_shape),
        out_shape=out_shape,
        compiler_params=pltpu.CompilerParams(vmem_limit_bytes=VMEM_BYTES),
        cost_estimate=pl.CostEstimate(flops=flops, bytes_accessed=4 * 2**20, transcendentals=0),
        name=name,
    )(*scalars, *arrays)


def send(array, axis, shift):
    size = lax.axis_size(axis)
    return lax.ppermute(array, axis, [(i, (i + shift) % size) for i in range(size)])


def local(
    normed_input,
    rotated_queries,
    rotated_keys,
    value_rows,
    output_gradient,
    document_length,
    document_adapter,
    adapter_in_slot,
    down_weight,
    up_weight,
):
    row_count, width = normed_input.shape
    local_slots, rank, _ = down_weight.shape
    share = local_slots * rank
    peers, parts = lax.axis_size("dp"), lax.axis_size("tensor")
    me = lax.axis_index("dp").astype(jnp.int32).reshape(1)
    scalars = (document_length, document_adapter, adapter_in_slot, me)
    own = jnp.concatenate(
        [down_weight.reshape(share, width), up_weight.reshape(share, width)], axis=0
    )
    factors = [own] + [send(own, "dp", shift) for shift in range(1, peers)]
    query_gradient, key_gradient, value_gradient = attention_backward(
        rotated_queries, rotated_keys, value_rows, output_gradient, document_length
    )
    low = call(
        functools.partial(low_kernel, peers, local_slots),
        scalars,
        (normed_input, query_gradient, *factors),
        jax.ShapeDtypeStruct((2 * rank, row_count), jnp.float32),
        10**9,
        "low",
    )
    lows = [low] + [send(low, "tensor", shift) for shift in range(1, parts)]
    *terms, low_grads = call(
        functools.partial(product_kernel, peers, local_slots, parts),
        scalars,
        (*lows, normed_input, query_gradient),
        [
            jax.ShapeDtypeStruct((2 * share, width), jnp.float32 if shift == 0 else jnp.bfloat16)
            for shift in range(peers)
        ]
        + [jax.ShapeDtypeStruct((rank, row_count), jnp.bfloat16)],
        10**9,
        "product",
    )
    received = [send(terms[shift], "dp", shift) for shift in range(1, peers)]
    input_gradient = call(
        functools.partial(input_kernel, peers, local_slots),
        scalars,
        (low_grads, *factors),
        jax.ShapeDtypeStruct((row_count, width), jnp.bfloat16),
        10**9,
        "input_gradient",
    )
    total = terms[0]
    for part in received:
        total = total + part.astype(jnp.float32)
    down_gradient = total[:share].reshape(local_slots, rank, width)
    up_gradient = total[share:].reshape(local_slots, rank, width)
    return (input_gradient, key_gradient, value_gradient, down_gradient, up_gradient)


def solution(mesh):
    return jax.shard_map(
        local,
        mesh=mesh,
        in_specs=(
            P(("groups", "dp"), "tensor"),
            P(("groups", "dp"), "tensor"),
            P(("groups", "dp"), "tensor"),
            P(("groups", "dp"), "tensor"),
            P(("groups", "dp"), "tensor"),
            P(("groups", "dp"), None),
            P(("groups", "dp"), None),
            P(),
            P(("groups", "dp"), None, "tensor"),
            P(("groups", "dp"), None, "tensor"),
        ),
        out_specs=(
            P(("groups", "dp"), "tensor"),
            P(("groups", "dp"), "tensor"),
            P(("groups", "dp"), "tensor"),
            P(("groups", "dp"), None, "tensor"),
            P(("groups", "dp"), None, "tensor"),
        ),
        check_vma=False,
    )
```

```python
import functools
import math

import jax
import jax.numpy as jnp
from jax import lax
from jax.experimental import pallas as pl
from jax.experimental.pallas import tpu as pltpu
from jax.sharding import PartitionSpec as P

QUERY_HEAD_COUNT = 64
KEY_VALUE_HEADS = 8
HEAD_SIZE = 128
GROUP_SHARE = QUERY_HEAD_COUNT // KEY_VALUE_HEADS
DOCUMENT_REACH = 256
BLOCK = 128

MASKED = -1e30
ADAPTER_SCALE = 2.0
LOG2_E = 1.4426950408889634
ATTENTION_VMEM = 24 * 1024 * 1024
VMEM_BYTES = 16 * 1024 * 1024

NN = (((1,), (0,)), ((), ()))
NT = (((1,), (1,)), ((), ()))
TN = (((0,), (0,)), ((), ()))


def mxu(a, b, dims):
    return lax.dot_general(a, b, dims, preferred_element_type=jnp.float32)


def query_spans(row_count):
    return [
        (at, max(0, (at - (DOCUMENT_REACH - 1)) // BLOCK * BLOCK), at + BLOCK)
        for at in range(0, row_count, BLOCK)
    ]


def attention_kernel(
    len_ref,
    q_hbm,
    g_hbm,
    k_hbm,
    v_hbm,
    gq_ref,
    gk_ref,
    gv_ref,
    bias_ref,
    q_ref,
    g_ref,
    k_ref,
    v_ref,
    row_sem,
    group_sem,
):
    row_count = q_hbm.shape[0]
    groups = k_hbm.shape[1] // HEAD_SIZE
    wide = GROUP_SHARE * HEAD_SIZE
    scale = 1.0 / math.sqrt(HEAD_SIZE)
    spans = query_spans(row_count)

    def group_copy(which, group):
        source, target = ((k_hbm, k_ref), (v_hbm, v_ref))[which]
        columns = pl.ds(group * HEAD_SIZE, HEAD_SIZE)
        return pltpu.make_async_copy(
            source.at[:, columns], target.at[group], group_sem.at[which, group]
        )

    def row_copy(which, group, block):
        source, target = ((q_hbm, q_ref), (g_hbm, g_ref))[which]
        rows = pl.ds(block * BLOCK, BLOCK)
        return pltpu.make_async_copy(
            source.at[rows, pl.ds(group * wide, wide)],
            target.at[group, rows],
            row_sem.at[which, group, block],
        )

    for group in range(groups):
        group_copy(0, group).start()
        group_copy(1, group).start()
        for block in range(len(spans)):
            row_copy(0, group, block).start()
            row_copy(1, group, block).start()

    at = 0
    for first, low, high in spans:
        width = high - low
        query = lax.broadcasted_iota(jnp.int32, (1, BLOCK), 1) + first
        start = jnp.zeros((1, BLOCK), jnp.int32)
        end = jnp.int32(0)
        for index in range(len_ref.shape[1] - 1):
            end = end + len_ref[0, index]
            start = jnp.where(query >= end, end, start)
        key = lax.broadcasted_iota(jnp.int32, (width, BLOCK), 0) + low
        bias_ref[at : at + width, :] = jnp.where((key >= start) & (key <= query), 0.0, MASKED)
        at += width

    heads = [slice(h * HEAD_SIZE, (h + 1) * HEAD_SIZE) for h in range(GROUP_SHARE)]

    def one_group(group):
        group_copy(0, group).wait()
        group_copy(1, group).wait()
        key_t = k_ref[group].T
        grad_key = [None] * len(spans)
        grad_value = [None] * len(spans)
        at = 0
        for block, (first, low, high) in enumerate(spans):
            width = high - low
            rows = slice(first, first + BLOCK)
            row_copy(0, group, block).wait()
            row_copy(1, group, block).wait()
            query = jnp.concatenate([q_ref[group, rows, head] for head in heads], axis=0)
            grad = jnp.concatenate([g_ref[group, rows, head] for head in heads], axis=0)
            all_scores = mxu(k_ref[group, low:high, :], query, NT)
            all_grad_weights = mxu(v_ref[group, low:high, :], grad, NT)
            bias = bias_ref[at : at + width, :]
            at += width
            rounded, grad_scores = [], []
            for h in range(GROUP_SHARE):
                part = slice(h * BLOCK, (h + 1) * BLOCK)
                scores = all_scores[:, part] * (scale * LOG2_E) + bias
                grad_weights = all_grad_weights[:, part]
                largest = jnp.max(scores, axis=0, keepdims=True)
                numerator = jnp.exp2(scores - largest)
                weights = numerator * (1.0 / jnp.sum(numerator, axis=0, keepdims=True))
                rounded.append(weights.astype(jnp.bfloat16))
                delta = jnp.sum(
                    rounded[-1].astype(jnp.float32) * grad_weights, axis=0, keepdims=True
                )
                grad_scores.append((weights * (grad_weights - delta)).astype(jnp.bfloat16))
            rounded = jnp.concatenate(rounded, axis=1)
            grad_scores = jnp.concatenate(grad_scores, axis=1)
            value_terms = mxu(rounded, grad, NN)
            key_terms = mxu(grad_scores, query, NN)
            for index in range(low // BLOCK, high // BLOCK):
                part = slice(index * BLOCK - low, (index + 1) * BLOCK - low)
                for total, terms in ((grad_value, value_terms), (grad_key, key_terms)):
                    total[index] = (
                        terms[part] if total[index] is None else total[index] + terms[part]
                    )
            grad_query = (mxu(key_t[:, low:high], grad_scores, NN) * scale).astype(jnp.bfloat16)
            for h in range(GROUP_SHARE):
                gq_ref[pl.ds(group * wide + h * HEAD_SIZE, HEAD_SIZE), rows] = grad_query[
                    :, h * BLOCK : (h + 1) * BLOCK
                ]
        columns = pl.ds(group * HEAD_SIZE, HEAD_SIZE)
        for index in range(len(spans)):
            rows = slice(index * BLOCK, (index + 1) * BLOCK)
            gk_ref[rows, columns] = (grad_key[index] * scale).astype(jnp.bfloat16)
            gv_ref[rows, columns] = grad_value[index].astype(jnp.bfloat16)

    for group in range(groups):
        one_group(group)


def attention_backward(queries, keys, values, output_gradient, lengths):
    row_count = queries.shape[0]
    groups = keys.shape[1] // HEAD_SIZE
    blocks = row_count // BLOCK
    pair_rows = sum(high - low for _, low, high in query_spans(row_count))
    wide = (groups, row_count, GROUP_SHARE * HEAD_SIZE)
    narrow = (groups, row_count, HEAD_SIZE)
    arrays = [
        pltpu.with_memory_space_constraint(array, pltpu.HBM)
        for array in (lengths, queries, output_gradient, keys, values)
    ]
    return pl.pallas_call(
        attention_kernel,
        in_specs=[pl.BlockSpec(memory_space=pltpu.SMEM)]
        + [pl.BlockSpec(memory_space=pltpu.HBM)] * 4,
        out_specs=[pl.BlockSpec(memory_space=pltpu.VMEM)] * 3,
        out_shape=[
            jax.ShapeDtypeStruct((queries.shape[1], row_count), jnp.bfloat16),
            jax.ShapeDtypeStruct(keys.shape, jnp.bfloat16),
            jax.ShapeDtypeStruct(values.shape, jnp.bfloat16),
        ],
        scratch_shapes=[
            pltpu.VMEM((pair_rows, BLOCK), jnp.float32),
            pltpu.VMEM(wide, jnp.bfloat16),
            pltpu.VMEM(wide, jnp.bfloat16),
            pltpu.VMEM(narrow, jnp.bfloat16),
            pltpu.VMEM(narrow, jnp.bfloat16),
            pltpu.SemaphoreType.DMA((2, groups, blocks)),
            pltpu.SemaphoreType.DMA((2, groups)),
        ],
        compiler_params=pltpu.CompilerParams(vmem_limit_bytes=ATTENTION_VMEM),
        cost_estimate=pl.CostEstimate(
            flops=8 * 10**9, bytes_accessed=8 * 2**20, transcendentals=0
        ),
        name="attention_backward",
    )(*arrays)


def slot_masks(len_ref, adapter_ref, slot_ref, row_count, slots):
    token = lax.broadcasted_iota(jnp.int32, (1, row_count), 1)
    adapter = jnp.full((1, row_count), adapter_ref[0, 0], jnp.int32)
    end = jnp.int32(0)
    for index in range(len_ref.shape[1] - 1):
        end = end + len_ref[0, index]
        adapter = jnp.where(token >= end, adapter_ref[0, index + 1], adapter)
    return [adapter == slot_ref[slot] for slot in slots]


def peer_slots(me, peers, local_slots, sign):
    return [
        lax.rem(me + sign * shift + peers, peers) * local_slots + own
        for shift in range(peers)
        for own in range(local_slots)
    ]


def select(wide, masks, rank):
    total = None
    for index, mask in enumerate(masks):
        part = jnp.where(mask, wide[index * rank : (index + 1) * rank], 0.0)
        total = part if total is None else total + part
    return total


def low_kernel(peers, local_slots, len_ref, adapter_ref, slot_ref, me_ref, x_ref, gq_ref, *refs):
    factors, out_ref = refs[:peers], refs[peers]
    rank = factors[0].shape[0] // (2 * local_slots)
    share = rank * local_slots
    row_count = x_ref.shape[0]
    masks = slot_masks(
        len_ref, adapter_ref, slot_ref, row_count, peer_slots(me_ref[0], peers, local_slots, -1)
    )
    down = jnp.concatenate([ref[:share] for ref in factors], axis=0)
    up = jnp.concatenate([ref[share:] for ref in factors], axis=0)
    out_ref[:rank] = select(mxu(down, x_ref[...], NT), masks, rank)
    out_ref[rank:] = select(mxu(up, gq_ref[...], NN), masks, rank)


def spread(low, masks):
    zero = jnp.zeros_like(low)
    return jnp.concatenate([jnp.where(mask, low, zero) for mask in masks], axis=0).astype(
        jnp.bfloat16
    )


def product_kernel(peers, local_slots, parts, len_ref, adapter_ref, slot_ref, me_ref, *refs):
    lows, (x_ref, gq_ref), outs = refs[:parts], refs[parts : parts + 2], refs[parts + 2 :]
    low = lows[0][...]
    for ref in lows[1:]:
        low = low + ref[...]
    rank = low.shape[0] // 2
    share = rank * local_slots
    low = low.astype(jnp.bfloat16).astype(jnp.float32)
    masks = slot_masks(
        len_ref,
        adapter_ref,
        slot_ref,
        x_ref.shape[0],
        peer_slots(me_ref[0], peers, local_slots, 1),
    )
    wide_in, wide_grad = spread(low[:rank], masks), spread(low[rank:], masks)
    down = mxu(wide_grad, x_ref[...], NN) * ADAPTER_SCALE
    up = mxu(wide_in, gq_ref[...], NT) * ADAPTER_SCALE
    for shift, ref in enumerate(outs[:peers]):
        rows = slice(shift * share, (shift + 1) * share)
        ref[:share] = down[rows].astype(ref.dtype)
        ref[share:] = up[rows].astype(ref.dtype)
    outs[peers][...] = low[rank:].astype(jnp.bfloat16)


def input_kernel(peers, local_slots, len_ref, adapter_ref, slot_ref, me_ref, low_ref, *refs):
    factors, out_ref = refs[:peers], refs[peers]
    rank = low_ref.shape[0]
    masks = slot_masks(
        len_ref,
        adapter_ref,
        slot_ref,
        low_ref.shape[1],
        peer_slots(me_ref[0], peers, local_slots, -1),
    )
    wide = spread(low_ref[...].astype(jnp.float32), masks)
    down = jnp.concatenate([ref[: rank * local_slots] for ref in factors], axis=0)
    out_ref[...] = (mxu(wide, down, TN) * ADAPTER_SCALE).astype(jnp.bfloat16)


def call(kernel, scalars, arrays, out_shape, flops, name):
    return pl.pallas_call(
        kernel,
        in_specs=[pl.BlockSpec(memory_space=pltpu.SMEM)] * len(scalars)
        + [pl.BlockSpec(memory_space=pltpu.VMEM)] * len(arrays),
        out_specs=jax.tree.map(lambda _: pl.BlockSpec(memory_space=pltpu.VMEM), out_shape),
        out_shape=out_shape,
        compiler_params=pltpu.CompilerParams(vmem_limit_bytes=VMEM_BYTES),
        cost_estimate=pl.CostEstimate(flops=flops, bytes_accessed=4 * 2**20, transcendentals=0),
        name=name,
    )(*scalars, *arrays)


def send(array, axis, shift):
    size = lax.axis_size(axis)
    return lax.ppermute(array, axis, [(i, (i + shift) % size) for i in range(size)])


def local(
    normed_input,
    rotated_queries,
    rotated_keys,
    value_rows,
    output_gradient,
    document_length,
    document_adapter,
    adapter_in_slot,
    down_weight,
    up_weight,
):
    row_count, width = normed_input.shape
    local_slots, rank, _ = down_weight.shape
    share = local_slots * rank
    peers, parts = lax.axis_size("dp"), lax.axis_size("tensor")
    me = lax.axis_index("dp").astype(jnp.int32).reshape(1)
    scalars = (document_length, document_adapter, adapter_in_slot, me)
    own = jnp.concatenate(
        [down_weight.reshape(share, width), up_weight.reshape(share, width)], axis=0
    )
    factors = [own] + [send(own, "dp", shift) for shift in range(1, peers)]
    query_gradient, key_gradient, value_gradient = attention_backward(
        rotated_queries, rotated_keys, value_rows, output_gradient, document_length
    )
    low = call(
        functools.partial(low_kernel, peers, local_slots),
        scalars,
        (normed_input, query_gradient, *factors),
        jax.ShapeDtypeStruct((2 * rank, row_count), jnp.float32),
        10**9,
        "low",
    )
    lows = [low] + [send(low, "tensor", shift) for shift in range(1, parts)]
    *terms, low_grads = call(
        functools.partial(product_kernel, peers, local_slots, parts),
        scalars,
        (*lows, normed_input, query_gradient),
        [
            jax.ShapeDtypeStruct((2 * share, width), jnp.float32 if shift == 0 else jnp.bfloat16)
            for shift in range(peers)
        ]
        + [jax.ShapeDtypeStruct((rank, row_count), jnp.bfloat16)],
        10**9,
        "product",
    )
    received = [send(terms[shift], "dp", shift) for shift in range(1, peers)]
    input_gradient = call(
        functools.partial(input_kernel, peers, local_slots),
        scalars,
        (low_grads, *factors),
        jax.ShapeDtypeStruct((row_count, width), jnp.bfloat16),
        10**9,
        "input_gradient",
    )
    total = terms[0]
    for part in received:
        total = total + part.astype(jnp.float32)
    down_gradient = total[:share].reshape(local_slots, rank, width)
    up_gradient = total[share:].reshape(local_slots, rank, width)
    return (input_gradient, key_gradient, value_gradient, down_gradient, up_gradient)


def solution(mesh):
    return jax.shard_map(
        local,
        mesh=mesh,
        in_specs=(
            P(("groups", "dp"), "tensor"),
            P(("groups", "dp"), "tensor"),
            P(("groups", "dp"), "tensor"),
            P(("groups", "dp"), "tensor"),
            P(("groups", "dp"), "tensor"),
            P(("groups", "dp"), None),
            P(("groups", "dp"), None),
            P(),
            P(("groups", "dp"), None, "tensor"),
            P(("groups", "dp"), None, "tensor"),
        ),
        out_specs=(
            P(("groups", "dp"), "tensor"),
            P(("groups", "dp"), "tensor"),
            P(("groups", "dp"), "tensor"),
            P(("groups", "dp"), None, "tensor"),
            P(("groups", "dp"), None, "tensor"),
        ),
        check_vma=False,
    )
```

```python
import functools
import math

import jax
import jax.numpy as jnp
from jax import lax
from jax.experimental import pallas as pl
from jax.experimental.pallas import tpu as pltpu
from jax.sharding import PartitionSpec as P

QUERY_HEAD_COUNT = 64
KEY_VALUE_HEADS = 8
HEAD_SIZE = 128
GROUP_SHARE = QUERY_HEAD_COUNT // KEY_VALUE_HEADS
DOCUMENT_REACH = 256
BLOCK = 128

MASKED = -1e30
ADAPTER_SCALE = 2.0
LOG2_E = 1.4426950408889634
ATTENTION_VMEM = 24 * 1024 * 1024
LOW_STEPS = 4
VMEM_BYTES = 16 * 1024 * 1024

NN = (((1,), (0,)), ((), ()))
NT = (((1,), (1,)), ((), ()))
TN = (((0,), (0,)), ((), ()))


def mxu(a, b, dims):
    return lax.dot_general(a, b, dims, preferred_element_type=jnp.float32)


def query_spans(row_count):
    return [
        (at, max(0, (at - (DOCUMENT_REACH - 1)) // BLOCK * BLOCK), at + BLOCK)
        for at in range(0, row_count, BLOCK)
    ]


def pack_kernel(row_count, len_ref, down_hbm, up_hbm, own_ref, bias_ref, sems):
    share = down_hbm.shape[0]
    copies = [
        pltpu.make_async_copy(down_hbm, own_ref.at[:share], sems.at[0]),
        pltpu.make_async_copy(up_hbm, own_ref.at[share:], sems.at[1]),
    ]
    for copy in copies:
        copy.start()
    at = 0
    for first, low, high in query_spans(row_count):
        width = high - low
        query = lax.broadcasted_iota(jnp.int32, (1, BLOCK), 1) + first
        start = jnp.zeros((1, BLOCK), jnp.int32)
        end = jnp.int32(0)
        for index in range(len_ref.shape[1] - 1):
            end = end + len_ref[0, index]
            start = jnp.where(query >= end, end, start)
        key = lax.broadcasted_iota(jnp.int32, (width, BLOCK), 0) + low
        bias_ref[at : at + width, :] = jnp.where((key >= start) & (key <= query), 0.0, MASKED)
        at += width
    for copy in copies:
        copy.wait()


def attention_kernel(
    bias_ref, q_ref, g_ref, k_ref, v_ref, gq_hbm, gk_ref, gv_ref, gq_ref, sems
):
    row_count = q_ref.shape[0]
    scale = 1.0 / math.sqrt(HEAD_SIZE)
    spans = query_spans(row_count)
    copies = []
    for group in range(k_ref.shape[1] // HEAD_SIZE):
        columns = slice(group * HEAD_SIZE, (group + 1) * HEAD_SIZE)
        heads = [
            slice(h * HEAD_SIZE, (h + 1) * HEAD_SIZE)
            for h in range(group * GROUP_SHARE, (group + 1) * GROUP_SHARE)
        ]
        key_t = k_ref[:, columns].T
        grad_key = [None] * len(spans)
        grad_value = [None] * len(spans)
        at = 0
        for first, low, high in spans:
            width = high - low
            rows = slice(first, first + BLOCK)
            query = jnp.concatenate([q_ref[rows, head] for head in heads], axis=0)
            grad = jnp.concatenate([g_ref[rows, head] for head in heads], axis=0)
            all_scores = mxu(k_ref[low:high, columns], query, NT)
            all_grad_weights = mxu(v_ref[low:high, columns], grad, NT)
            bias = bias_ref[at : at + width, :]
            at += width
            rounded, grad_scores = [], []
            for h in range(GROUP_SHARE):
                part = slice(h * BLOCK, (h + 1) * BLOCK)
                scores = all_scores[:, part] * (scale * LOG2_E) + bias
                grad_weights = all_grad_weights[:, part]
                largest = jnp.max(scores, axis=0, keepdims=True)
                numerator = jnp.exp2(scores - largest)
                weights = numerator * (1.0 / jnp.sum(numerator, axis=0, keepdims=True))
                rounded.append(weights.astype(jnp.bfloat16))
                delta = jnp.sum(
                    rounded[-1].astype(jnp.float32) * grad_weights, axis=0, keepdims=True
                )
                grad_scores.append((weights * (grad_weights - delta)).astype(jnp.bfloat16))
            rounded = jnp.concatenate(rounded, axis=1)
            grad_scores = jnp.concatenate(grad_scores, axis=1)
            value_terms = mxu(rounded, grad, NN)
            key_terms = mxu(grad_scores, query, NN)
            for index in range(low // BLOCK, high // BLOCK):
                part = slice(index * BLOCK - low, (index + 1) * BLOCK - low)
                for total, terms in ((grad_value, value_terms), (grad_key, key_terms)):
                    total[index] = (
                        terms[part] if total[index] is None else total[index] + terms[part]
                    )
            grad_query = (mxu(key_t[:, low:high], grad_scores, NN) * scale).astype(jnp.bfloat16)
            for h, head in enumerate(heads):
                gq_ref[head, rows] = grad_query[:, h * BLOCK : (h + 1) * BLOCK]
            block = (slice(heads[0].start, heads[-1].stop), rows)
            copies.append(
                pltpu.make_async_copy(gq_ref.at[block], gq_hbm.at[block], sems.at[len(copies)])
            )
            copies[-1].start()
        for index in range(len(spans)):
            rows = slice(index * BLOCK, (index + 1) * BLOCK)
            gk_ref[rows, columns] = (grad_key[index] * scale).astype(jnp.bfloat16)
            gv_ref[rows, columns] = grad_value[index].astype(jnp.bfloat16)
    for copy in copies:
        copy.wait()


def attention_backward(bias, queries, output_gradient, keys, values):
    turned = (queries.shape[1], queries.shape[0])
    chunks = keys.shape[1] // HEAD_SIZE * (queries.shape[0] // BLOCK)
    vmem = pl.BlockSpec(memory_space=pltpu.VMEM)
    return pl.pallas_call(
        attention_kernel,
        in_specs=[vmem] * 5,
        out_specs=[pl.BlockSpec(memory_space=pltpu.HBM), vmem, vmem],
        out_shape=[
            pltpu.HBM(turned, jnp.bfloat16),
            jax.ShapeDtypeStruct(keys.shape, jnp.bfloat16),
            jax.ShapeDtypeStruct(values.shape, jnp.bfloat16),
        ],
        scratch_shapes=[
            pltpu.VMEM(turned, jnp.bfloat16),
            pltpu.SemaphoreType.DMA((chunks,)),
        ],
        compiler_params=pltpu.CompilerParams(vmem_limit_bytes=ATTENTION_VMEM),
        cost_estimate=pl.CostEstimate(
            flops=8 * 10**9, bytes_accessed=8 * 2**20, transcendentals=0
        ),
        name="attention_backward",
    )(bias, queries, output_gradient, keys, values)


def slot_masks(len_ref, adapter_ref, slot_ref, row_count, slots):
    token = lax.broadcasted_iota(jnp.int32, (1, row_count), 1)
    adapter = jnp.full((1, row_count), adapter_ref[0, 0], jnp.int32)
    end = jnp.int32(0)
    for index in range(len_ref.shape[1] - 1):
        end = end + len_ref[0, index]
        adapter = jnp.where(token >= end, adapter_ref[0, index + 1], adapter)
    return [adapter == slot_ref[slot] for slot in slots]


def peer_slots(me, peers, local_slots, sign):
    return [
        lax.rem(me + sign * shift + peers, peers) * local_slots + own
        for shift in range(peers)
        for own in range(local_slots)
    ]


def select(wide, masks, rank):
    total = None
    for index, mask in enumerate(masks):
        part = jnp.where(mask, wide[index * rank : (index + 1) * rank], 0.0)
        total = part if total is None else total + part
    return total


def low_kernel(peers, local_slots, len_ref, adapter_ref, slot_ref, me_ref, x_ref, gq_hbm, *refs):
    factors, (out_ref, gq_ref, sems) = refs[:peers], refs[peers:]
    step = gq_ref.shape[0] // LOW_STEPS
    pieces = [pl.ds(index * step, step) for index in range(LOW_STEPS)]
    copies = [
        pltpu.make_async_copy(gq_hbm.at[piece], gq_ref.at[piece], sems.at[index])
        for index, piece in enumerate(pieces)
    ]
    for copy in copies:
        copy.start()
    rank = factors[0].shape[0] // (2 * local_slots)
    share = rank * local_slots
    row_count = x_ref.shape[0]
    masks = slot_masks(
        len_ref, adapter_ref, slot_ref, row_count, peer_slots(me_ref[0], peers, local_slots, -1)
    )
    down = jnp.concatenate([ref[:share] for ref in factors], axis=0)
    out_ref[:rank] = select(mxu(down, x_ref[...], NT), masks, rank)
    total = None
    for piece, copy in zip(pieces, copies):
        up = jnp.concatenate([ref[share:, piece] for ref in factors], axis=0)
        copy.wait()
        part = mxu(up, gq_ref[piece], NN)
        total = part if total is None else total + part
    out_ref[rank:] = select(total, masks, rank)


def spread(low, masks):
    zero = jnp.zeros_like(low)
    return jnp.concatenate([jnp.where(mask, low, zero) for mask in masks], axis=0).astype(
        jnp.bfloat16
    )


def product_kernel(peers, local_slots, parts, len_ref, adapter_ref, slot_ref, me_ref, *refs):
    lows, (x_ref, gq_ref), outs = refs[:parts], refs[parts : parts + 2], refs[parts + 2 :]
    low = lows[0][...]
    for ref in lows[1:]:
        low = low + ref[...]
    rank = low.shape[0] // 2
    share = rank * local_slots
    low = low.astype(jnp.bfloat16).astype(jnp.float32)
    masks = slot_masks(
        len_ref,
        adapter_ref,
        slot_ref,
        x_ref.shape[0],
        peer_slots(me_ref[0], peers, local_slots, 1),
    )
    wide_in, wide_grad = spread(low[:rank], masks), spread(low[rank:], masks)
    down = mxu(wide_grad, x_ref[...], NN) * ADAPTER_SCALE
    up = mxu(wide_in, gq_ref[...], NT) * ADAPTER_SCALE
    for shift, ref in enumerate(outs[:peers]):
        rows = slice(shift * share, (shift + 1) * share)
        ref[:share] = down[rows].astype(ref.dtype)
        ref[share:] = up[rows].astype(ref.dtype)
    outs[peers][...] = low[rank:].astype(jnp.bfloat16)


def input_kernel(peers, local_slots, len_ref, adapter_ref, slot_ref, me_ref, low_ref, *refs):
    factors, out_ref = refs[:peers], refs[peers]
    rank = low_ref.shape[0]
    masks = slot_masks(
        len_ref,
        adapter_ref,
        slot_ref,
        low_ref.shape[1],
        peer_slots(me_ref[0], peers, local_slots, -1),
    )
    wide = spread(low_ref[...].astype(jnp.float32), masks)
    down = jnp.concatenate([ref[: rank * local_slots] for ref in factors], axis=0)
    out_ref[...] = (mxu(wide, down, TN) * ADAPTER_SCALE).astype(jnp.bfloat16)


def call(kernel, scalars, arrays, out_shape, flops, name, in_hbm=(), scratch=()):
    return pl.pallas_call(
        kernel,
        in_specs=[pl.BlockSpec(memory_space=pltpu.SMEM)] * len(scalars)
        + [
            pl.BlockSpec(memory_space=pltpu.HBM if index in in_hbm else pltpu.VMEM)
            for index in range(len(arrays))
        ],
        out_specs=jax.tree.map(lambda _: pl.BlockSpec(memory_space=pltpu.VMEM), out_shape),
        out_shape=out_shape,
        scratch_shapes=scratch,
        compiler_params=pltpu.CompilerParams(vmem_limit_bytes=VMEM_BYTES),
        cost_estimate=pl.CostEstimate(flops=flops, bytes_accessed=4 * 2**20, transcendentals=0),
        name=name,
    )(*scalars, *arrays)


def send(array, axis, shift):
    size = lax.axis_size(axis)
    return lax.ppermute(array, axis, [(i, (i + shift) % size) for i in range(size)])


def local(
    normed_input,
    rotated_queries,
    rotated_keys,
    value_rows,
    output_gradient,
    document_length,
    document_adapter,
    adapter_in_slot,
    down_weight,
    up_weight,
):
    row_count, width = normed_input.shape
    local_slots, rank, _ = down_weight.shape
    share = local_slots * rank
    peers, parts = lax.axis_size("dp"), lax.axis_size("tensor")
    me = lax.axis_index("dp").astype(jnp.int32).reshape(1)
    scalars = (document_length, document_adapter, adapter_in_slot, me)
    pair_rows = sum(high - low for _, low, high in query_spans(row_count))
    own, bias = pl.pallas_call(
        functools.partial(pack_kernel, row_count),
        in_specs=[pl.BlockSpec(memory_space=pltpu.SMEM)]
        + [pl.BlockSpec(memory_space=pltpu.HBM)] * 2,
        out_specs=[pl.BlockSpec(memory_space=pltpu.VMEM)] * 2,
        out_shape=[
            jax.ShapeDtypeStruct((2 * share, width), down_weight.dtype),
            jax.ShapeDtypeStruct((pair_rows, BLOCK), jnp.float32),
        ],
        scratch_shapes=[pltpu.SemaphoreType.DMA((2,))],
        compiler_params=pltpu.CompilerParams(vmem_limit_bytes=VMEM_BYTES),
        cost_estimate=pl.CostEstimate(flops=10**10, bytes_accessed=2**20, transcendentals=0),
        name="pack",
    )(
        *(
            pltpu.with_memory_space_constraint(array, pltpu.HBM)
            for array in (
                document_length,
                down_weight.reshape(share, width),
                up_weight.reshape(share, width),
            )
        )
    )
    factors = [own] + [send(own, "dp", shift) for shift in range(1, peers)]
    query_gradient, key_gradient, value_gradient = attention_backward(
        bias, rotated_queries, output_gradient, rotated_keys, value_rows
    )
    low = call(
        functools.partial(low_kernel, peers, local_slots),
        scalars,
        (
            normed_input,
            pltpu.with_memory_space_constraint(query_gradient, pltpu.HBM),
            *factors,
        ),
        jax.ShapeDtypeStruct((2 * rank, row_count), jnp.float32),
        10**9,
        "low",
        in_hbm=(1,),
        scratch=[
            pltpu.VMEM((width, row_count), jnp.bfloat16),
            pltpu.SemaphoreType.DMA((LOW_STEPS,)),
        ],
    )
    lows = [low] + [send(low, "tensor", shift) for shift in range(1, parts)]
    *terms, low_grads = call(
        functools.partial(product_kernel, peers, local_slots, parts),
        scalars,
        (*lows, normed_input, query_gradient),
        [
            jax.ShapeDtypeStruct((2 * share, width), jnp.float32 if shift == 0 else jnp.bfloat16)
            for shift in range(peers)
        ]
        + [jax.ShapeDtypeStruct((rank, row_count), jnp.bfloat16)],
        10**9,
        "product",
    )
    received = [send(terms[shift], "dp", shift) for shift in range(1, peers)]
    input_gradient = call(
        functools.partial(input_kernel, peers, local_slots),
        scalars,
        (low_grads, *factors),
        jax.ShapeDtypeStruct((row_count, width), jnp.bfloat16),
        10**9,
        "input_gradient",
    )
    total = terms[0]
    for part in received:
        total = total + part.astype(jnp.float32)
    down_gradient = total[:share].reshape(local_slots, rank, width)
    up_gradient = total[share:].reshape(local_slots, rank, width)
    return (input_gradient, key_gradient, value_gradient, down_gradient, up_gradient)


def solution(mesh):
    return jax.shard_map(
        local,
        mesh=mesh,
        in_specs=(
            P(("groups", "dp"), "tensor"),
            P(("groups", "dp"), "tensor"),
            P(("groups", "dp"), "tensor"),
            P(("groups", "dp"), "tensor"),
            P(("groups", "dp"), "tensor"),
            P(("groups", "dp"), None),
            P(("groups", "dp"), None),
            P(),
            P(("groups", "dp"), None, "tensor"),
            P(("groups", "dp"), None, "tensor"),
        ),
        out_specs=(
            P(("groups", "dp"), "tensor"),
            P(("groups", "dp"), "tensor"),
            P(("groups", "dp"), "tensor"),
            P(("groups", "dp"), None, "tensor"),
            P(("groups", "dp"), None, "tensor"),
        ),
        check_vma=False,
    )
```

```python
import functools
import math

import jax
import jax.numpy as jnp
from jax import lax
from jax.experimental import pallas as pl
from jax.experimental.pallas import tpu as pltpu
from jax.sharding import PartitionSpec as P

QUERY_HEAD_COUNT = 64
KEY_VALUE_HEADS = 8
HEAD_SIZE = 128
GROUP_SHARE = QUERY_HEAD_COUNT // KEY_VALUE_HEADS
DOCUMENT_REACH = 256
BLOCK = 128

MASKED = -1e30
ADAPTER_SCALE = 2.0
LOG2_E = 1.4426950408889634
ATTENTION_VMEM = 24 * 1024 * 1024
LOW_STEPS = 4
VMEM_BYTES = 16 * 1024 * 1024

NN = (((1,), (0,)), ((), ()))
NT = (((1,), (1,)), ((), ()))
TN = (((0,), (0,)), ((), ()))


def mxu(a, b, dims):
    return lax.dot_general(a, b, dims, preferred_element_type=jnp.float32)


def query_spans(row_count):
    return [
        (at, max(0, (at - (DOCUMENT_REACH - 1)) // BLOCK * BLOCK), at + BLOCK)
        for at in range(0, row_count, BLOCK)
    ]


def pack_kernel(row_count, len_ref, down_hbm, up_hbm, own_ref, bias_ref, sems):
    share = down_hbm.shape[0]
    copies = [
        pltpu.make_async_copy(down_hbm, own_ref.at[:share], sems.at[0]),
        pltpu.make_async_copy(up_hbm, own_ref.at[share:], sems.at[1]),
    ]
    for copy in copies:
        copy.start()
    at = 0
    for first, low, high in query_spans(row_count):
        width = high - low
        query = lax.broadcasted_iota(jnp.int32, (1, BLOCK), 1) + first
        start = jnp.zeros((1, BLOCK), jnp.int32)
        end = jnp.int32(0)
        for index in range(len_ref.shape[1] - 1):
            end = end + len_ref[0, index]
            start = jnp.where(query >= end, end, start)
        key = lax.broadcasted_iota(jnp.int32, (width, BLOCK), 0) + low
        bias_ref[at : at + width, :] = jnp.where((key >= start) & (key <= query), 0.0, MASKED)
        at += width
    for copy in copies:
        copy.wait()


def attention_kernel(
    bias_ref, q_ref, g_ref, k_ref, v_ref, gq_hbm, gk_ref, gv_ref, gq_ref, sems
):
    row_count = q_ref.shape[0]
    scale = 1.0 / math.sqrt(HEAD_SIZE)
    spans = query_spans(row_count)
    copies = []
    for group in range(k_ref.shape[1] // HEAD_SIZE):
        columns = slice(group * HEAD_SIZE, (group + 1) * HEAD_SIZE)
        heads = [
            slice(h * HEAD_SIZE, (h + 1) * HEAD_SIZE)
            for h in range(group * GROUP_SHARE, (group + 1) * GROUP_SHARE)
        ]
        key_t = k_ref[:, columns].T
        grad_key = [None] * len(spans)
        grad_value = [None] * len(spans)
        at = 0
        for first, low, high in spans:
            width = high - low
            rows = slice(first, first + BLOCK)
            query = jnp.concatenate([q_ref[rows, head] for head in heads], axis=0)
            grad = jnp.concatenate([g_ref[rows, head] for head in heads], axis=0)
            all_scores = mxu(k_ref[low:high, columns], query, NT)
            all_grad_weights = mxu(v_ref[low:high, columns], grad, NT)
            bias = bias_ref[at : at + width, :]
            at += width
            rounded, grad_scores = [], []
            for h in range(GROUP_SHARE):
                part = slice(h * BLOCK, (h + 1) * BLOCK)
                scores = all_scores[:, part] * (scale * LOG2_E) + bias
                grad_weights = all_grad_weights[:, part]
                largest = jnp.max(scores, axis=0, keepdims=True)
                numerator = jnp.exp2(scores - largest)
                weights = numerator * (1.0 / jnp.sum(numerator, axis=0, keepdims=True))
                rounded.append(weights.astype(jnp.bfloat16))
                delta = jnp.sum(
                    rounded[-1].astype(jnp.float32) * grad_weights, axis=0, keepdims=True
                )
                grad_scores.append((weights * (grad_weights - delta)).astype(jnp.bfloat16))
            rounded = jnp.concatenate(rounded, axis=1)
            grad_scores = jnp.concatenate(grad_scores, axis=1)
            value_terms = mxu(rounded, grad, NN)
            key_terms = mxu(grad_scores, query, NN)
            for index in range(low // BLOCK, high // BLOCK):
                part = slice(index * BLOCK - low, (index + 1) * BLOCK - low)
                for total, terms in ((grad_value, value_terms), (grad_key, key_terms)):
                    total[index] = (
                        terms[part] if total[index] is None else total[index] + terms[part]
                    )
            grad_query = (mxu(key_t[:, low:high], grad_scores, NN) * scale).astype(jnp.bfloat16)
            for h, head in enumerate(heads):
                gq_ref[head, rows] = grad_query[:, h * BLOCK : (h + 1) * BLOCK]
            block = (slice(heads[0].start, heads[-1].stop), rows)
            copies.append(
                pltpu.make_async_copy(gq_ref.at[block], gq_hbm.at[block], sems.at[len(copies)])
            )
            copies[-1].start()
        for index in range(len(spans)):
            rows = slice(index * BLOCK, (index + 1) * BLOCK)
            gk_ref[rows, columns] = (grad_key[index] * scale).astype(jnp.bfloat16)
            gv_ref[rows, columns] = grad_value[index].astype(jnp.bfloat16)
    for copy in copies:
        copy.wait()


def attention_backward(bias, queries, output_gradient, keys, values):
    turned = (queries.shape[1], queries.shape[0])
    chunks = keys.shape[1] // HEAD_SIZE * (queries.shape[0] // BLOCK)
    vmem = pl.BlockSpec(memory_space=pltpu.VMEM)
    return pl.pallas_call(
        attention_kernel,
        in_specs=[vmem] * 5,
        out_specs=[pl.BlockSpec(memory_space=pltpu.HBM), vmem, vmem],
        out_shape=[
            pltpu.HBM(turned, jnp.bfloat16),
            jax.ShapeDtypeStruct(keys.shape, jnp.bfloat16),
            jax.ShapeDtypeStruct(values.shape, jnp.bfloat16),
        ],
        scratch_shapes=[
            pltpu.VMEM(turned, jnp.bfloat16),
            pltpu.SemaphoreType.DMA((chunks,)),
        ],
        compiler_params=pltpu.CompilerParams(vmem_limit_bytes=ATTENTION_VMEM),
        cost_estimate=pl.CostEstimate(
            flops=8 * 10**9, bytes_accessed=8 * 2**20, transcendentals=0
        ),
        name="attention_backward",
    )(bias, queries, output_gradient, keys, values)


def slot_masks(len_ref, adapter_ref, slot_ref, row_count, slots):
    token = lax.broadcasted_iota(jnp.int32, (1, row_count), 1)
    adapter = jnp.full((1, row_count), adapter_ref[0, 0], jnp.int32)
    end = jnp.int32(0)
    for index in range(len_ref.shape[1] - 1):
        end = end + len_ref[0, index]
        adapter = jnp.where(token >= end, adapter_ref[0, index + 1], adapter)
    return [adapter == slot_ref[slot] for slot in slots]


def peer_slots(me, peers, local_slots):
    return [
        (me ^ distance) * local_slots + own
        for distance in range(peers)
        for own in range(local_slots)
    ]


def select(wide, masks, rank):
    total = None
    for index, mask in enumerate(masks):
        part = jnp.where(mask, wide[index * rank : (index + 1) * rank], 0.0)
        total = part if total is None else total + part
    return total


def low_kernel(peers, local_slots, len_ref, adapter_ref, slot_ref, me_ref, x_ref, gq_hbm, *refs):
    factors, (out_ref, sent_ref, gq_ref, sems) = refs[:peers], refs[peers:]
    step = gq_ref.shape[0] // LOW_STEPS
    pieces = [pl.ds(index * step, step) for index in range(LOW_STEPS)]
    copies = [
        pltpu.make_async_copy(gq_hbm.at[piece], gq_ref.at[piece], sems.at[index])
        for index, piece in enumerate(pieces)
    ]
    for copy in copies:
        copy.start()
    rank = factors[0].shape[0] // (2 * local_slots)
    share = rank * local_slots
    row_count = x_ref.shape[0]
    masks = slot_masks(
        len_ref, adapter_ref, slot_ref, row_count, peer_slots(me_ref[0], peers, local_slots)
    )
    down = jnp.concatenate([ref[:share] for ref in factors], axis=0)
    out_ref[:rank] = select(mxu(down, x_ref[...], NT), masks, rank)
    total = None
    for piece, copy in zip(pieces, copies):
        up = jnp.concatenate([ref[share:, piece] for ref in factors], axis=0)
        copy.wait()
        part = mxu(up, gq_ref[piece], NN)
        total = part if total is None else total + part
    out_ref[rank:] = select(total, masks, rank)
    sent_ref[...] = out_ref[...].astype(jnp.bfloat16)


def spread(low, masks):
    zero = jnp.zeros_like(low)
    return jnp.concatenate([jnp.where(mask, low, zero) for mask in masks], axis=0).astype(
        jnp.bfloat16
    )


def product_kernel(peers, local_slots, parts, len_ref, adapter_ref, slot_ref, me_ref, *refs):
    lows, (x_ref, gq_ref), outs = refs[:parts], refs[parts : parts + 2], refs[parts + 2 :]
    low = lows[0][...]
    for ref in lows[1:]:
        low = low + ref[...].astype(jnp.float32)
    rank = low.shape[0] // 2
    share = rank * local_slots
    low = low.astype(jnp.bfloat16).astype(jnp.float32)
    masks = slot_masks(
        len_ref,
        adapter_ref,
        slot_ref,
        x_ref.shape[0],
        peer_slots(me_ref[0], peers, local_slots),
    )
    wide_in, wide_grad = spread(low[:rank], masks), spread(low[rank:], masks)
    down = mxu(wide_grad, x_ref[...], NN) * ADAPTER_SCALE
    up = mxu(wide_in, gq_ref[...], NT) * ADAPTER_SCALE
    for distance, ref in enumerate(outs[:peers]):
        rows = slice(distance * share, (distance + 1) * share)
        ref[:share] = down[rows].astype(ref.dtype)
        ref[share:] = up[rows].astype(ref.dtype)
    outs[peers][...] = low[rank:].astype(jnp.bfloat16)


def input_kernel(peers, local_slots, len_ref, adapter_ref, slot_ref, me_ref, low_ref, *refs):
    factors, out_ref = refs[:peers], refs[peers]
    rank = low_ref.shape[0]
    masks = slot_masks(
        len_ref,
        adapter_ref,
        slot_ref,
        low_ref.shape[1],
        peer_slots(me_ref[0], peers, local_slots),
    )
    wide = spread(low_ref[...].astype(jnp.float32), masks)
    down = jnp.concatenate([ref[: rank * local_slots] for ref in factors], axis=0)
    out_ref[...] = (mxu(wide, down, TN) * ADAPTER_SCALE).astype(jnp.bfloat16)


def call(kernel, scalars, arrays, out_shape, flops, name, in_hbm=(), scratch=()):
    return pl.pallas_call(
        kernel,
        in_specs=[pl.BlockSpec(memory_space=pltpu.SMEM)] * len(scalars)
        + [
            pl.BlockSpec(memory_space=pltpu.HBM if index in in_hbm else pltpu.VMEM)
            for index in range(len(arrays))
        ],
        out_specs=jax.tree.map(lambda _: pl.BlockSpec(memory_space=pltpu.VMEM), out_shape),
        out_shape=out_shape,
        scratch_shapes=scratch,
        compiler_params=pltpu.CompilerParams(vmem_limit_bytes=VMEM_BYTES),
        cost_estimate=pl.CostEstimate(flops=flops, bytes_accessed=4 * 2**20, transcendentals=0),
        name=name,
    )(*scalars, *arrays)


def swap(array, axis, distance):
    size = lax.axis_size(axis)
    return lax.ppermute(array, axis, [(i, i ^ distance) for i in range(size)])


def local(
    normed_input,
    rotated_queries,
    rotated_keys,
    value_rows,
    output_gradient,
    document_length,
    document_adapter,
    adapter_in_slot,
    down_weight,
    up_weight,
):
    row_count, width = normed_input.shape
    local_slots, rank, _ = down_weight.shape
    share = local_slots * rank
    peers, parts = lax.axis_size("dp"), lax.axis_size("tensor")
    me = lax.axis_index("dp").astype(jnp.int32).reshape(1)
    scalars = (document_length, document_adapter, adapter_in_slot, me)
    pair_rows = sum(high - low for _, low, high in query_spans(row_count))
    own, bias = pl.pallas_call(
        functools.partial(pack_kernel, row_count),
        in_specs=[pl.BlockSpec(memory_space=pltpu.SMEM)]
        + [pl.BlockSpec(memory_space=pltpu.HBM)] * 2,
        out_specs=[pl.BlockSpec(memory_space=pltpu.VMEM)] * 2,
        out_shape=[
            jax.ShapeDtypeStruct((2 * share, width), down_weight.dtype),
            jax.ShapeDtypeStruct((pair_rows, BLOCK), jnp.float32),
        ],
        scratch_shapes=[pltpu.SemaphoreType.DMA((2,))],
        compiler_params=pltpu.CompilerParams(vmem_limit_bytes=VMEM_BYTES),
        cost_estimate=pl.CostEstimate(flops=10**10, bytes_accessed=2**20, transcendentals=0),
        name="pack",
    )(
        *(
            pltpu.with_memory_space_constraint(array, pltpu.HBM)
            for array in (
                document_length,
                down_weight.reshape(share, width),
                up_weight.reshape(share, width),
            )
        )
    )
    factors = [own] + [swap(own, "dp", distance) for distance in range(1, peers)]
    query_gradient, key_gradient, value_gradient = attention_backward(
        bias, rotated_queries, output_gradient, rotated_keys, value_rows
    )
    low, low_sent = call(
        functools.partial(low_kernel, peers, local_slots),
        scalars,
        (
            normed_input,
            pltpu.with_memory_space_constraint(query_gradient, pltpu.HBM),
            *factors,
        ),
        [
            jax.ShapeDtypeStruct((2 * rank, row_count), dtype)
            for dtype in (jnp.float32, jnp.bfloat16)
        ],
        10**9,
        "low",
        in_hbm=(1,),
        scratch=[
            pltpu.VMEM((width, row_count), jnp.bfloat16),
            pltpu.SemaphoreType.DMA((LOW_STEPS,)),
        ],
    )
    lows = [low] + [swap(low_sent, "tensor", distance) for distance in range(1, parts)]
    *terms, low_grads = call(
        functools.partial(product_kernel, peers, local_slots, parts),
        scalars,
        (*lows, normed_input, query_gradient),
        [
            jax.ShapeDtypeStruct((2 * share, width), jnp.bfloat16 if distance else jnp.float32)
            for distance in range(peers)
        ]
        + [jax.ShapeDtypeStruct((rank, row_count), jnp.bfloat16)],
        10**9,
        "product",
    )
    received = [swap(terms[distance], "dp", distance) for distance in range(1, peers)]
    input_gradient = call(
        functools.partial(input_kernel, peers, local_slots),
        scalars,
        (low_grads, *factors),
        jax.ShapeDtypeStruct((row_count, width), jnp.bfloat16),
        10**9,
        "input_gradient",
    )
    total = terms[0]
    for part in received:
        total = total + part.astype(jnp.float32)
    down_gradient = total[:share].reshape(local_slots, rank, width)
    up_gradient = total[share:].reshape(local_slots, rank, width)
    return (input_gradient, key_gradient, value_gradient, down_gradient, up_gradient)


def solution(mesh):
    return jax.shard_map(
        local,
        mesh=mesh,
        in_specs=(
            P(("groups", "dp"), "tensor"),
            P(("groups", "dp"), "tensor"),
            P(("groups", "dp"), "tensor"),
            P(("groups", "dp"), "tensor"),
            P(("groups", "dp"), "tensor"),
            P(("groups", "dp"), None),
            P(("groups", "dp"), None),
            P(),
            P(("groups", "dp"), None, "tensor"),
            P(("groups", "dp"), None, "tensor"),
        ),
        out_specs=(
            P(("groups", "dp"), "tensor"),
            P(("groups", "dp"), "tensor"),
            P(("groups", "dp"), "tensor"),
            P(("groups", "dp"), None, "tensor"),
            P(("groups", "dp"), None, "tensor"),
        ),
        check_vma=False,
    )
```

```python
import functools
import math

import jax
import jax.numpy as jnp
from jax import lax
from jax.experimental import pallas as pl
from jax.experimental.pallas import tpu as pltpu
from jax.sharding import PartitionSpec as P

QUERY_HEAD_COUNT = 64
KEY_VALUE_HEADS = 8
HEAD_SIZE = 128
GROUP_SHARE = QUERY_HEAD_COUNT // KEY_VALUE_HEADS
DOCUMENT_REACH = 256
BLOCK = 128

MASKED = -1e30
ADAPTER_SCALE = 2.0
LOG2_E = 1.4426950408889634
ATTENTION_VMEM = 24 * 1024 * 1024
LOW_STEPS = 4
VMEM_BYTES = 16 * 1024 * 1024

NN = (((1,), (0,)), ((), ()))
NT = (((1,), (1,)), ((), ()))
TN = (((0,), (0,)), ((), ()))


def mxu(a, b, dims):
    return lax.dot_general(a, b, dims, preferred_element_type=jnp.float32)


def query_spans(row_count):
    return [
        (at, max(0, (at - (DOCUMENT_REACH - 1)) // BLOCK * BLOCK), at + BLOCK)
        for at in range(0, row_count, BLOCK)
    ]


def pack_kernel(
    row_count,
    peers,
    len_hbm,
    adapter_hbm,
    slot_hbm,
    down_hbm,
    up_hbm,
    own_ref,
    bias_ref,
    mask_ref,
    len_ref,
    adapter_ref,
    slot_ref,
    sems,
):
    share = down_hbm.shape[0]
    local_slots = slot_hbm.shape[0] // peers
    pairs = (
        (len_hbm, len_ref),
        (adapter_hbm, adapter_ref),
        (slot_hbm, slot_ref),
        (down_hbm, own_ref.at[:share]),
        (up_hbm, own_ref.at[share:]),
    )
    copies = [
        pltpu.make_async_copy(source, target, sems.at[index])
        for index, (source, target) in enumerate(pairs)
    ]
    for copy in copies:
        copy.start()
    for copy in copies[:3]:
        copy.wait()
    lengths = [len_ref[0, index] for index in range(len_ref.shape[1] - 1)]

    token = lax.broadcasted_iota(jnp.int32, (1, row_count), 1)
    adapter = jnp.full((1, row_count), adapter_ref[0, 0], jnp.int32)
    begin = jnp.zeros((1, row_count), jnp.int32)
    end = jnp.int32(0)
    for index, length in enumerate(lengths):
        end = end + length
        adapter = jnp.where(token >= end, adapter_ref[0, index + 1], adapter)
        begin = jnp.where(token >= end, end, begin)
    me = lax.axis_index("dp")
    for distance in range(peers):
        for own in range(local_slots):
            row = distance * local_slots + own
            held = slot_ref[(me ^ distance) * local_slots + own]
            mask_ref[row : row + 1, :] = jnp.where(adapter == held, 1.0, 0.0)
    at = 0
    for first, low, high in query_spans(row_count):
        width = high - low
        query = lax.broadcasted_iota(jnp.int32, (1, BLOCK), 1) + first
        start = begin[:, first : first + BLOCK]
        key = lax.broadcasted_iota(jnp.int32, (width, BLOCK), 0) + low
        bias_ref[at : at + width, :] = jnp.where((key >= start) & (key <= query), 0.0, MASKED)
        at += width
    for copy in copies[3:]:
        copy.wait()


def pack(row_count, peers, lengths, adapters, slots, down, up):
    pair_rows = sum(high - low for _, low, high in query_spans(row_count))
    arrays = [
        pltpu.with_memory_space_constraint(array, pltpu.HBM)
        for array in (lengths, adapters, slots, down, up)
    ]
    return pl.pallas_call(
        functools.partial(pack_kernel, row_count, peers),
        in_specs=[pl.BlockSpec(memory_space=pltpu.HBM)] * 5,
        out_specs=[pl.BlockSpec(memory_space=pltpu.VMEM)] * 3,
        out_shape=[
            jax.ShapeDtypeStruct((2 * down.shape[0], down.shape[1]), down.dtype),
            jax.ShapeDtypeStruct((pair_rows, BLOCK), jnp.float32),
            jax.ShapeDtypeStruct((slots.shape[0], row_count), jnp.float32),
        ],
        scratch_shapes=[
            pltpu.SMEM(lengths.shape, jnp.int32),
            pltpu.SMEM(adapters.shape, jnp.int32),
            pltpu.SMEM(slots.shape, jnp.int32),
            pltpu.SemaphoreType.DMA((5,)),
        ],
        compiler_params=pltpu.CompilerParams(vmem_limit_bytes=VMEM_BYTES),
        cost_estimate=pl.CostEstimate(flops=10**10, bytes_accessed=2**20, transcendentals=0),
        name="pack",
    )(*arrays)


def attention_kernel(
    bias_ref, q_ref, g_ref, k_ref, v_ref, gq_hbm, gk_ref, gv_ref, gq_ref, sems
):
    row_count = q_ref.shape[0]
    scale = 1.0 / math.sqrt(HEAD_SIZE)
    spans = query_spans(row_count)
    copies = []
    for group in range(k_ref.shape[1] // HEAD_SIZE):
        columns = slice(group * HEAD_SIZE, (group + 1) * HEAD_SIZE)
        heads = [
            slice(h * HEAD_SIZE, (h + 1) * HEAD_SIZE)
            for h in range(group * GROUP_SHARE, (group + 1) * GROUP_SHARE)
        ]
        key_t = k_ref[:, columns].T
        grad_key = [None] * len(spans)
        grad_value = [None] * len(spans)
        at = 0
        for first, low, high in spans:
            width = high - low
            rows = slice(first, first + BLOCK)
            query = jnp.concatenate([q_ref[rows, head] for head in heads], axis=0)
            grad = jnp.concatenate([g_ref[rows, head] for head in heads], axis=0)
            all_scores = mxu(k_ref[low:high, columns], query, NT)
            all_grad_weights = mxu(v_ref[low:high, columns], grad, NT)
            bias = bias_ref[at : at + width, :]
            at += width
            rounded, grad_scores = [], []
            for h in range(GROUP_SHARE):
                part = slice(h * BLOCK, (h + 1) * BLOCK)
                scores = all_scores[:, part] * (scale * LOG2_E) + bias
                grad_weights = all_grad_weights[:, part]
                largest = jnp.max(scores, axis=0, keepdims=True)
                numerator = jnp.exp2(scores - largest)
                weights = numerator * (1.0 / jnp.sum(numerator, axis=0, keepdims=True))
                rounded.append(weights.astype(jnp.bfloat16))
                delta = jnp.sum(
                    rounded[-1].astype(jnp.float32) * grad_weights, axis=0, keepdims=True
                )
                grad_scores.append((weights * (grad_weights - delta)).astype(jnp.bfloat16))
            rounded = jnp.concatenate(rounded, axis=1)
            grad_scores = jnp.concatenate(grad_scores, axis=1)
            value_terms = mxu(rounded, grad, NN)
            key_terms = mxu(grad_scores, query, NN)
            for index in range(low // BLOCK, high // BLOCK):
                part = slice(index * BLOCK - low, (index + 1) * BLOCK - low)
                for total, terms in ((grad_value, value_terms), (grad_key, key_terms)):
                    total[index] = (
                        terms[part] if total[index] is None else total[index] + terms[part]
                    )
            grad_query = (mxu(key_t[:, low:high], grad_scores, NN) * scale).astype(jnp.bfloat16)
            for h, head in enumerate(heads):
                gq_ref[head, rows] = grad_query[:, h * BLOCK : (h + 1) * BLOCK]
            block = (slice(heads[0].start, heads[-1].stop), rows)
            copies.append(
                pltpu.make_async_copy(gq_ref.at[block], gq_hbm.at[block], sems.at[len(copies)])
            )
            copies[-1].start()
        for index in range(len(spans)):
            rows = slice(index * BLOCK, (index + 1) * BLOCK)
            gk_ref[rows, columns] = (grad_key[index] * scale).astype(jnp.bfloat16)
            gv_ref[rows, columns] = grad_value[index].astype(jnp.bfloat16)
    for copy in copies:
        copy.wait()


def attention_backward(bias, queries, output_gradient, keys, values):
    turned = (queries.shape[1], queries.shape[0])
    chunks = keys.shape[1] // HEAD_SIZE * (queries.shape[0] // BLOCK)
    vmem = pl.BlockSpec(memory_space=pltpu.VMEM)
    return pl.pallas_call(
        attention_kernel,
        in_specs=[vmem] * 5,
        out_specs=[pl.BlockSpec(memory_space=pltpu.HBM), vmem, vmem],
        out_shape=[
            pltpu.HBM(turned, jnp.bfloat16),
            jax.ShapeDtypeStruct(keys.shape, jnp.bfloat16),
            jax.ShapeDtypeStruct(values.shape, jnp.bfloat16),
        ],
        scratch_shapes=[
            pltpu.VMEM(turned, jnp.bfloat16),
            pltpu.SemaphoreType.DMA((chunks,)),
        ],
        compiler_params=pltpu.CompilerParams(vmem_limit_bytes=ATTENTION_VMEM),
        cost_estimate=pl.CostEstimate(
            flops=8 * 10**9, bytes_accessed=8 * 2**20, transcendentals=0
        ),
        name="attention_backward",
    )(bias, queries, output_gradient, keys, values)


def select(wide, mask_ref, rank):
    total = None
    for slot in range(mask_ref.shape[0]):
        part = wide[slot * rank : (slot + 1) * rank] * mask_ref[slot : slot + 1, :]
        total = part if total is None else total + part
    return total


def spread(low, mask_ref):
    return jnp.concatenate(
        [low * mask_ref[slot : slot + 1, :] for slot in range(mask_ref.shape[0])], axis=0
    ).astype(jnp.bfloat16)


def low_kernel(peers, local_slots, mask_ref, x_ref, gq_hbm, *refs):
    factors, (out_ref, sent_ref, gq_ref, sems) = refs[:peers], refs[peers:]
    step = gq_ref.shape[0] // LOW_STEPS
    pieces = [pl.ds(index * step, step) for index in range(LOW_STEPS)]
    copies = [
        pltpu.make_async_copy(gq_hbm.at[piece], gq_ref.at[piece], sems.at[index])
        for index, piece in enumerate(pieces)
    ]
    for copy in copies:
        copy.start()
    rank = factors[0].shape[0] // (2 * local_slots)
    share = rank * local_slots
    down = jnp.concatenate([ref[:share] for ref in factors], axis=0)
    out_ref[:rank] = select(mxu(down, x_ref[...], NT), mask_ref, rank)
    total = None
    for piece, copy in zip(pieces, copies):
        up = jnp.concatenate([ref[share:, piece] for ref in factors], axis=0)
        copy.wait()
        part = mxu(up, gq_ref[piece], NN)
        total = part if total is None else total + part
    out_ref[rank:] = select(total, mask_ref, rank)
    sent_ref[...] = out_ref[...].astype(jnp.bfloat16)


def product_kernel(peers, local_slots, parts, mask_ref, *refs):
    lows, (x_ref, gq_ref), outs = refs[:parts], refs[parts : parts + 2], refs[parts + 2 :]
    low = lows[0][...]
    for ref in lows[1:]:
        low = low + ref[...].astype(jnp.float32)
    rank = low.shape[0] // 2
    share = rank * local_slots
    low = low.astype(jnp.bfloat16).astype(jnp.float32)
    wide_in, wide_grad = spread(low[:rank], mask_ref), spread(low[rank:], mask_ref)
    down = mxu(wide_grad, x_ref[...], NN) * ADAPTER_SCALE
    up = mxu(wide_in, gq_ref[...], NT) * ADAPTER_SCALE
    for distance, ref in enumerate(outs[:peers]):
        rows = slice(distance * share, (distance + 1) * share)
        ref[:share] = down[rows].astype(ref.dtype)
        ref[share:] = up[rows].astype(ref.dtype)
    outs[peers][...] = low[rank:].astype(jnp.bfloat16)


def input_kernel(peers, local_slots, mask_ref, low_ref, *refs):
    factors, out_ref = refs[:peers], refs[peers]
    rank = low_ref.shape[0]
    wide = spread(low_ref[...].astype(jnp.float32), mask_ref)
    down = jnp.concatenate([ref[: rank * local_slots] for ref in factors], axis=0)
    out_ref[...] = (mxu(wide, down, TN) * ADAPTER_SCALE).astype(jnp.bfloat16)


def call(kernel, arrays, out_shape, flops, name, in_hbm=(), scratch=()):
    return pl.pallas_call(
        kernel,
        in_specs=[
            pl.BlockSpec(memory_space=pltpu.HBM if index in in_hbm else pltpu.VMEM)
            for index in range(len(arrays))
        ],
        out_specs=jax.tree.map(lambda _: pl.BlockSpec(memory_space=pltpu.VMEM), out_shape),
        out_shape=out_shape,
        scratch_shapes=scratch,
        compiler_params=pltpu.CompilerParams(vmem_limit_bytes=VMEM_BYTES),
        cost_estimate=pl.CostEstimate(flops=flops, bytes_accessed=4 * 2**20, transcendentals=0),
        name=name,
    )(*arrays)


def swap(array, axis, distance):
    size = lax.axis_size(axis)
    return lax.ppermute(array, axis, [(i, i ^ distance) for i in range(size)])


def local(
    normed_input,
    rotated_queries,
    rotated_keys,
    value_rows,
    output_gradient,
    document_length,
    document_adapter,
    adapter_in_slot,
    down_weight,
    up_weight,
):
    row_count, width = normed_input.shape
    local_slots, rank, _ = down_weight.shape
    share = local_slots * rank
    peers, parts = lax.axis_size("dp"), lax.axis_size("tensor")
    own, bias, mask = pack(
        row_count,
        peers,
        document_length,
        document_adapter,
        adapter_in_slot,
        down_weight.reshape(share, width),
        up_weight.reshape(share, width),
    )
    factors = [own] + [swap(own, "dp", distance) for distance in range(1, peers)]
    query_gradient, key_gradient, value_gradient = attention_backward(
        bias, rotated_queries, output_gradient, rotated_keys, value_rows
    )
    low, low_sent = call(
        functools.partial(low_kernel, peers, local_slots),
        (
            mask,
            normed_input,
            pltpu.with_memory_space_constraint(query_gradient, pltpu.HBM),
            *factors,
        ),
        [
            jax.ShapeDtypeStruct((2 * rank, row_count), dtype)
            for dtype in (jnp.float32, jnp.bfloat16)
        ],
        10**9,
        "low",
        in_hbm=(2,),
        scratch=[
            pltpu.VMEM((width, row_count), jnp.bfloat16),
            pltpu.SemaphoreType.DMA((LOW_STEPS,)),
        ],
    )
    lows = [low] + [swap(low_sent, "tensor", distance) for distance in range(1, parts)]
    *terms, low_grads = call(
        functools.partial(product_kernel, peers, local_slots, parts),
        (mask, *lows, normed_input, query_gradient),
        [
            jax.ShapeDtypeStruct((2 * share, width), jnp.bfloat16 if distance else jnp.float32)
            for distance in range(peers)
        ]
        + [jax.ShapeDtypeStruct((rank, row_count), jnp.bfloat16)],
        10**9,
        "product",
    )
    received = [swap(terms[distance], "dp", distance) for distance in reversed(range(1, peers))]
    input_gradient = call(
        functools.partial(input_kernel, peers, local_slots),
        (mask, low_grads, *factors),
        jax.ShapeDtypeStruct((row_count, width), jnp.bfloat16),
        10**9,
        "input_gradient",
    )
    total = terms[0]
    for part in received:
        total = total + part.astype(jnp.float32)
    down_gradient = total[:share].reshape(local_slots, rank, width)
    up_gradient = total[share:].reshape(local_slots, rank, width)
    return (input_gradient, key_gradient, value_gradient, down_gradient, up_gradient)


def solution(mesh):
    return jax.shard_map(
        local,
        mesh=mesh,
        in_specs=(
            P(("groups", "dp"), "tensor"),
            P(("groups", "dp"), "tensor"),
            P(("groups", "dp"), "tensor"),
            P(("groups", "dp"), "tensor"),
            P(("groups", "dp"), "tensor"),
            P(("groups", "dp"), None),
            P(("groups", "dp"), None),
            P(),
            P(("groups", "dp"), None, "tensor"),
            P(("groups", "dp"), None, "tensor"),
        ),
        out_specs=(
            P(("groups", "dp"), "tensor"),
            P(("groups", "dp"), "tensor"),
            P(("groups", "dp"), "tensor"),
            P(("groups", "dp"), None, "tensor"),
            P(("groups", "dp"), None, "tensor"),
        ),
        check_vma=False,
    )
```

```python
import functools
import math

import jax
import jax.numpy as jnp
from jax import lax
from jax.experimental import pallas as pl
from jax.experimental.pallas import tpu as pltpu
from jax.sharding import PartitionSpec as P

QUERY_HEAD_COUNT = 64
KEY_VALUE_HEADS = 8
HEAD_SIZE = 128
GROUP_SHARE = QUERY_HEAD_COUNT // KEY_VALUE_HEADS
DOCUMENT_REACH = 256
BLOCK = 128
UNIT_HEADS = 2

MASKED = -1e30
ADAPTER_SCALE = 2.0
LOG2_E = 1.4426950408889634
ATTENTION_VMEM = 24 * 1024 * 1024
VMEM_BYTES = 16 * 1024 * 1024

NN = (((1,), (0,)), ((), ()))
NT = (((1,), (1,)), ((), ()))
TN = (((0,), (0,)), ((), ()))


def mxu(a, b, dims):
    return lax.dot_general(a, b, dims, preferred_element_type=jnp.float32)


def query_spans(row_count):
    return [
        (at, max(0, (at - (DOCUMENT_REACH - 1)) // BLOCK * BLOCK), at + BLOCK)
        for at in range(0, row_count, BLOCK)
    ]


def pack_kernel(
    row_count,
    peers,
    len_hbm,
    adapter_hbm,
    slot_hbm,
    down_hbm,
    up_hbm,
    own_ref,
    bias_ref,
    mask_ref,
    len_ref,
    adapter_ref,
    slot_ref,
    sems,
):
    share = down_hbm.shape[0]
    local_slots = slot_hbm.shape[0] // peers
    pairs = (
        (len_hbm, len_ref),
        (adapter_hbm, adapter_ref),
        (slot_hbm, slot_ref),
        (down_hbm, own_ref.at[:share]),
        (up_hbm, own_ref.at[share:]),
    )
    copies = [
        pltpu.make_async_copy(source, target, sems.at[index])
        for index, (source, target) in enumerate(pairs)
    ]
    for copy in copies:
        copy.start()
    for copy in copies[:3]:
        copy.wait()
    lengths = [len_ref[0, index] for index in range(len_ref.shape[1] - 1)]

    token = lax.broadcasted_iota(jnp.int32, (1, row_count), 1)
    adapter = jnp.full((1, row_count), adapter_ref[0, 0], jnp.int32)
    begin = jnp.zeros((1, row_count), jnp.int32)
    end = jnp.int32(0)
    for index, length in enumerate(lengths):
        end = end + length
        adapter = jnp.where(token >= end, adapter_ref[0, index + 1], adapter)
        begin = jnp.where(token >= end, end, begin)
    me = lax.axis_index("dp")
    for distance in range(peers):
        for own in range(local_slots):
            row = distance * local_slots + own
            held = slot_ref[(me ^ distance) * local_slots + own]
            mask_ref[row : row + 1, :] = jnp.where(adapter == held, 1.0, 0.0)
    at = 0
    for first, low, high in query_spans(row_count):
        width = high - low
        query = lax.broadcasted_iota(jnp.int32, (1, BLOCK), 1) + first
        start = begin[:, first : first + BLOCK]
        key = lax.broadcasted_iota(jnp.int32, (width, BLOCK), 0) + low
        bias_ref[at : at + width, :] = jnp.where((key >= start) & (key <= query), 0.0, MASKED)
        at += width
    for copy in copies[3:]:
        copy.wait()


def pack(row_count, peers, lengths, adapters, slots, down, up):
    pair_rows = sum(high - low for _, low, high in query_spans(row_count))
    arrays = [
        pltpu.with_memory_space_constraint(array, pltpu.HBM)
        for array in (lengths, adapters, slots, down, up)
    ]
    return pl.pallas_call(
        functools.partial(pack_kernel, row_count, peers),
        in_specs=[pl.BlockSpec(memory_space=pltpu.HBM)] * 5,
        out_specs=[pl.BlockSpec(memory_space=pltpu.VMEM)] * 3,
        out_shape=[
            jax.ShapeDtypeStruct((2 * down.shape[0], down.shape[1]), down.dtype),
            jax.ShapeDtypeStruct((pair_rows, BLOCK), jnp.float32),
            jax.ShapeDtypeStruct((slots.shape[0], row_count), jnp.float32),
        ],
        scratch_shapes=[
            pltpu.SMEM(lengths.shape, jnp.int32),
            pltpu.SMEM(adapters.shape, jnp.int32),
            pltpu.SMEM(slots.shape, jnp.int32),
            pltpu.SemaphoreType.DMA((5,)),
        ],
        compiler_params=pltpu.CompilerParams(vmem_limit_bytes=VMEM_BYTES),
        cost_estimate=pl.CostEstimate(flops=10**10, bytes_accessed=2**20, transcendentals=0),
        name="pack",
    )(*arrays)


def attention_kernel(
    bias_ref, q_ref, g_ref, k_ref, v_ref, gq_hbm, gk_ref, gv_ref, gq_ref, sems
):
    row_count = q_ref.shape[0]
    groups = k_ref.shape[1] // HEAD_SIZE
    scale = 1.0 / math.sqrt(HEAD_SIZE)
    spans = query_spans(row_count)

    units = []
    for group in range(groups):
        at = 0
        for block, (first, low, high) in enumerate(spans):
            for part in range(0, GROUP_SHARE, UNIT_HEADS):
                heads = [
                    slice(h * HEAD_SIZE, (h + 1) * HEAD_SIZE)
                    for h in range(
                        group * GROUP_SHARE + part, group * GROUP_SHARE + part + UNIT_HEADS
                    )
                ]
                units.append((group, block, heads, slice(first, first + BLOCK), low, high, at))
            at += high - low

    columns = [slice(group * HEAD_SIZE, (group + 1) * HEAD_SIZE) for group in range(groups)]
    key_t = [k_ref[:, column].T for column in columns]
    grad_key = [[None] * len(spans) for _ in range(groups)]
    grad_value = [[None] * len(spans) for _ in range(groups)]
    copies = []

    def products(unit):
        group, _, heads, rows, low, high, _ = unit
        query = jnp.concatenate([q_ref[rows, head] for head in heads], axis=0)
        grad = jnp.concatenate([g_ref[rows, head] for head in heads], axis=0)
        scores = mxu(k_ref[low:high, columns[group]], query, NT)
        grad_weights = mxu(v_ref[low:high, columns[group]], grad, NT)
        return query, grad, scores, grad_weights

    def softmax(unit, query, grad, all_scores, all_grad_weights):
        low, high, at = unit[4:]
        bias = bias_ref[at : at + high - low, :]
        rounded, grad_scores = [], []
        for h in range(UNIT_HEADS):
            part = slice(h * BLOCK, (h + 1) * BLOCK)
            scores = all_scores[:, part] * (scale * LOG2_E) + bias
            grad_weights = all_grad_weights[:, part]
            largest = jnp.max(scores, axis=0, keepdims=True)
            numerator = jnp.exp2(scores - largest)
            weights = numerator * (1.0 / jnp.sum(numerator, axis=0, keepdims=True))
            rounded.append(weights.astype(jnp.bfloat16))
            delta = jnp.sum(rounded[-1].astype(jnp.float32) * grad_weights, axis=0, keepdims=True)
            grad_scores.append((weights * (grad_weights - delta)).astype(jnp.bfloat16))
        return query, grad, jnp.concatenate(rounded, axis=1), jnp.concatenate(grad_scores, axis=1)

    def add(total, terms, low, high):
        for index in range(low // BLOCK, high // BLOCK):
            part = terms[index * BLOCK - low : (index + 1) * BLOCK - low]
            total[index] = part if total[index] is None else total[index] + part

    def gradients(unit, query, grad, rounded, grad_scores):
        group, block, heads, rows, low, high, _ = unit
        grad_query = (mxu(key_t[group][:, low:high], grad_scores, NN) * scale).astype(jnp.bfloat16)
        for h, head in enumerate(heads):
            gq_ref[head, rows] = grad_query[:, h * BLOCK : (h + 1) * BLOCK]
        add(grad_value[group], mxu(rounded, grad, NN), low, high)
        add(grad_key[group], mxu(grad_scores, query, NN), low, high)
        width = GROUP_SHARE * HEAD_SIZE
        if heads[-1].stop == (group + 1) * width:
            done = (slice(group * width, (group + 1) * width), rows)
            copies.append(
                pltpu.make_async_copy(gq_ref.at[done], gq_hbm.at[done], sems.at[len(copies)])
            )
            copies[-1].start()
            if block == len(spans) - 1:
                for index in range(len(spans)):
                    keys = slice(index * BLOCK, (index + 1) * BLOCK)
                    gk_ref[keys, columns[group]] = (grad_key[group][index] * scale).astype(
                        jnp.bfloat16
                    )
                    gv_ref[keys, columns[group]] = grad_value[group][index].astype(jnp.bfloat16)

    ahead, behind = products(units[0]), None
    for index, unit in enumerate(units):
        held = ahead
        if index + 1 < len(units):
            ahead = products(units[index + 1])
        held = softmax(unit, *held)
        if behind is not None:
            gradients(units[index - 1], *behind)
        behind = held
    gradients(units[-1], *behind)
    for copy in copies:
        copy.wait()


def attention_backward(bias, queries, output_gradient, keys, values):
    turned = (queries.shape[1], queries.shape[0])
    chunks = keys.shape[1] // HEAD_SIZE * (queries.shape[0] // BLOCK)
    vmem = pl.BlockSpec(memory_space=pltpu.VMEM)
    return pl.pallas_call(
        attention_kernel,
        in_specs=[vmem] * 5,
        out_specs=[pl.BlockSpec(memory_space=pltpu.HBM), vmem, vmem, vmem],
        out_shape=[
            pltpu.HBM(turned, jnp.bfloat16),
            jax.ShapeDtypeStruct(keys.shape, jnp.bfloat16),
            jax.ShapeDtypeStruct(values.shape, jnp.bfloat16),
            jax.ShapeDtypeStruct(turned, jnp.bfloat16),
        ],
        scratch_shapes=[
            pltpu.SemaphoreType.DMA((chunks,)),
        ],
        compiler_params=pltpu.CompilerParams(vmem_limit_bytes=ATTENTION_VMEM),
        cost_estimate=pl.CostEstimate(
            flops=8 * 10**9, bytes_accessed=8 * 2**20, transcendentals=0
        ),
        name="attention_backward",
    )(bias, queries, output_gradient, keys, values)


def select(wide, mask_ref, rank):
    total = None
    for slot in range(mask_ref.shape[0]):
        part = wide[slot * rank : (slot + 1) * rank] * mask_ref[slot : slot + 1, :]
        total = part if total is None else total + part
    return total


def spread(low, mask_ref):
    return jnp.concatenate(
        [low * mask_ref[slot : slot + 1, :] for slot in range(mask_ref.shape[0])], axis=0
    ).astype(jnp.bfloat16)


def low_kernel(peers, local_slots, mask_ref, x_ref, gq_ref, *refs):
    factors, (out_ref, sent_ref) = refs[:peers], refs[peers:]
    rank = factors[0].shape[0] // (2 * local_slots)
    share = rank * local_slots
    down = jnp.concatenate([ref[:share] for ref in factors], axis=0)
    out_ref[:rank] = select(mxu(down, x_ref[...], NT), mask_ref, rank)
    up = jnp.concatenate([ref[share:] for ref in factors], axis=0)
    total = mxu(up, gq_ref[...], NN)
    out_ref[rank:] = select(total, mask_ref, rank)
    sent_ref[...] = out_ref[...].astype(jnp.bfloat16)


def product_kernel(peers, local_slots, parts, mask_ref, *refs):
    lows, (x_ref, gq_ref), outs = refs[:parts], refs[parts : parts + 2], refs[parts + 2 :]
    low = lows[0][...]
    for ref in lows[1:]:
        low = low + ref[...].astype(jnp.float32)
    rank = low.shape[0] // 2
    share = rank * local_slots
    low = low.astype(jnp.bfloat16).astype(jnp.float32)
    wide_in, wide_grad = spread(low[:rank], mask_ref), spread(low[rank:], mask_ref)
    down = mxu(wide_grad, x_ref[...], NN) * ADAPTER_SCALE
    up = mxu(wide_in, gq_ref[...], NT) * ADAPTER_SCALE
    for distance, ref in enumerate(outs[:peers]):
        rows = slice(distance * share, (distance + 1) * share)
        ref[:share] = down[rows].astype(ref.dtype)
        ref[share:] = up[rows].astype(ref.dtype)
    outs[peers][...] = low[rank:].astype(jnp.bfloat16)


def input_kernel(peers, local_slots, mask_ref, low_ref, *refs):
    factors, out_ref = refs[:peers], refs[peers]
    rank = low_ref.shape[0]
    wide = spread(low_ref[...].astype(jnp.float32), mask_ref)
    down = jnp.concatenate([ref[: rank * local_slots] for ref in factors], axis=0)
    out_ref[...] = (mxu(wide, down, TN) * ADAPTER_SCALE).astype(jnp.bfloat16)


def call(kernel, arrays, out_shape, flops, name):
    return pl.pallas_call(
        kernel,
        in_specs=[pl.BlockSpec(memory_space=pltpu.VMEM)] * len(arrays),
        out_specs=jax.tree.map(lambda _: pl.BlockSpec(memory_space=pltpu.VMEM), out_shape),
        out_shape=out_shape,
        compiler_params=pltpu.CompilerParams(vmem_limit_bytes=VMEM_BYTES),
        cost_estimate=pl.CostEstimate(flops=flops, bytes_accessed=4 * 2**20, transcendentals=0),
        name=name,
    )(*arrays)


def swap(array, axis, distance):
    size = lax.axis_size(axis)
    return lax.ppermute(array, axis, [(i, i ^ distance) for i in range(size)])


def local(
    normed_input,
    rotated_queries,
    rotated_keys,
    value_rows,
    output_gradient,
    document_length,
    document_adapter,
    adapter_in_slot,
    down_weight,
    up_weight,
):
    row_count, width = normed_input.shape
    local_slots, rank, _ = down_weight.shape
    share = local_slots * rank
    peers, parts = lax.axis_size("dp"), lax.axis_size("tensor")
    own, bias, mask = pack(
        row_count,
        peers,
        document_length,
        document_adapter,
        adapter_in_slot,
        down_weight.reshape(share, width),
        up_weight.reshape(share, width),
    )
    factors = [own] + [swap(own, "dp", distance) for distance in range(1, peers)]
    query_gradient, key_gradient, value_gradient, near = attention_backward(
        bias, rotated_queries, output_gradient, rotated_keys, value_rows
    )
    low, low_sent = call(
        functools.partial(low_kernel, peers, local_slots),
        (
            mask,
            normed_input,
            near,
            *factors,
        ),
        [
            jax.ShapeDtypeStruct((2 * rank, row_count), dtype)
            for dtype in (jnp.float32, jnp.bfloat16)
        ],
        10**9,
        "low",
    )
    lows = [low] + [swap(low_sent, "tensor", distance) for distance in range(1, parts)]
    *terms, low_grads = call(
        functools.partial(product_kernel, peers, local_slots, parts),
        (mask, *lows, normed_input, query_gradient),
        [
            jax.ShapeDtypeStruct((2 * share, width), jnp.bfloat16 if distance else jnp.float32)
            for distance in range(peers)
        ]
        + [jax.ShapeDtypeStruct((rank, row_count), jnp.bfloat16)],
        10**9,
        "product",
    )
    received = [swap(terms[distance], "dp", distance) for distance in reversed(range(1, peers))]
    input_gradient = call(
        functools.partial(input_kernel, peers, local_slots),
        (mask, low_grads, *factors),
        jax.ShapeDtypeStruct((row_count, width), jnp.bfloat16),
        10**9,
        "input_gradient",
    )
    total = terms[0]
    for part in received:
        total = total + part.astype(jnp.float32)
    down_gradient = total[:share].reshape(local_slots, rank, width)
    up_gradient = total[share:].reshape(local_slots, rank, width)
    return (input_gradient, key_gradient, value_gradient, down_gradient, up_gradient)


def solution(mesh):
    return jax.shard_map(
        local,
        mesh=mesh,
        in_specs=(
            P(("groups", "dp"), "tensor"),
            P(("groups", "dp"), "tensor"),
            P(("groups", "dp"), "tensor"),
            P(("groups", "dp"), "tensor"),
            P(("groups", "dp"), "tensor"),
            P(("groups", "dp"), None),
            P(("groups", "dp"), None),
            P(),
            P(("groups", "dp"), None, "tensor"),
            P(("groups", "dp"), None, "tensor"),
        ),
        out_specs=(
            P(("groups", "dp"), "tensor"),
            P(("groups", "dp"), "tensor"),
            P(("groups", "dp"), "tensor"),
            P(("groups", "dp"), None, "tensor"),
            P(("groups", "dp"), None, "tensor"),
        ),
        check_vma=False,
    )
```

```python
import functools
import math

import jax
import jax.numpy as jnp
from jax import lax
from jax.experimental import pallas as pl
from jax.experimental.pallas import tpu as pltpu
from jax.sharding import PartitionSpec as P

QUERY_HEAD_COUNT = 64
KEY_VALUE_HEADS = 8
HEAD_SIZE = 128
GROUP_SHARE = QUERY_HEAD_COUNT // KEY_VALUE_HEADS
DOCUMENT_REACH = 256
BLOCK = 128
UNIT_HEADS = 2

MASKED = -1e30
ADAPTER_SCALE = 2.0
LOG2_E = 1.4426950408889634
ATTENTION_VMEM = 24 * 1024 * 1024
VMEM_BYTES = 16 * 1024 * 1024

NN = (((1,), (0,)), ((), ()))
NT = (((1,), (1,)), ((), ()))
TN = (((0,), (0,)), ((), ()))


def mxu(a, b, dims):
    return lax.dot_general(a, b, dims, preferred_element_type=jnp.float32)


def query_spans(row_count):
    return [
        (at, max(0, (at - (DOCUMENT_REACH - 1)) // BLOCK * BLOCK), at + BLOCK)
        for at in range(0, row_count, BLOCK)
    ]


def distances(size):
    return [0, *range(size - 1, 0, -1)]


def pack_kernel(
    row_count,
    peers,
    len_hbm,
    adapter_hbm,
    slot_hbm,
    down_hbm,
    up_hbm,
    own_ref,
    bias_ref,
    mask_ref,
    len_ref,
    adapter_ref,
    slot_ref,
    sems,
):
    share = down_hbm.shape[0]
    local_slots = slot_hbm.shape[0] // peers
    pairs = (
        (len_hbm, len_ref),
        (adapter_hbm, adapter_ref),
        (slot_hbm, slot_ref),
        (down_hbm, own_ref.at[:share]),
        (up_hbm, own_ref.at[share:]),
    )
    copies = [
        pltpu.make_async_copy(source, target, sems.at[index])
        for index, (source, target) in enumerate(pairs)
    ]
    for copy in copies:
        copy.start()
    for copy in copies[:3]:
        copy.wait()
    lengths = [len_ref[0, index] for index in range(len_ref.shape[1] - 1)]

    token = lax.broadcasted_iota(jnp.int32, (1, row_count), 1)
    adapter = jnp.full((1, row_count), adapter_ref[0, 0], jnp.int32)
    begin = jnp.zeros((1, row_count), jnp.int32)
    end = jnp.int32(0)
    for index, length in enumerate(lengths):
        end = end + length
        adapter = jnp.where(token >= end, adapter_ref[0, index + 1], adapter)
        begin = jnp.where(token >= end, end, begin)
    me = lax.axis_index("dp")
    for place, distance in enumerate(distances(peers)):
        for own in range(local_slots):
            row = place * local_slots + own
            held = slot_ref[(me ^ distance) * local_slots + own]
            mask_ref[row : row + 1, :] = jnp.where(adapter == held, 1.0, 0.0)
    at = 0
    for first, low, high in query_spans(row_count):
        width = high - low
        query = lax.broadcasted_iota(jnp.int32, (1, BLOCK), 1) + first
        start = begin[:, first : first + BLOCK]
        key = lax.broadcasted_iota(jnp.int32, (width, BLOCK), 0) + low
        bias_ref[at : at + width, :] = jnp.where((key >= start) & (key <= query), 0.0, MASKED)
        at += width
    for copy in copies[3:]:
        copy.wait()


def pack(row_count, peers, lengths, adapters, slots, down, up):
    pair_rows = sum(high - low for _, low, high in query_spans(row_count))
    arrays = [
        pltpu.with_memory_space_constraint(array, pltpu.HBM)
        for array in (lengths, adapters, slots, down, up)
    ]
    return pl.pallas_call(
        functools.partial(pack_kernel, row_count, peers),
        in_specs=[pl.BlockSpec(memory_space=pltpu.HBM)] * 5,
        out_specs=[pl.BlockSpec(memory_space=pltpu.VMEM)] * 3,
        out_shape=[
            jax.ShapeDtypeStruct((2 * down.shape[0], down.shape[1]), down.dtype),
            jax.ShapeDtypeStruct((pair_rows, BLOCK), jnp.float32),
            jax.ShapeDtypeStruct((slots.shape[0], row_count), jnp.float32),
        ],
        scratch_shapes=[
            pltpu.SMEM(lengths.shape, jnp.int32),
            pltpu.SMEM(adapters.shape, jnp.int32),
            pltpu.SMEM(slots.shape, jnp.int32),
            pltpu.SemaphoreType.DMA((5,)),
        ],
        compiler_params=pltpu.CompilerParams(vmem_limit_bytes=VMEM_BYTES),
        cost_estimate=pl.CostEstimate(flops=10**10, bytes_accessed=2**20, transcendentals=0),
        name="pack",
    )(*arrays)


def attention_kernel(
    bias_ref, q_ref, g_ref, k_ref, v_ref, gq_hbm, gk_ref, gv_ref, gq_ref, sems
):
    row_count = q_ref.shape[0]
    groups = k_ref.shape[1] // HEAD_SIZE
    scale = 1.0 / math.sqrt(HEAD_SIZE)
    spans = query_spans(row_count)

    units = []
    for group in range(groups):
        at = 0
        for block, (first, low, high) in enumerate(spans):
            for part in range(0, GROUP_SHARE, UNIT_HEADS):
                heads = [
                    slice(h * HEAD_SIZE, (h + 1) * HEAD_SIZE)
                    for h in range(
                        group * GROUP_SHARE + part, group * GROUP_SHARE + part + UNIT_HEADS
                    )
                ]
                units.append((group, block, heads, slice(first, first + BLOCK), low, high, at))
            at += high - low

    columns = [slice(group * HEAD_SIZE, (group + 1) * HEAD_SIZE) for group in range(groups)]
    key_t = [k_ref[:, column].T for column in columns]
    grad_key = [[None] * len(spans) for _ in range(groups)]
    grad_value = [[None] * len(spans) for _ in range(groups)]
    copies = []

    def products(unit):
        group, _, heads, rows, low, high, _ = unit
        query = jnp.concatenate([q_ref[rows, head] for head in heads], axis=0)
        grad = jnp.concatenate([g_ref[rows, head] for head in heads], axis=0)
        scores = mxu(k_ref[low:high, columns[group]], query, NT)
        grad_weights = mxu(v_ref[low:high, columns[group]], grad, NT)
        return query, grad, scores, grad_weights

    def softmax(unit, query, grad, all_scores, all_grad_weights):
        low, high, at = unit[4:]
        bias = bias_ref[at : at + high - low, :]
        rounded, grad_scores = [], []
        for h in range(UNIT_HEADS):
            part = slice(h * BLOCK, (h + 1) * BLOCK)
            scores = all_scores[:, part] * (scale * LOG2_E) + bias
            grad_weights = all_grad_weights[:, part]
            largest = jnp.max(scores, axis=0, keepdims=True)
            numerator = jnp.exp2(scores - largest)
            weights = numerator * (1.0 / jnp.sum(numerator, axis=0, keepdims=True))
            rounded.append(weights.astype(jnp.bfloat16))
            delta = jnp.sum(rounded[-1].astype(jnp.float32) * grad_weights, axis=0, keepdims=True)
            grad_scores.append((weights * (grad_weights - delta)).astype(jnp.bfloat16))
        return query, grad, jnp.concatenate(rounded, axis=1), jnp.concatenate(grad_scores, axis=1)

    def add(total, terms, low, high):
        for index in range(low // BLOCK, high // BLOCK):
            part = terms[index * BLOCK - low : (index + 1) * BLOCK - low]
            total[index] = part if total[index] is None else total[index] + part

    def gradients(unit, query, grad, rounded, grad_scores):
        group, block, heads, rows, low, high, _ = unit
        grad_query = (mxu(key_t[group][:, low:high], grad_scores, NN) * scale).astype(jnp.bfloat16)
        for h, head in enumerate(heads):
            gq_ref[head, rows] = grad_query[:, h * BLOCK : (h + 1) * BLOCK]
        add(grad_value[group], mxu(rounded, grad, NN), low, high)
        add(grad_key[group], mxu(grad_scores, query, NN), low, high)
        width = GROUP_SHARE * HEAD_SIZE
        if heads[-1].stop == (group + 1) * width:
            done = (slice(group * width, (group + 1) * width), rows)
            copies.append(
                pltpu.make_async_copy(gq_ref.at[done], gq_hbm.at[done], sems.at[len(copies)])
            )
            copies[-1].start()
            if block == len(spans) - 1:
                for index in range(len(spans)):
                    keys = slice(index * BLOCK, (index + 1) * BLOCK)
                    gk_ref[keys, columns[group]] = (grad_key[group][index] * scale).astype(
                        jnp.bfloat16
                    )
                    gv_ref[keys, columns[group]] = grad_value[group][index].astype(jnp.bfloat16)

    ahead, behind = products(units[0]), None
    for index, unit in enumerate(units):
        held = ahead
        if index + 1 < len(units):
            ahead = products(units[index + 1])
        held = softmax(unit, *held)
        if behind is not None:
            gradients(units[index - 1], *behind)
        behind = held
    gradients(units[-1], *behind)
    for copy in copies:
        copy.wait()


def attention_backward(bias, queries, output_gradient, keys, values):
    turned = (queries.shape[1], queries.shape[0])
    chunks = keys.shape[1] // HEAD_SIZE * (queries.shape[0] // BLOCK)
    vmem = pl.BlockSpec(memory_space=pltpu.VMEM)
    return pl.pallas_call(
        attention_kernel,
        in_specs=[vmem] * 5,
        out_specs=[pl.BlockSpec(memory_space=pltpu.HBM), vmem, vmem, vmem],
        out_shape=[
            pltpu.HBM(turned, jnp.bfloat16),
            jax.ShapeDtypeStruct(keys.shape, jnp.bfloat16),
            jax.ShapeDtypeStruct(values.shape, jnp.bfloat16),
            jax.ShapeDtypeStruct(turned, jnp.bfloat16),
        ],
        scratch_shapes=[
            pltpu.SemaphoreType.DMA((chunks,)),
        ],
        compiler_params=pltpu.CompilerParams(vmem_limit_bytes=ATTENTION_VMEM),
        cost_estimate=pl.CostEstimate(
            flops=8 * 10**9, bytes_accessed=8 * 2**20, transcendentals=0
        ),
        name="attention_backward",
    )(bias, queries, output_gradient, keys, values)


def select(wide, mask_ref, rank):
    total = None
    for slot in range(mask_ref.shape[0]):
        part = wide[slot * rank : (slot + 1) * rank] * mask_ref[slot : slot + 1, :]
        total = part if total is None else total + part
    return total


def spread(low, mask_ref):
    return jnp.concatenate(
        [low * mask_ref[slot : slot + 1, :] for slot in range(mask_ref.shape[0])], axis=0
    ).astype(jnp.bfloat16)


def low_kernel(peers, local_slots, mask_ref, x_ref, gq_ref, *refs):
    factors, (out_ref, sent_ref) = refs[:peers], refs[peers:]
    rank = factors[0].shape[0] // (2 * local_slots)
    share = rank * local_slots
    down = jnp.concatenate([ref[:share] for ref in factors], axis=0)
    out_ref[:rank] = select(mxu(down, x_ref[...], NT), mask_ref, rank)
    up = jnp.concatenate([ref[share:] for ref in factors], axis=0)
    total = mxu(up, gq_ref[...], NN)
    out_ref[rank:] = select(total, mask_ref, rank)
    sent_ref[...] = out_ref[...].astype(jnp.bfloat16)


def product_kernel(peers, local_slots, parts, mask_ref, *refs):
    lows, (x_ref, gq_ref), outs = refs[:parts], refs[parts : parts + 2], refs[parts + 2 :]
    low = lows[0][...]
    for ref in lows[1:]:
        low = low + ref[...].astype(jnp.float32)
    rank = low.shape[0] // 2
    share = rank * local_slots
    low = low.astype(jnp.bfloat16).astype(jnp.float32)
    wide_in, wide_grad = spread(low[:rank], mask_ref), spread(low[rank:], mask_ref)
    down = mxu(wide_grad, x_ref[...], NN) * ADAPTER_SCALE
    up = mxu(wide_in, gq_ref[...], NT) * ADAPTER_SCALE
    for place, ref in enumerate(outs[:peers]):
        rows = slice(place * share, (place + 1) * share)
        ref[:share] = down[rows].astype(ref.dtype)
        ref[share:] = up[rows].astype(ref.dtype)
    outs[peers][...] = low[rank:].astype(jnp.bfloat16)


def input_kernel(peers, local_slots, mask_ref, low_ref, *refs):
    factors, out_ref = refs[:peers], refs[peers]
    rank = low_ref.shape[0]
    wide = spread(low_ref[...].astype(jnp.float32), mask_ref)
    down = jnp.concatenate([ref[: rank * local_slots] for ref in factors], axis=0)
    out_ref[...] = (mxu(wide, down, TN) * ADAPTER_SCALE).astype(jnp.bfloat16)


def call(kernel, arrays, out_shape, flops, name):
    return pl.pallas_call(
        kernel,
        in_specs=[pl.BlockSpec(memory_space=pltpu.VMEM)] * len(arrays),
        out_specs=jax.tree.map(lambda _: pl.BlockSpec(memory_space=pltpu.VMEM), out_shape),
        out_shape=out_shape,
        compiler_params=pltpu.CompilerParams(vmem_limit_bytes=VMEM_BYTES),
        cost_estimate=pl.CostEstimate(flops=flops, bytes_accessed=4 * 2**20, transcendentals=0),
        name=name,
    )(*arrays)


def swap(array, axis, distance):
    size = lax.axis_size(axis)
    return lax.ppermute(array, axis, [(i, i ^ distance) for i in range(size)])


def local(
    normed_input,
    rotated_queries,
    rotated_keys,
    value_rows,
    output_gradient,
    document_length,
    document_adapter,
    adapter_in_slot,
    down_weight,
    up_weight,
):
    row_count, width = normed_input.shape
    local_slots, rank, _ = down_weight.shape
    share = local_slots * rank
    peers, parts = lax.axis_size("dp"), lax.axis_size("tensor")
    own, bias, mask = pack(
        row_count,
        peers,
        document_length,
        document_adapter,
        adapter_in_slot,
        down_weight.reshape(share, width),
        up_weight.reshape(share, width),
    )
    factors = [own] + [swap(own, "dp", distance) for distance in distances(peers)[1:]]
    query_gradient, key_gradient, value_gradient, near = attention_backward(
        bias, rotated_queries, output_gradient, rotated_keys, value_rows
    )
    low, low_sent = call(
        functools.partial(low_kernel, peers, local_slots),
        (
            mask,
            normed_input,
            near,
            *factors,
        ),
        [
            jax.ShapeDtypeStruct((2 * rank, row_count), dtype)
            for dtype in (jnp.float32, jnp.bfloat16)
        ],
        10**9,
        "low",
    )
    lows = [low] + [swap(low_sent, "tensor", distance) for distance in distances(parts)[1:]]
    *terms, low_grads = call(
        functools.partial(product_kernel, peers, local_slots, parts),
        (mask, *lows, normed_input, query_gradient),
        [
            jax.ShapeDtypeStruct((2 * share, width), jnp.bfloat16 if place else jnp.float32)
            for place in range(peers)
        ]
        + [jax.ShapeDtypeStruct((rank, row_count), jnp.bfloat16)],
        10**9,
        "product",
    )
    received = [
        swap(part, "dp", distance) for distance, part in zip(distances(peers)[1:], terms[1:])
    ]
    input_gradient = call(
        functools.partial(input_kernel, peers, local_slots),
        (mask, low_grads, *factors),
        jax.ShapeDtypeStruct((row_count, width), jnp.bfloat16),
        10**9,
        "input_gradient",
    )
    total = terms[0]
    for part in received[::-1]:
        total = total + part.astype(jnp.float32)
    down_gradient = total[:share].reshape(local_slots, rank, width)
    up_gradient = total[share:].reshape(local_slots, rank, width)
    return (input_gradient, key_gradient, value_gradient, down_gradient, up_gradient)


def solution(mesh):
    return jax.shard_map(
        local,
        mesh=mesh,
        in_specs=(
            P(("groups", "dp"), "tensor"),
            P(("groups", "dp"), "tensor"),
            P(("groups", "dp"), "tensor"),
            P(("groups", "dp"), "tensor"),
            P(("groups", "dp"), "tensor"),
            P(("groups", "dp"), None),
            P(("groups", "dp"), None),
            P(),
            P(("groups", "dp"), None, "tensor"),
            P(("groups", "dp"), None, "tensor"),
        ),
        out_specs=(
            P(("groups", "dp"), "tensor"),
            P(("groups", "dp"), "tensor"),
            P(("groups", "dp"), "tensor"),
            P(("groups", "dp"), None, "tensor"),
            P(("groups", "dp"), None, "tensor"),
        ),
        check_vma=False,
    )
```

```python
import functools
import math

import jax
import jax.numpy as jnp
from jax import lax
from jax.experimental import pallas as pl
from jax.experimental.pallas import tpu as pltpu
from jax.sharding import PartitionSpec as P

QUERY_HEAD_COUNT = 64
KEY_VALUE_HEADS = 8
HEAD_SIZE = 128
GROUP_SHARE = QUERY_HEAD_COUNT // KEY_VALUE_HEADS
DOCUMENT_REACH = 256
BLOCK = 128
UNIT_HEADS = 2

MASKED = -1e30
ADAPTER_SCALE = 2.0
LOG2_E = 1.4426950408889634
ATTENTION_VMEM = 24 * 1024 * 1024
VMEM_BYTES = 16 * 1024 * 1024

NN = (((1,), (0,)), ((), ()))
NT = (((1,), (1,)), ((), ()))
TN = (((0,), (0,)), ((), ()))


def mxu(a, b, dims):
    return lax.dot_general(a, b, dims, preferred_element_type=jnp.float32)


def query_spans(row_count):
    return [
        (at, max(0, (at - (DOCUMENT_REACH - 1)) // BLOCK * BLOCK), at + BLOCK)
        for at in range(0, row_count, BLOCK)
    ]


def distances(size):
    return [0, *range(size - 1, 0, -1)]


def pack_kernel(
    row_count,
    peers,
    len_hbm,
    adapter_hbm,
    slot_hbm,
    down_hbm,
    up_hbm,
    own_ref,
    bias_ref,
    mask_ref,
    len_ref,
    adapter_ref,
    slot_ref,
    sems,
):
    share = down_hbm.shape[0]
    local_slots = slot_hbm.shape[0] // peers
    pairs = (
        (len_hbm, len_ref),
        (adapter_hbm, adapter_ref),
        (slot_hbm, slot_ref),
        (down_hbm, own_ref.at[:share]),
        (up_hbm, own_ref.at[share:]),
    )
    copies = [
        pltpu.make_async_copy(source, target, sems.at[index])
        for index, (source, target) in enumerate(pairs)
    ]
    for copy in copies:
        copy.start()
    for copy in copies[:3]:
        copy.wait()
    lengths = [len_ref[0, index] for index in range(len_ref.shape[1] - 1)]

    token = lax.broadcasted_iota(jnp.int32, (1, row_count), 1)
    adapter = jnp.full((1, row_count), adapter_ref[0, 0], jnp.int32)
    begin = jnp.zeros((1, row_count), jnp.int32)
    end = jnp.int32(0)
    for index, length in enumerate(lengths):
        end = end + length
        adapter = jnp.where(token >= end, adapter_ref[0, index + 1], adapter)
        begin = jnp.where(token >= end, end, begin)
    me = lax.axis_index("dp")
    for place, distance in enumerate(distances(peers)):
        for own in range(local_slots):
            row = place * local_slots + own
            held = slot_ref[(me ^ distance) * local_slots + own]
            mask_ref[row : row + 1, :] = jnp.where(adapter == held, 1.0, 0.0)
    at = 0
    for first, low, high in query_spans(row_count):
        width = high - low
        query = lax.broadcasted_iota(jnp.int32, (1, BLOCK), 1) + first
        start = begin[:, first : first + BLOCK]
        key = lax.broadcasted_iota(jnp.int32, (width, BLOCK), 0) + low
        bias_ref[at : at + width, :] = jnp.where((key >= start) & (key <= query), 0.0, MASKED)
        at += width
    for copy in copies[3:]:
        copy.wait()


def pack(row_count, peers, lengths, adapters, slots, down, up):
    pair_rows = sum(high - low for _, low, high in query_spans(row_count))
    arrays = [
        pltpu.with_memory_space_constraint(array, pltpu.HBM)
        for array in (lengths, adapters, slots, down, up)
    ]
    return pl.pallas_call(
        functools.partial(pack_kernel, row_count, peers),
        in_specs=[pl.BlockSpec(memory_space=pltpu.HBM)] * 5,
        out_specs=[pl.BlockSpec(memory_space=pltpu.VMEM)] * 3,
        out_shape=[
            jax.ShapeDtypeStruct((2 * down.shape[0], down.shape[1]), down.dtype),
            jax.ShapeDtypeStruct((pair_rows, BLOCK), jnp.float32),
            jax.ShapeDtypeStruct((slots.shape[0], row_count), jnp.float32),
        ],
        scratch_shapes=[
            pltpu.SMEM(lengths.shape, jnp.int32),
            pltpu.SMEM(adapters.shape, jnp.int32),
            pltpu.SMEM(slots.shape, jnp.int32),
            pltpu.SemaphoreType.DMA((5,)),
        ],
        compiler_params=pltpu.CompilerParams(vmem_limit_bytes=VMEM_BYTES),
        cost_estimate=pl.CostEstimate(flops=10**10, bytes_accessed=2**20, transcendentals=0),
        name="pack",
    )(*arrays)


def attention_kernel(
    bias_ref, q_ref, g_ref, k_ref, v_ref, gq_hbm, gk_ref, gv_ref, gq_ref, sems
):
    row_count = q_ref.shape[0]
    groups = k_ref.shape[1] // HEAD_SIZE
    scale = 1.0 / math.sqrt(HEAD_SIZE)
    spans = query_spans(row_count)

    units = []
    for group in range(groups):
        at = 0
        for block, (first, low, high) in enumerate(spans):
            for part in range(0, GROUP_SHARE, UNIT_HEADS):
                heads = [
                    slice(h * HEAD_SIZE, (h + 1) * HEAD_SIZE)
                    for h in range(
                        group * GROUP_SHARE + part, group * GROUP_SHARE + part + UNIT_HEADS
                    )
                ]
                units.append((group, block, heads, slice(first, first + BLOCK), low, high, at))
            at += high - low

    columns = [slice(group * HEAD_SIZE, (group + 1) * HEAD_SIZE) for group in range(groups)]
    key_t = [k_ref[:, column].T for column in columns]
    grad_key = [[None] * len(spans) for _ in range(groups)]
    grad_value = [[None] * len(spans) for _ in range(groups)]
    copies = []

    def products(unit):
        group, _, heads, rows, low, high, _ = unit
        query = jnp.concatenate([q_ref[rows, head] for head in heads], axis=0)
        grad = jnp.concatenate([g_ref[rows, head] for head in heads], axis=0)
        scores = mxu(k_ref[low:high, columns[group]], query, NT)
        grad_weights = mxu(v_ref[low:high, columns[group]], grad, NT)
        return query, grad, scores, grad_weights

    def softmax(unit, query, grad, all_scores, all_grad_weights):
        low, high, at = unit[4:]
        bias = bias_ref[at : at + high - low, :]
        rounded, grad_scores = [], []
        for h in range(UNIT_HEADS):
            part = slice(h * BLOCK, (h + 1) * BLOCK)
            scores = all_scores[:, part] * (scale * LOG2_E) + bias
            grad_weights = all_grad_weights[:, part]
            largest = jnp.max(scores, axis=0, keepdims=True)
            numerator = jnp.exp2(scores - largest)
            weights = numerator * (1.0 / jnp.sum(numerator, axis=0, keepdims=True))
            rounded.append(weights.astype(jnp.bfloat16))
            delta = jnp.sum(rounded[-1].astype(jnp.float32) * grad_weights, axis=0, keepdims=True)
            grad_scores.append((weights * (grad_weights - delta)).astype(jnp.bfloat16))
        return query, grad, jnp.concatenate(rounded, axis=1), jnp.concatenate(grad_scores, axis=1)

    def add(total, terms, low, high):
        for index in range(low // BLOCK, high // BLOCK):
            part = terms[index * BLOCK - low : (index + 1) * BLOCK - low]
            total[index] = part if total[index] is None else total[index] + part

    def gradients(unit, query, grad, rounded, grad_scores):
        group, block, heads, rows, low, high, _ = unit
        grad_query = (mxu(key_t[group][:, low:high], grad_scores, NN) * scale).astype(jnp.bfloat16)
        for h, head in enumerate(heads):
            gq_ref[head, rows] = grad_query[:, h * BLOCK : (h + 1) * BLOCK]
        add(grad_value[group], mxu(rounded, grad, NN), low, high)
        add(grad_key[group], mxu(grad_scores, query, NN), low, high)
        width = GROUP_SHARE * HEAD_SIZE
        if heads[-1].stop == (group + 1) * width:
            done = (slice(group * width, (group + 1) * width), rows)
            copies.append(
                pltpu.make_async_copy(gq_ref.at[done], gq_hbm.at[done], sems.at[len(copies)])
            )
            copies[-1].start()
            if block == len(spans) - 1:
                for index in range(len(spans)):
                    keys = slice(index * BLOCK, (index + 1) * BLOCK)
                    gk_ref[keys, columns[group]] = (grad_key[group][index] * scale).astype(
                        jnp.bfloat16
                    )
                    gv_ref[keys, columns[group]] = grad_value[group][index].astype(jnp.bfloat16)

    ahead, behind = products(units[0]), None
    for index, unit in enumerate(units):
        held = ahead
        if index + 1 < len(units):
            ahead = products(units[index + 1])
        held = softmax(unit, *held)
        if behind is not None:
            gradients(units[index - 1], *behind)
        behind = held
    gradients(units[-1], *behind)
    for copy in copies:
        copy.wait()


def attention_backward(bias, queries, output_gradient, keys, values):
    turned = (queries.shape[1], queries.shape[0])
    chunks = keys.shape[1] // HEAD_SIZE * (queries.shape[0] // BLOCK)
    vmem = pl.BlockSpec(memory_space=pltpu.VMEM)
    return pl.pallas_call(
        attention_kernel,
        in_specs=[vmem] * 5,
        out_specs=[pl.BlockSpec(memory_space=pltpu.HBM), vmem, vmem, vmem],
        out_shape=[
            pltpu.HBM(turned, jnp.bfloat16),
            jax.ShapeDtypeStruct(keys.shape, jnp.bfloat16),
            jax.ShapeDtypeStruct(values.shape, jnp.bfloat16),
            jax.ShapeDtypeStruct(turned, jnp.bfloat16),
        ],
        scratch_shapes=[
            pltpu.SemaphoreType.DMA((chunks,)),
        ],
        compiler_params=pltpu.CompilerParams(vmem_limit_bytes=ATTENTION_VMEM),
        cost_estimate=pl.CostEstimate(
            flops=8 * 10**9, bytes_accessed=8 * 2**20, transcendentals=0
        ),
        name="attention_backward",
    )(bias, queries, output_gradient, keys, values)


def select(wide, mask_ref, rank):
    total = None
    for slot in range(mask_ref.shape[0]):
        part = wide[slot * rank : (slot + 1) * rank] * mask_ref[slot : slot + 1, :]
        total = part if total is None else total + part
    return total


def spread(low, mask_ref):
    return jnp.concatenate(
        [low * mask_ref[slot : slot + 1, :] for slot in range(mask_ref.shape[0])], axis=0
    ).astype(jnp.bfloat16)


def low_kernel(peers, local_slots, mask_ref, x_ref, gq_ref, *refs):
    factors, (out_ref, sent_ref) = refs[:peers], refs[peers:]
    rank = factors[0].shape[0] // (2 * local_slots)
    share = rank * local_slots
    down = jnp.concatenate([ref[:share] for ref in factors], axis=0)
    out_ref[:rank] = select(mxu(down, x_ref[...], NT), mask_ref, rank)
    up = jnp.concatenate([ref[share:] for ref in factors], axis=0)
    total = mxu(up, gq_ref[...], NN)
    out_ref[rank:] = select(total, mask_ref, rank)
    sent_ref[...] = out_ref[...].astype(jnp.bfloat16)


def relayed(peers):
    return [distance for distance in distances(peers)[1:] if distance % 2 and distance > 1]


def product_kernel(peers, local_slots, parts, mask_ref, *refs):
    lows, (x_ref, gq_ref), outs = refs[:parts], refs[parts : parts + 2], refs[parts + 2 :]
    low = lows[0][...]
    for ref in lows[1:]:
        low = low + ref[...].astype(jnp.float32)
    rank = low.shape[0] // 2
    share = rank * local_slots
    low = low.astype(jnp.bfloat16).astype(jnp.float32)
    wide_in, wide_grad = spread(low[:rank], mask_ref), spread(low[rank:], mask_ref)
    up = mxu(wide_in, gq_ref[...], NT) * ADAPTER_SCALE
    down = mxu(wide_grad, x_ref[...], NN) * ADAPTER_SCALE
    place = {distance: index for index, distance in enumerate(distances(peers))}
    rows = {
        distance: slice(index * share, (index + 1) * share) for distance, index in place.items()
    }
    own_ref, near_ref, low_ref, relay_ref, kept_ref, *far_refs = outs
    own_ref[:share], own_ref[share:] = down[rows[0]], up[rows[0]]
    near_ref[:share] = down[rows[1]].astype(jnp.bfloat16)
    near_ref[share:] = up[rows[1]].astype(jnp.bfloat16)
    low_ref[...] = low[rank:].astype(jnp.bfloat16)
    for index, distance in enumerate(relayed(peers)):
        part = slice(index * share, (index + 1) * share)
        relay_ref[part] = up[rows[distance]].astype(jnp.bfloat16)
        kept_ref[part] = up[rows[distance ^ 1]]
    for distance, ref in zip(distances(peers)[1:-1], far_refs):
        ref[...] = down[rows[distance]].astype(jnp.bfloat16)


def input_kernel(peers, local_slots, mask_ref, low_ref, *refs):
    factors, out_ref = refs[:peers], refs[peers]
    rank = low_ref.shape[0]
    wide = spread(low_ref[...].astype(jnp.float32), mask_ref)
    down = jnp.concatenate([ref[: rank * local_slots] for ref in factors], axis=0)
    out_ref[...] = (mxu(wide, down, TN) * ADAPTER_SCALE).astype(jnp.bfloat16)


def call(kernel, arrays, out_shape, flops, name):
    return pl.pallas_call(
        kernel,
        in_specs=[pl.BlockSpec(memory_space=pltpu.VMEM)] * len(arrays),
        out_specs=jax.tree.map(lambda _: pl.BlockSpec(memory_space=pltpu.VMEM), out_shape),
        out_shape=out_shape,
        compiler_params=pltpu.CompilerParams(vmem_limit_bytes=VMEM_BYTES),
        cost_estimate=pl.CostEstimate(flops=flops, bytes_accessed=4 * 2**20, transcendentals=0),
        name=name,
    )(*arrays)


def swap(array, axis, distance):
    size = lax.axis_size(axis)
    return lax.ppermute(array, axis, [(i, i ^ distance) for i in range(size)])


def local(
    normed_input,
    rotated_queries,
    rotated_keys,
    value_rows,
    output_gradient,
    document_length,
    document_adapter,
    adapter_in_slot,
    down_weight,
    up_weight,
):
    row_count, width = normed_input.shape
    local_slots, rank, _ = down_weight.shape
    share = local_slots * rank
    peers, parts = lax.axis_size("dp"), lax.axis_size("tensor")
    own, bias, mask = pack(
        row_count,
        peers,
        document_length,
        document_adapter,
        adapter_in_slot,
        down_weight.reshape(share, width),
        up_weight.reshape(share, width),
    )
    factors = [own] + [swap(own, "dp", distance) for distance in distances(peers)[1:]]
    query_gradient, key_gradient, value_gradient, near = attention_backward(
        bias, rotated_queries, output_gradient, rotated_keys, value_rows
    )
    low, low_sent = call(
        functools.partial(low_kernel, peers, local_slots),
        (
            mask,
            normed_input,
            near,
            *factors,
        ),
        [
            jax.ShapeDtypeStruct((2 * rank, row_count), dtype)
            for dtype in (jnp.float32, jnp.bfloat16)
        ],
        10**9,
        "low",
    )
    lows = [low] + [swap(low_sent, "tensor", distance) for distance in distances(parts)[1:]]
    relays = relayed(peers)
    far = distances(peers)[1:-1]
    own_terms, near_terms, low_grads, relay, kept, *far_terms = call(
        functools.partial(product_kernel, peers, local_slots, parts),
        (mask, *lows, normed_input, query_gradient),
        [
            jax.ShapeDtypeStruct((2 * share, width), jnp.float32),
            jax.ShapeDtypeStruct((2 * share, width), jnp.bfloat16),
            jax.ShapeDtypeStruct((rank, row_count), jnp.bfloat16),
            jax.ShapeDtypeStruct((len(relays) * share, width), jnp.bfloat16),
            jax.ShapeDtypeStruct((len(relays) * share, width), jnp.float32),
        ]
        + [jax.ShapeDtypeStruct((share, width), jnp.bfloat16)] * len(far),
        10**9,
        "product",
    )
    relay = swap(relay, "dp", 1)
    far_terms = [swap(part, "dp", distance) for distance, part in zip(far, far_terms)]
    relay, near_terms = lax.optimization_barrier((relay, near_terms))
    near_terms = swap(near_terms, "dp", 1)
    paired = (kept + relay.astype(jnp.float32)).astype(jnp.bfloat16)
    paired = [
        swap(paired[index * share : (index + 1) * share], "dp", distance ^ 1)
        for index, distance in enumerate(relays)
    ]
    input_gradient = call(
        functools.partial(input_kernel, peers, local_slots),
        (mask, low_grads, *factors),
        jax.ShapeDtypeStruct((row_count, width), jnp.bfloat16),
        10**9,
        "input_gradient",
    )
    down_gradient = own_terms[:share] + near_terms[:share].astype(jnp.float32)
    up_gradient = own_terms[share:] + near_terms[share:].astype(jnp.float32)
    for part in far_terms[::-1]:
        down_gradient = down_gradient + part.astype(jnp.float32)
    for part in paired:
        up_gradient = up_gradient + part.astype(jnp.float32)
    down_gradient = down_gradient.reshape(local_slots, rank, width)
    up_gradient = up_gradient.reshape(local_slots, rank, width)
    return (input_gradient, key_gradient, value_gradient, down_gradient, up_gradient)


def solution(mesh):
    return jax.shard_map(
        local,
        mesh=mesh,
        in_specs=(
            P(("groups", "dp"), "tensor"),
            P(("groups", "dp"), "tensor"),
            P(("groups", "dp"), "tensor"),
            P(("groups", "dp"), "tensor"),
            P(("groups", "dp"), "tensor"),
            P(("groups", "dp"), None),
            P(("groups", "dp"), None),
            P(),
            P(("groups", "dp"), None, "tensor"),
            P(("groups", "dp"), None, "tensor"),
        ),
        out_specs=(
            P(("groups", "dp"), "tensor"),
            P(("groups", "dp"), "tensor"),
            P(("groups", "dp"), "tensor"),
            P(("groups", "dp"), None, "tensor"),
            P(("groups", "dp"), None, "tensor"),
        ),
        check_vma=False,
    )
```

```python
import functools
import math

import jax
import jax.numpy as jnp
from jax import lax
from jax.experimental import pallas as pl
from jax.experimental.pallas import tpu as pltpu
from jax.sharding import PartitionSpec as P

QUERY_HEAD_COUNT = 64
KEY_VALUE_HEADS = 8
HEAD_SIZE = 128
GROUP_SHARE = QUERY_HEAD_COUNT // KEY_VALUE_HEADS
DOCUMENT_REACH = 256
BLOCK = 128
UNIT_HEADS = 2

MASKED = -1e30
ADAPTER_SCALE = 2.0
LOG2_E = 1.4426950408889634
ATTENTION_VMEM = 24 * 1024 * 1024
VMEM_BYTES = 16 * 1024 * 1024

NN = (((1,), (0,)), ((), ()))
NT = (((1,), (1,)), ((), ()))
TN = (((0,), (0,)), ((), ()))


def mxu(a, b, dims):
    return lax.dot_general(a, b, dims, preferred_element_type=jnp.float32)


def query_spans(row_count):
    return [
        (at, max(0, (at - (DOCUMENT_REACH - 1)) // BLOCK * BLOCK), at + BLOCK)
        for at in range(0, row_count, BLOCK)
    ]


def distances(size):
    return [0, *range(size - 1, 0, -1)]


def pack_kernel(
    row_count,
    peers,
    len_hbm,
    adapter_hbm,
    slot_hbm,
    down_hbm,
    up_hbm,
    own_ref,
    bias_ref,
    mask_ref,
    len_ref,
    adapter_ref,
    slot_ref,
    sems,
):
    share = down_hbm.shape[0]
    local_slots = slot_hbm.shape[0] // peers
    pairs = (
        (len_hbm, len_ref),
        (adapter_hbm, adapter_ref),
        (slot_hbm, slot_ref),
        (down_hbm, own_ref.at[:share]),
        (up_hbm, own_ref.at[share:]),
    )
    copies = [
        pltpu.make_async_copy(source, target, sems.at[index])
        for index, (source, target) in enumerate(pairs)
    ]
    for copy in copies:
        copy.start()
    for copy in copies[:3]:
        copy.wait()
    lengths = [len_ref[0, index] for index in range(len_ref.shape[1] - 1)]

    token = lax.broadcasted_iota(jnp.int32, (1, row_count), 1)
    adapter = jnp.full((1, row_count), adapter_ref[0, 0], jnp.int32)
    begin = jnp.zeros((1, row_count), jnp.int32)
    end = jnp.int32(0)
    for index, length in enumerate(lengths):
        end = end + length
        adapter = jnp.where(token >= end, adapter_ref[0, index + 1], adapter)
        begin = jnp.where(token >= end, end, begin)
    me = lax.axis_index("dp")
    for place, distance in enumerate(distances(peers)):
        for own in range(local_slots):
            row = place * local_slots + own
            held = slot_ref[(me ^ distance) * local_slots + own]
            mask_ref[row : row + 1, :] = jnp.where(adapter == held, 1.0, 0.0)
    at = 0
    for first, low, high in query_spans(row_count):
        width = high - low
        query = lax.broadcasted_iota(jnp.int32, (1, BLOCK), 1) + first
        start = begin[:, first : first + BLOCK]
        key = lax.broadcasted_iota(jnp.int32, (width, BLOCK), 0) + low
        bias_ref[at : at + width, :] = jnp.where((key >= start) & (key <= query), 0.0, MASKED)
        at += width
    for copy in copies[3:]:
        copy.wait()


def pack(row_count, peers, lengths, adapters, slots, down, up):
    pair_rows = sum(high - low for _, low, high in query_spans(row_count))
    arrays = [
        pltpu.with_memory_space_constraint(array, pltpu.HBM)
        for array in (lengths, adapters, slots, down, up)
    ]
    return pl.pallas_call(
        functools.partial(pack_kernel, row_count, peers),
        in_specs=[pl.BlockSpec(memory_space=pltpu.HBM)] * 5,
        out_specs=[pl.BlockSpec(memory_space=pltpu.VMEM)] * 3,
        out_shape=[
            jax.ShapeDtypeStruct((2 * down.shape[0], down.shape[1]), down.dtype),
            jax.ShapeDtypeStruct((pair_rows, BLOCK), jnp.float32),
            jax.ShapeDtypeStruct((slots.shape[0], row_count), jnp.float32),
        ],
        scratch_shapes=[
            pltpu.SMEM(lengths.shape, jnp.int32),
            pltpu.SMEM(adapters.shape, jnp.int32),
            pltpu.SMEM(slots.shape, jnp.int32),
            pltpu.SemaphoreType.DMA((5,)),
        ],
        compiler_params=pltpu.CompilerParams(vmem_limit_bytes=VMEM_BYTES),
        cost_estimate=pl.CostEstimate(flops=10**10, bytes_accessed=2**20, transcendentals=0),
        name="pack",
    )(*arrays)


def attention_kernel(
    bias_ref, q_ref, g_ref, k_ref, v_ref, gq_hbm, gk_ref, gv_ref, gq_ref, sems
):
    row_count = q_ref.shape[0]
    groups = k_ref.shape[1] // HEAD_SIZE
    scale = 1.0 / math.sqrt(HEAD_SIZE)
    spans = query_spans(row_count)

    units = []
    for group in range(groups):
        at = 0
        for block, (first, low, high) in enumerate(spans):
            for part in range(0, GROUP_SHARE, UNIT_HEADS):
                heads = [
                    slice(h * HEAD_SIZE, (h + 1) * HEAD_SIZE)
                    for h in range(
                        group * GROUP_SHARE + part, group * GROUP_SHARE + part + UNIT_HEADS
                    )
                ]
                units.append((group, block, heads, slice(first, first + BLOCK), low, high, at))
            at += high - low

    columns = [slice(group * HEAD_SIZE, (group + 1) * HEAD_SIZE) for group in range(groups)]
    key_t = [k_ref[:, column].T for column in columns]
    grad_key = [[None] * len(spans) for _ in range(groups)]
    grad_value = [[None] * len(spans) for _ in range(groups)]
    copies = []

    def products(unit):
        group, _, heads, rows, low, high, _ = unit
        query = jnp.concatenate([q_ref[rows, head] for head in heads], axis=0)
        grad = jnp.concatenate([g_ref[rows, head] for head in heads], axis=0)
        scores = mxu(k_ref[low:high, columns[group]], query, NT)
        grad_weights = mxu(v_ref[low:high, columns[group]], grad, NT)
        return query, grad, scores, grad_weights

    def softmax(unit, query, grad, all_scores, all_grad_weights):
        low, high, at = unit[4:]
        bias = bias_ref[at : at + high - low, :]
        rounded, grad_scores = [], []
        for h in range(UNIT_HEADS):
            part = slice(h * BLOCK, (h + 1) * BLOCK)
            scores = all_scores[:, part] * (scale * LOG2_E) + bias
            grad_weights = all_grad_weights[:, part]
            largest = jnp.max(scores, axis=0, keepdims=True)
            numerator = jnp.exp2(scores - largest)
            weights = numerator * (1.0 / jnp.sum(numerator, axis=0, keepdims=True))
            rounded.append(weights.astype(jnp.bfloat16))
            delta = jnp.sum(rounded[-1].astype(jnp.float32) * grad_weights, axis=0, keepdims=True)
            grad_scores.append((weights * (grad_weights - delta)).astype(jnp.bfloat16))
        return query, grad, jnp.concatenate(rounded, axis=1), jnp.concatenate(grad_scores, axis=1)

    def add(total, terms, low, high):
        for index in range(low // BLOCK, high // BLOCK):
            part = terms[index * BLOCK - low : (index + 1) * BLOCK - low]
            total[index] = part if total[index] is None else total[index] + part

    def gradients(unit, query, grad, rounded, grad_scores):
        group, block, heads, rows, low, high, _ = unit
        grad_query = (mxu(key_t[group][:, low:high], grad_scores, NN) * scale).astype(jnp.bfloat16)
        for h, head in enumerate(heads):
            gq_ref[head, rows] = grad_query[:, h * BLOCK : (h + 1) * BLOCK]
        add(grad_value[group], mxu(rounded, grad, NN), low, high)
        add(grad_key[group], mxu(grad_scores, query, NN), low, high)
        width = GROUP_SHARE * HEAD_SIZE
        if heads[-1].stop == (group + 1) * width:
            done = (slice(group * width, (group + 1) * width), rows)
            copies.append(
                pltpu.make_async_copy(gq_ref.at[done], gq_hbm.at[done], sems.at[len(copies)])
            )
            copies[-1].start()
            if block == len(spans) - 1:
                for index in range(len(spans)):
                    keys = slice(index * BLOCK, (index + 1) * BLOCK)
                    gk_ref[keys, columns[group]] = (grad_key[group][index] * scale).astype(
                        jnp.bfloat16
                    )
                    gv_ref[keys, columns[group]] = grad_value[group][index].astype(jnp.bfloat16)

    ahead, behind = products(units[0]), None
    for index, unit in enumerate(units):
        held = ahead
        if index + 1 < len(units):
            ahead = products(units[index + 1])
        held = softmax(unit, *held)
        if behind is not None:
            gradients(units[index - 1], *behind)
        behind = held
    gradients(units[-1], *behind)
    for copy in copies:
        copy.wait()


def attention_backward(bias, queries, output_gradient, keys, values):
    turned = (queries.shape[1], queries.shape[0])
    chunks = keys.shape[1] // HEAD_SIZE * (queries.shape[0] // BLOCK)
    vmem = pl.BlockSpec(memory_space=pltpu.VMEM)
    return pl.pallas_call(
        attention_kernel,
        in_specs=[vmem] * 5,
        out_specs=[pl.BlockSpec(memory_space=pltpu.HBM), vmem, vmem, vmem],
        out_shape=[
            pltpu.HBM(turned, jnp.bfloat16),
            jax.ShapeDtypeStruct(keys.shape, jnp.bfloat16),
            jax.ShapeDtypeStruct(values.shape, jnp.bfloat16),
            jax.ShapeDtypeStruct(turned, jnp.bfloat16),
        ],
        scratch_shapes=[
            pltpu.SemaphoreType.DMA((chunks,)),
        ],
        compiler_params=pltpu.CompilerParams(vmem_limit_bytes=ATTENTION_VMEM),
        cost_estimate=pl.CostEstimate(
            flops=8 * 10**9, bytes_accessed=8 * 2**20, transcendentals=0
        ),
        name="attention_backward",
    )(bias, queries, output_gradient, keys, values)


def select(wide, mask_ref, rank):
    total = None
    for slot in range(mask_ref.shape[0]):
        part = wide[slot * rank : (slot + 1) * rank] * mask_ref[slot : slot + 1, :]
        total = part if total is None else total + part
    return total


def spread(low, mask_ref):
    return jnp.concatenate(
        [low * mask_ref[slot : slot + 1, :] for slot in range(mask_ref.shape[0])], axis=0
    ).astype(jnp.bfloat16)


def low_kernel(peers, local_slots, mask_ref, x_ref, gq_ref, *refs):
    factors, (out_ref, sent_ref) = refs[:peers], refs[peers:]
    rank = factors[0].shape[0] // (2 * local_slots)
    share = rank * local_slots
    down = jnp.concatenate([ref[:share] for ref in factors], axis=0)
    out_ref[:rank] = select(mxu(down, x_ref[...], NT), mask_ref, rank)
    up = jnp.concatenate([ref[share:] for ref in factors], axis=0)
    total = mxu(up, gq_ref[...], NN)
    out_ref[rank:] = select(total, mask_ref, rank)
    sent_ref[...] = out_ref[...].astype(jnp.bfloat16)


def relayed(peers):
    return [distance for distance in distances(peers)[1:] if distance % 2 and distance > 1]


def product_kernel(peers, local_slots, parts, mask_ref, *refs):
    lows, (x_ref, gq_ref), outs = refs[:parts], refs[parts : parts + 2], refs[parts + 2 :]
    low = lows[0][...]
    for ref in lows[1:]:
        low = low + ref[...].astype(jnp.float32)
    rank = low.shape[0] // 2
    share = rank * local_slots
    low = low.astype(jnp.bfloat16).astype(jnp.float32)
    wide_in, wide_grad = spread(low[:rank], mask_ref), spread(low[rank:], mask_ref)
    up = mxu(wide_in, gq_ref[...], NT) * ADAPTER_SCALE
    down = mxu(wide_grad, x_ref[...], NN) * ADAPTER_SCALE
    place = {distance: index for index, distance in enumerate(distances(peers))}
    rows = {
        distance: slice(index * share, (index + 1) * share) for distance, index in place.items()
    }
    own_ref, near_ref, low_ref, relay_ref, kept_ref, *far_refs = outs
    own_ref[:share], own_ref[share:] = down[rows[0]], up[rows[0]]
    near_ref[:share] = down[rows[1]].astype(jnp.bfloat16)
    near_ref[share:] = up[rows[1]].astype(jnp.bfloat16)
    low_ref[...] = low[rank:].astype(jnp.bfloat16)
    for index, distance in enumerate(relayed(peers)):
        part = slice(index * share, (index + 1) * share)
        relay_ref[part] = up[rows[distance]].astype(jnp.bfloat16)
        kept_ref[part] = up[rows[distance ^ 1]]
    for distance, ref in zip(distances(peers)[1:-1], far_refs):
        ref[...] = down[rows[distance]].astype(jnp.bfloat16)


def input_kernel(peers, local_slots, mask_ref, low_ref, *refs):
    factors, out_ref = refs[:peers], refs[peers]
    rank = low_ref.shape[0]
    wide = spread(low_ref[...].astype(jnp.float32), mask_ref)
    down = jnp.concatenate([ref[: rank * local_slots] for ref in factors], axis=0)
    out_ref[...] = (mxu(wide, down, TN) * ADAPTER_SCALE).astype(jnp.bfloat16)


def call(kernel, arrays, out_shape, flops, name):
    return pl.pallas_call(
        kernel,
        in_specs=[pl.BlockSpec(memory_space=pltpu.VMEM)] * len(arrays),
        out_specs=jax.tree.map(lambda _: pl.BlockSpec(memory_space=pltpu.VMEM), out_shape),
        out_shape=out_shape,
        compiler_params=pltpu.CompilerParams(vmem_limit_bytes=VMEM_BYTES),
        cost_estimate=pl.CostEstimate(flops=flops, bytes_accessed=4 * 2**20, transcendentals=0),
        name=name,
    )(*arrays)


def swap(array, axis, distance):
    size = lax.axis_size(axis)
    return lax.ppermute(array, axis, [(i, i ^ distance) for i in range(size)])


def local(
    normed_input,
    rotated_queries,
    rotated_keys,
    value_rows,
    output_gradient,
    document_length,
    document_adapter,
    adapter_in_slot,
    down_weight,
    up_weight,
):
    row_count, width = normed_input.shape
    local_slots, rank, _ = down_weight.shape
    share = local_slots * rank
    peers, parts = lax.axis_size("dp"), lax.axis_size("tensor")
    own, bias, mask = pack(
        row_count,
        peers,
        document_length,
        document_adapter,
        adapter_in_slot,
        down_weight.reshape(share, width),
        up_weight.reshape(share, width),
    )
    factors = [own] + [swap(own, "dp", distance) for distance in distances(peers)[1:]]
    query_gradient, key_gradient, value_gradient, near = attention_backward(
        bias, rotated_queries, output_gradient, rotated_keys, value_rows
    )
    low, low_sent = call(
        functools.partial(low_kernel, peers, local_slots),
        (
            mask,
            normed_input,
            near,
            *factors,
        ),
        [
            jax.ShapeDtypeStruct((2 * rank, row_count), dtype)
            for dtype in (jnp.float32, jnp.bfloat16)
        ],
        10**9,
        "low",
    )
    lows = [low] + [swap(low_sent, "tensor", distance) for distance in distances(parts)[1:]]
    relays = relayed(peers)
    far = distances(peers)[1:-1]
    own_terms, near_terms, low_grads, relay, kept, *far_terms = call(
        functools.partial(product_kernel, peers, local_slots, parts),
        (mask, *lows, normed_input, query_gradient),
        [
            jax.ShapeDtypeStruct((2 * share, width), jnp.float32),
            jax.ShapeDtypeStruct((2 * share, width), jnp.bfloat16),
            jax.ShapeDtypeStruct((rank, row_count), jnp.bfloat16),
            jax.ShapeDtypeStruct((len(relays) * share, width), jnp.bfloat16),
            jax.ShapeDtypeStruct((len(relays) * share, width), jnp.float32),
        ]
        + [jax.ShapeDtypeStruct((share, width), jnp.bfloat16)] * len(far),
        10**9,
        "product",
    )
    relay = swap(relay, "dp", 1)
    far_terms = [swap(part, "dp", distance) for distance, part in zip(far, far_terms)]
    near_terms = swap(near_terms, "dp", 1)
    paired = (kept + relay.astype(jnp.float32)).astype(jnp.bfloat16)
    paired = [
        swap(paired[index * share : (index + 1) * share], "dp", distance ^ 1)
        for index, distance in enumerate(relays)
    ]
    input_gradient = call(
        functools.partial(input_kernel, peers, local_slots),
        (mask, low_grads, *factors),
        jax.ShapeDtypeStruct((row_count, width), jnp.bfloat16),
        10**9,
        "input_gradient",
    )
    down_gradient, up_gradient = own_terms[:share], own_terms[share:]
    for part in far_terms[::-1]:
        down_gradient = down_gradient + part.astype(jnp.float32)
    for part in paired:
        up_gradient = up_gradient + part.astype(jnp.float32)
    down_gradient = down_gradient + near_terms[:share].astype(jnp.float32)
    up_gradient = up_gradient + near_terms[share:].astype(jnp.float32)
    down_gradient = down_gradient.reshape(local_slots, rank, width)
    up_gradient = up_gradient.reshape(local_slots, rank, width)
    return (input_gradient, key_gradient, value_gradient, down_gradient, up_gradient)


def solution(mesh):
    return jax.shard_map(
        local,
        mesh=mesh,
        in_specs=(
            P(("groups", "dp"), "tensor"),
            P(("groups", "dp"), "tensor"),
            P(("groups", "dp"), "tensor"),
            P(("groups", "dp"), "tensor"),
            P(("groups", "dp"), "tensor"),
            P(("groups", "dp"), None),
            P(("groups", "dp"), None),
            P(),
            P(("groups", "dp"), None, "tensor"),
            P(("groups", "dp"), None, "tensor"),
        ),
        out_specs=(
            P(("groups", "dp"), "tensor"),
            P(("groups", "dp"), "tensor"),
            P(("groups", "dp"), "tensor"),
            P(("groups", "dp"), None, "tensor"),
            P(("groups", "dp"), None, "tensor"),
        ),
        check_vma=False,
    )
```

```python
import functools
import math

import jax
import jax.numpy as jnp
from jax import lax
from jax.experimental import pallas as pl
from jax.experimental.pallas import tpu as pltpu
from jax.sharding import PartitionSpec as P

QUERY_HEAD_COUNT = 64
KEY_VALUE_HEADS = 8
HEAD_SIZE = 128
GROUP_SHARE = QUERY_HEAD_COUNT // KEY_VALUE_HEADS
DOCUMENT_REACH = 256
BLOCK = 128
UNIT_HEADS = 2

MASKED = -1e30
ADAPTER_SCALE = 2.0
LOG2_E = 1.4426950408889634
ATTENTION_VMEM = 24 * 1024 * 1024
VMEM_BYTES = 16 * 1024 * 1024

NN = (((1,), (0,)), ((), ()))
NT = (((1,), (1,)), ((), ()))
TN = (((0,), (0,)), ((), ()))


def mxu(a, b, dims):
    return lax.dot_general(a, b, dims, preferred_element_type=jnp.float32)


def query_spans(row_count):
    return [
        (at, max(0, (at - (DOCUMENT_REACH - 1)) // BLOCK * BLOCK), at + BLOCK)
        for at in range(0, row_count, BLOCK)
    ]


def distances(size):
    return [0, *range(size - 1, 0, -1)]


def pack_kernel(
    row_count,
    peers,
    len_hbm,
    adapter_hbm,
    slot_hbm,
    down_hbm,
    up_hbm,
    own_ref,
    bias_ref,
    mask_ref,
    len_ref,
    adapter_ref,
    slot_ref,
    sems,
):
    share = down_hbm.shape[0]
    local_slots = slot_hbm.shape[0] // peers
    pairs = (
        (len_hbm, len_ref),
        (adapter_hbm, adapter_ref),
        (slot_hbm, slot_ref),
        (down_hbm, own_ref.at[:share]),
        (up_hbm, own_ref.at[share:]),
    )
    copies = [
        pltpu.make_async_copy(source, target, sems.at[index])
        for index, (source, target) in enumerate(pairs)
    ]
    for copy in copies:
        copy.start()
    for copy in copies[:3]:
        copy.wait()
    lengths = [len_ref[0, index] for index in range(len_ref.shape[1] - 1)]

    token = lax.broadcasted_iota(jnp.int32, (1, row_count), 1)
    adapter = jnp.full((1, row_count), adapter_ref[0, 0], jnp.int32)
    begin = jnp.zeros((1, row_count), jnp.int32)
    end = jnp.int32(0)
    for index, length in enumerate(lengths):
        end = end + length
        adapter = jnp.where(token >= end, adapter_ref[0, index + 1], adapter)
        begin = jnp.where(token >= end, end, begin)
    me = lax.axis_index("dp")
    for place, distance in enumerate(distances(peers)):
        for own in range(local_slots):
            row = place * local_slots + own
            held = slot_ref[(me ^ distance) * local_slots + own]
            mask_ref[row : row + 1, :] = jnp.where(adapter == held, 1.0, 0.0)
    at = 0
    for first, low, high in query_spans(row_count):
        width = high - low
        query = lax.broadcasted_iota(jnp.int32, (1, BLOCK), 1) + first
        start = begin[:, first : first + BLOCK]
        key = lax.broadcasted_iota(jnp.int32, (width, BLOCK), 0) + low
        bias_ref[at : at + width, :] = jnp.where((key >= start) & (key <= query), 0.0, MASKED)
        at += width
    for copy in copies[3:]:
        copy.wait()


def pack(row_count, peers, lengths, adapters, slots, down, up):
    pair_rows = sum(high - low for _, low, high in query_spans(row_count))
    arrays = [
        pltpu.with_memory_space_constraint(array, pltpu.HBM)
        for array in (lengths, adapters, slots, down, up)
    ]
    return pl.pallas_call(
        functools.partial(pack_kernel, row_count, peers),
        in_specs=[pl.BlockSpec(memory_space=pltpu.HBM)] * 5,
        out_specs=[pl.BlockSpec(memory_space=pltpu.VMEM)] * 3,
        out_shape=[
            jax.ShapeDtypeStruct((2 * down.shape[0], down.shape[1]), down.dtype),
            jax.ShapeDtypeStruct((pair_rows, BLOCK), jnp.float32),
            jax.ShapeDtypeStruct((slots.shape[0], row_count), jnp.float32),
        ],
        scratch_shapes=[
            pltpu.SMEM(lengths.shape, jnp.int32),
            pltpu.SMEM(adapters.shape, jnp.int32),
            pltpu.SMEM(slots.shape, jnp.int32),
            pltpu.SemaphoreType.DMA((5,)),
        ],
        compiler_params=pltpu.CompilerParams(vmem_limit_bytes=VMEM_BYTES),
        cost_estimate=pl.CostEstimate(flops=10**10, bytes_accessed=2**20, transcendentals=0),
        name="pack",
    )(*arrays)


def attention_kernel(
    bias_ref, q_ref, g_ref, k_ref, v_ref, gq_hbm, gk_ref, gv_ref, gq_ref, sems
):
    row_count = q_ref.shape[0]
    groups = k_ref.shape[1] // HEAD_SIZE
    scale = 1.0 / math.sqrt(HEAD_SIZE)
    spans = query_spans(row_count)

    units = []
    for group in range(groups):
        at = 0
        for block, (first, low, high) in enumerate(spans):
            for part in range(0, GROUP_SHARE, UNIT_HEADS):
                heads = [
                    slice(h * HEAD_SIZE, (h + 1) * HEAD_SIZE)
                    for h in range(
                        group * GROUP_SHARE + part, group * GROUP_SHARE + part + UNIT_HEADS
                    )
                ]
                units.append((group, block, heads, slice(first, first + BLOCK), low, high, at))
            at += high - low

    columns = [slice(group * HEAD_SIZE, (group + 1) * HEAD_SIZE) for group in range(groups)]
    key_t = [k_ref[:, column].T for column in columns]
    grad_key = [[None] * len(spans) for _ in range(groups)]
    grad_value = [[None] * len(spans) for _ in range(groups)]
    copies = []

    def products(unit):
        group, _, heads, rows, low, high, _ = unit
        query = jnp.concatenate([q_ref[rows, head] for head in heads], axis=0)
        grad = jnp.concatenate([g_ref[rows, head] for head in heads], axis=0)
        scores = mxu(k_ref[low:high, columns[group]], query, NT)
        grad_weights = mxu(v_ref[low:high, columns[group]], grad, NT)
        return query, grad, scores, grad_weights

    def softmax(unit, query, grad, all_scores, all_grad_weights):
        low, high, at = unit[4:]
        bias = bias_ref[at : at + high - low, :]
        rounded, grad_scores = [], []
        for h in range(UNIT_HEADS):
            part = slice(h * BLOCK, (h + 1) * BLOCK)
            scores = all_scores[:, part] * (scale * LOG2_E) + bias
            grad_weights = all_grad_weights[:, part]
            largest = jnp.max(scores, axis=0, keepdims=True)
            numerator = jnp.exp2(scores - largest)
            weights = numerator * (1.0 / jnp.sum(numerator, axis=0, keepdims=True))
            rounded.append(weights.astype(jnp.bfloat16))
            delta = jnp.sum(rounded[-1].astype(jnp.float32) * grad_weights, axis=0, keepdims=True)
            grad_scores.append((weights * (grad_weights - delta)).astype(jnp.bfloat16))
        return query, grad, jnp.concatenate(rounded, axis=1), jnp.concatenate(grad_scores, axis=1)

    def add(total, terms, low, high):
        for index in range(low // BLOCK, high // BLOCK):
            part = terms[index * BLOCK - low : (index + 1) * BLOCK - low]
            total[index] = part if total[index] is None else total[index] + part

    def gradients(unit, query, grad, rounded, grad_scores):
        group, block, heads, rows, low, high, _ = unit
        grad_query = (mxu(key_t[group][:, low:high], grad_scores, NN) * scale).astype(jnp.bfloat16)
        for h, head in enumerate(heads):
            gq_ref[head, rows] = grad_query[:, h * BLOCK : (h + 1) * BLOCK]
        add(grad_value[group], mxu(rounded, grad, NN), low, high)
        add(grad_key[group], mxu(grad_scores, query, NN), low, high)
        width = GROUP_SHARE * HEAD_SIZE
        if heads[-1].stop == (group + 1) * width:
            done = (slice(group * width, (group + 1) * width), rows)
            copies.append(
                pltpu.make_async_copy(gq_ref.at[done], gq_hbm.at[done], sems.at[len(copies)])
            )
            copies[-1].start()
            if block == len(spans) - 1:
                for index in range(len(spans)):
                    keys = slice(index * BLOCK, (index + 1) * BLOCK)
                    gk_ref[keys, columns[group]] = (grad_key[group][index] * scale).astype(
                        jnp.bfloat16
                    )
                    gv_ref[keys, columns[group]] = grad_value[group][index].astype(jnp.bfloat16)

    ahead, behind = products(units[0]), None
    for index, unit in enumerate(units):
        held = ahead
        if index + 1 < len(units):
            ahead = products(units[index + 1])
        held = softmax(unit, *held)
        if behind is not None:
            gradients(units[index - 1], *behind)
        behind = held
    gradients(units[-1], *behind)
    for copy in copies:
        copy.wait()


def attention_backward(bias, queries, output_gradient, keys, values):
    turned = (queries.shape[1], queries.shape[0])
    chunks = keys.shape[1] // HEAD_SIZE * (queries.shape[0] // BLOCK)
    vmem = pl.BlockSpec(memory_space=pltpu.VMEM)
    return pl.pallas_call(
        attention_kernel,
        in_specs=[vmem] * 5,
        out_specs=[pl.BlockSpec(memory_space=pltpu.HBM), vmem, vmem, vmem],
        out_shape=[
            pltpu.HBM(turned, jnp.bfloat16),
            jax.ShapeDtypeStruct(keys.shape, jnp.bfloat16),
            jax.ShapeDtypeStruct(values.shape, jnp.bfloat16),
            jax.ShapeDtypeStruct(turned, jnp.bfloat16),
        ],
        scratch_shapes=[
            pltpu.SemaphoreType.DMA((chunks,)),
        ],
        compiler_params=pltpu.CompilerParams(vmem_limit_bytes=ATTENTION_VMEM),
        cost_estimate=pl.CostEstimate(
            flops=8 * 10**9, bytes_accessed=8 * 2**20, transcendentals=0
        ),
        name="attention_backward",
    )(bias, queries, output_gradient, keys, values)


def select(wide, mask_ref, rank):
    total = None
    for slot in range(mask_ref.shape[0]):
        part = wide[slot * rank : (slot + 1) * rank] * mask_ref[slot : slot + 1, :]
        total = part if total is None else total + part
    return total


def spread(low, mask_ref):
    return jnp.concatenate(
        [low * mask_ref[slot : slot + 1, :] for slot in range(mask_ref.shape[0])], axis=0
    ).astype(jnp.bfloat16)


def low_kernel(peers, local_slots, mask_ref, x_ref, gq_ref, *refs):
    factors, (out_ref, sent_ref) = refs[:peers], refs[peers:]
    rank = factors[0].shape[0] // (2 * local_slots)
    share = rank * local_slots
    down = jnp.concatenate([ref[:share] for ref in factors], axis=0)
    out_ref[:rank] = select(mxu(down, x_ref[...], NT), mask_ref, rank)
    up = jnp.concatenate([ref[share:] for ref in factors], axis=0)
    total = mxu(up, gq_ref[...], NN)
    out_ref[rank:] = select(total, mask_ref, rank)
    sent_ref[...] = out_ref[...].astype(jnp.bfloat16)


def relayed(peers):
    return [distance for distance in distances(peers)[1:] if distance % 2 and distance > 1]


def product_kernel(peers, local_slots, parts, mask_ref, *refs):
    lows, (x_ref, gq_ref), outs = refs[:parts], refs[parts : parts + 2], refs[parts + 2 :]
    low = lows[0][...]
    for ref in lows[1:]:
        low = low + ref[...].astype(jnp.float32)
    rank = low.shape[0] // 2
    share = rank * local_slots
    low = low.astype(jnp.bfloat16).astype(jnp.float32)
    wide_in, wide_grad = spread(low[:rank], mask_ref), spread(low[rank:], mask_ref)
    up = mxu(wide_in, gq_ref[...], NT) * ADAPTER_SCALE
    down = mxu(wide_grad, x_ref[...], NN) * ADAPTER_SCALE
    place = {distance: index for index, distance in enumerate(distances(peers))}
    rows = {
        distance: slice(index * share, (index + 1) * share) for distance, index in place.items()
    }
    own_ref, near_down_ref, near_up_ref, low_ref, relay_ref, kept_ref, *far_refs = outs
    own_ref[:share], own_ref[share:] = down[rows[0]], up[rows[0]]
    near_down_ref[...] = down[rows[1]].astype(jnp.bfloat16)
    near_up_ref[...] = up[rows[1]].astype(jnp.bfloat16)
    low_ref[...] = low[rank:].astype(jnp.bfloat16)
    for index, distance in enumerate(relayed(peers)):
        part = slice(index * share, (index + 1) * share)
        relay_ref[part] = up[rows[distance]].astype(jnp.bfloat16)
        kept_ref[part] = up[rows[distance ^ 1]]
    for distance, ref in zip(distances(peers)[1:-1], far_refs):
        ref[...] = down[rows[distance]].astype(jnp.bfloat16)


def input_kernel(peers, local_slots, mask_ref, low_ref, *refs):
    factors, out_ref = refs[:peers], refs[peers]
    rank = low_ref.shape[0]
    wide = spread(low_ref[...].astype(jnp.float32), mask_ref)
    down = jnp.concatenate([ref[: rank * local_slots] for ref in factors], axis=0)
    out_ref[...] = (mxu(wide, down, TN) * ADAPTER_SCALE).astype(jnp.bfloat16)


def call(kernel, arrays, out_shape, flops, name):
    return pl.pallas_call(
        kernel,
        in_specs=[pl.BlockSpec(memory_space=pltpu.VMEM)] * len(arrays),
        out_specs=jax.tree.map(lambda _: pl.BlockSpec(memory_space=pltpu.VMEM), out_shape),
        out_shape=out_shape,
        compiler_params=pltpu.CompilerParams(vmem_limit_bytes=VMEM_BYTES),
        cost_estimate=pl.CostEstimate(flops=flops, bytes_accessed=4 * 2**20, transcendentals=0),
        name=name,
    )(*arrays)


def swap(array, axis, distance):
    size = lax.axis_size(axis)
    return lax.ppermute(array, axis, [(i, i ^ distance) for i in range(size)])


def local(
    normed_input,
    rotated_queries,
    rotated_keys,
    value_rows,
    output_gradient,
    document_length,
    document_adapter,
    adapter_in_slot,
    down_weight,
    up_weight,
):
    row_count, width = normed_input.shape
    local_slots, rank, _ = down_weight.shape
    share = local_slots * rank
    peers, parts = lax.axis_size("dp"), lax.axis_size("tensor")
    own, bias, mask = pack(
        row_count,
        peers,
        document_length,
        document_adapter,
        adapter_in_slot,
        down_weight.reshape(share, width),
        up_weight.reshape(share, width),
    )
    factors = [own] + [swap(own, "dp", distance) for distance in distances(peers)[1:]]
    query_gradient, key_gradient, value_gradient, near = attention_backward(
        bias, rotated_queries, output_gradient, rotated_keys, value_rows
    )
    low, low_sent = call(
        functools.partial(low_kernel, peers, local_slots),
        (
            mask,
            normed_input,
            near,
            *factors,
        ),
        [
            jax.ShapeDtypeStruct((2 * rank, row_count), dtype)
            for dtype in (jnp.float32, jnp.bfloat16)
        ],
        10**9,
        "low",
    )
    lows = [low] + [swap(low_sent, "tensor", distance) for distance in distances(parts)[1:]]
    relays = relayed(peers)
    far = distances(peers)[1:-1]
    own_terms, near_down, near_up, low_grads, relay, kept, *far_terms = call(
        functools.partial(product_kernel, peers, local_slots, parts),
        (mask, *lows, normed_input, query_gradient),
        [
            jax.ShapeDtypeStruct((2 * share, width), jnp.float32),
            jax.ShapeDtypeStruct((share, width), jnp.bfloat16),
            jax.ShapeDtypeStruct((share, width), jnp.bfloat16),
            jax.ShapeDtypeStruct((rank, row_count), jnp.bfloat16),
            jax.ShapeDtypeStruct((len(relays) * share, width), jnp.bfloat16),
            jax.ShapeDtypeStruct((len(relays) * share, width), jnp.float32),
        ]
        + [jax.ShapeDtypeStruct((share, width), jnp.bfloat16)] * len(far),
        10**9,
        "product",
    )
    relay = swap(relay, "dp", 1)
    far_terms = [swap(part, "dp", distance) for distance, part in zip(far, far_terms)]
    relay, near_down, near_up = lax.optimization_barrier((relay, near_down, near_up))
    near_down, near_up = swap(near_down, "dp", 1), swap(near_up, "dp", 1)
    paired = (kept + relay.astype(jnp.float32)).astype(jnp.bfloat16)
    paired = [
        swap(paired[index * share : (index + 1) * share], "dp", distance ^ 1)
        for index, distance in enumerate(relays)
    ]
    input_gradient = call(
        functools.partial(input_kernel, peers, local_slots),
        (mask, low_grads, *factors),
        jax.ShapeDtypeStruct((row_count, width), jnp.bfloat16),
        10**9,
        "input_gradient",
    )
    down_gradient = own_terms[:share] + near_down.astype(jnp.float32)
    up_gradient = own_terms[share:] + near_up.astype(jnp.float32)
    for part in far_terms[::-1]:
        down_gradient = down_gradient + part.astype(jnp.float32)
    for part in paired:
        up_gradient = up_gradient + part.astype(jnp.float32)
    down_gradient = down_gradient.reshape(local_slots, rank, width)
    up_gradient = up_gradient.reshape(local_slots, rank, width)
    return (input_gradient, key_gradient, value_gradient, down_gradient, up_gradient)


def solution(mesh):
    return jax.shard_map(
        local,
        mesh=mesh,
        in_specs=(
            P(("groups", "dp"), "tensor"),
            P(("groups", "dp"), "tensor"),
            P(("groups", "dp"), "tensor"),
            P(("groups", "dp"), "tensor"),
            P(("groups", "dp"), "tensor"),
            P(("groups", "dp"), None),
            P(("groups", "dp"), None),
            P(),
            P(("groups", "dp"), None, "tensor"),
            P(("groups", "dp"), None, "tensor"),
        ),
        out_specs=(
            P(("groups", "dp"), "tensor"),
            P(("groups", "dp"), "tensor"),
            P(("groups", "dp"), "tensor"),
            P(("groups", "dp"), None, "tensor"),
            P(("groups", "dp"), None, "tensor"),
        ),
        check_vma=False,
    )
```

```python
import functools
import math

import jax
import jax.numpy as jnp
from jax import lax
from jax.experimental import pallas as pl
from jax.experimental.pallas import tpu as pltpu
from jax.sharding import PartitionSpec as P

QUERY_HEAD_COUNT = 64
KEY_VALUE_HEADS = 8
HEAD_SIZE = 128
GROUP_SHARE = QUERY_HEAD_COUNT // KEY_VALUE_HEADS
DOCUMENT_REACH = 256
BLOCK = 128
UNIT_HEADS = 2

MASKED = -1e30
ADAPTER_SCALE = 2.0
LOG2_E = 1.4426950408889634
ATTENTION_VMEM = 24 * 1024 * 1024
VMEM_BYTES = 16 * 1024 * 1024

NN = (((1,), (0,)), ((), ()))
NT = (((1,), (1,)), ((), ()))
TN = (((0,), (0,)), ((), ()))


def mxu(a, b, dims):
    return lax.dot_general(a, b, dims, preferred_element_type=jnp.float32)


def query_spans(row_count):
    return [
        (at, max(0, (at - (DOCUMENT_REACH - 1)) // BLOCK * BLOCK), at + BLOCK)
        for at in range(0, row_count, BLOCK)
    ]


def distances(size):
    return [0, *range(size - 1, 0, -1)]


def pack_kernel(
    row_count,
    peers,
    len_hbm,
    adapter_hbm,
    slot_hbm,
    down_hbm,
    up_hbm,
    own_ref,
    bias_ref,
    mask_ref,
    len_ref,
    adapter_ref,
    slot_ref,
    sems,
):
    share = down_hbm.shape[0]
    local_slots = slot_hbm.shape[0] // peers
    pairs = (
        (len_hbm, len_ref),
        (adapter_hbm, adapter_ref),
        (slot_hbm, slot_ref),
        (down_hbm, own_ref.at[:share]),
        (up_hbm, own_ref.at[share:]),
    )
    copies = [
        pltpu.make_async_copy(source, target, sems.at[index])
        for index, (source, target) in enumerate(pairs)
    ]
    for copy in copies:
        copy.start()
    for copy in copies[:3]:
        copy.wait()
    lengths = [len_ref[0, index] for index in range(len_ref.shape[1] - 1)]

    token = lax.broadcasted_iota(jnp.int32, (1, row_count), 1)
    adapter = jnp.full((1, row_count), adapter_ref[0, 0], jnp.int32)
    begin = jnp.zeros((1, row_count), jnp.int32)
    end = jnp.int32(0)
    for index, length in enumerate(lengths):
        end = end + length
        adapter = jnp.where(token >= end, adapter_ref[0, index + 1], adapter)
        begin = jnp.where(token >= end, end, begin)
    me = lax.axis_index("dp")
    for place, distance in enumerate(distances(peers)):
        for own in range(local_slots):
            row = place * local_slots + own
            held = slot_ref[(me ^ distance) * local_slots + own]
            mask_ref[row : row + 1, :] = jnp.where(adapter == held, 1.0, 0.0)
    at = 0
    for first, low, high in query_spans(row_count):
        width = high - low
        query = lax.broadcasted_iota(jnp.int32, (1, BLOCK), 1) + first
        start = begin[:, first : first + BLOCK]
        key = lax.broadcasted_iota(jnp.int32, (width, BLOCK), 0) + low
        bias_ref[at : at + width, :] = jnp.where((key >= start) & (key <= query), 0.0, MASKED)
        at += width
    for copy in copies[3:]:
        copy.wait()


def pack(row_count, peers, lengths, adapters, slots, down, up):
    pair_rows = sum(high - low for _, low, high in query_spans(row_count))
    arrays = [
        pltpu.with_memory_space_constraint(array, pltpu.HBM)
        for array in (lengths, adapters, slots, down, up)
    ]
    return pl.pallas_call(
        functools.partial(pack_kernel, row_count, peers),
        in_specs=[pl.BlockSpec(memory_space=pltpu.HBM)] * 5,
        out_specs=[pl.BlockSpec(memory_space=pltpu.VMEM)] * 3,
        out_shape=[
            jax.ShapeDtypeStruct((2 * down.shape[0], down.shape[1]), down.dtype),
            jax.ShapeDtypeStruct((pair_rows, BLOCK), jnp.float32),
            jax.ShapeDtypeStruct((slots.shape[0], row_count), jnp.float32),
        ],
        scratch_shapes=[
            pltpu.SMEM(lengths.shape, jnp.int32),
            pltpu.SMEM(adapters.shape, jnp.int32),
            pltpu.SMEM(slots.shape, jnp.int32),
            pltpu.SemaphoreType.DMA((5,)),
        ],
        compiler_params=pltpu.CompilerParams(vmem_limit_bytes=VMEM_BYTES),
        cost_estimate=pl.CostEstimate(flops=10**10, bytes_accessed=2**20, transcendentals=0),
        name="pack",
    )(*arrays)


def attention_kernel(
    bias_ref, q_ref, g_ref, k_ref, v_ref, gq_hbm, gk_ref, gv_ref, gq_ref, sems
):
    row_count = q_ref.shape[0]
    groups = k_ref.shape[1] // HEAD_SIZE
    scale = 1.0 / math.sqrt(HEAD_SIZE)
    spans = query_spans(row_count)

    units = []
    for group in range(groups):
        at = 0
        for block, (first, low, high) in enumerate(spans):
            for part in range(0, GROUP_SHARE, UNIT_HEADS):
                heads = [
                    slice(h * HEAD_SIZE, (h + 1) * HEAD_SIZE)
                    for h in range(
                        group * GROUP_SHARE + part, group * GROUP_SHARE + part + UNIT_HEADS
                    )
                ]
                units.append((group, block, heads, slice(first, first + BLOCK), low, high, at))
            at += high - low

    columns = [slice(group * HEAD_SIZE, (group + 1) * HEAD_SIZE) for group in range(groups)]
    key_t = [k_ref[:, column].T for column in columns]
    grad_key = [[None] * len(spans) for _ in range(groups)]
    grad_value = [[None] * len(spans) for _ in range(groups)]
    copies = []

    def products(unit):
        group, _, heads, rows, low, high, _ = unit
        query = jnp.concatenate([q_ref[rows, head] for head in heads], axis=0)
        grad = jnp.concatenate([g_ref[rows, head] for head in heads], axis=0)
        scores = mxu(k_ref[low:high, columns[group]], query, NT)
        grad_weights = mxu(v_ref[low:high, columns[group]], grad, NT)
        return query, grad, scores, grad_weights

    def softmax(unit, query, grad, all_scores, all_grad_weights):
        low, high, at = unit[4:]
        bias = bias_ref[at : at + high - low, :]
        rounded, grad_scores = [], []
        for h in range(UNIT_HEADS):
            part = slice(h * BLOCK, (h + 1) * BLOCK)
            scores = all_scores[:, part] * (scale * LOG2_E) + bias
            grad_weights = all_grad_weights[:, part]
            largest = jnp.max(scores, axis=0, keepdims=True)
            numerator = jnp.exp2(scores - largest)
            weights = numerator * (1.0 / jnp.sum(numerator, axis=0, keepdims=True))
            rounded.append(weights.astype(jnp.bfloat16))
            delta = jnp.sum(rounded[-1].astype(jnp.float32) * grad_weights, axis=0, keepdims=True)
            grad_scores.append((weights * (grad_weights - delta)).astype(jnp.bfloat16))
        return query, grad, jnp.concatenate(rounded, axis=1), jnp.concatenate(grad_scores, axis=1)

    def add(total, terms, low, high):
        for index in range(low // BLOCK, high // BLOCK):
            part = terms[index * BLOCK - low : (index + 1) * BLOCK - low]
            total[index] = part if total[index] is None else total[index] + part

    def gradients(unit, query, grad, rounded, grad_scores):
        group, block, heads, rows, low, high, _ = unit
        grad_query = (mxu(key_t[group][:, low:high], grad_scores, NN) * scale).astype(jnp.bfloat16)
        for h, head in enumerate(heads):
            gq_ref[head, rows] = grad_query[:, h * BLOCK : (h + 1) * BLOCK]
        add(grad_value[group], mxu(rounded, grad, NN), low, high)
        add(grad_key[group], mxu(grad_scores, query, NN), low, high)
        width = GROUP_SHARE * HEAD_SIZE
        if heads[-1].stop == (group + 1) * width:
            done = (slice(group * width, (group + 1) * width), rows)
            copies.append(
                pltpu.make_async_copy(gq_ref.at[done], gq_hbm.at[done], sems.at[len(copies)])
            )
            copies[-1].start()
            if block == len(spans) - 1:
                for index in range(len(spans)):
                    keys = slice(index * BLOCK, (index + 1) * BLOCK)
                    gk_ref[keys, columns[group]] = (grad_key[group][index] * scale).astype(
                        jnp.bfloat16
                    )
                    gv_ref[keys, columns[group]] = grad_value[group][index].astype(jnp.bfloat16)

    ahead, behind = products(units[0]), None
    for index, unit in enumerate(units):
        held = ahead
        if index + 1 < len(units):
            ahead = products(units[index + 1])
        held = softmax(unit, *held)
        if behind is not None:
            gradients(units[index - 1], *behind)
        behind = held
    gradients(units[-1], *behind)
    for copy in copies:
        copy.wait()


def attention_backward(bias, queries, output_gradient, keys, values):
    turned = (queries.shape[1], queries.shape[0])
    chunks = keys.shape[1] // HEAD_SIZE * (queries.shape[0] // BLOCK)
    vmem = pl.BlockSpec(memory_space=pltpu.VMEM)
    return pl.pallas_call(
        attention_kernel,
        in_specs=[vmem] * 5,
        out_specs=[pl.BlockSpec(memory_space=pltpu.HBM), vmem, vmem, vmem],
        out_shape=[
            pltpu.HBM(turned, jnp.bfloat16),
            jax.ShapeDtypeStruct(keys.shape, jnp.bfloat16),
            jax.ShapeDtypeStruct(values.shape, jnp.bfloat16),
            jax.ShapeDtypeStruct(turned, jnp.bfloat16),
        ],
        scratch_shapes=[
            pltpu.SemaphoreType.DMA((chunks,)),
        ],
        compiler_params=pltpu.CompilerParams(vmem_limit_bytes=ATTENTION_VMEM),
        cost_estimate=pl.CostEstimate(
            flops=8 * 10**9, bytes_accessed=8 * 2**20, transcendentals=0
        ),
        name="attention_backward",
    )(bias, queries, output_gradient, keys, values)


def select(wide, mask_ref, rank):
    total = None
    for slot in range(mask_ref.shape[0]):
        part = wide[slot * rank : (slot + 1) * rank] * mask_ref[slot : slot + 1, :]
        total = part if total is None else total + part
    return total


def spread(low, mask_ref):
    return jnp.concatenate(
        [low * mask_ref[slot : slot + 1, :] for slot in range(mask_ref.shape[0])], axis=0
    ).astype(jnp.bfloat16)


def low_kernel(peers, local_slots, mask_ref, x_ref, gq_ref, *refs):
    factors, (out_ref, sent_ref) = refs[:peers], refs[peers:]
    rank = factors[0].shape[0] // (2 * local_slots)
    share = rank * local_slots
    down = jnp.concatenate([ref[:share] for ref in factors], axis=0)
    out_ref[:rank] = select(mxu(down, x_ref[...], NT), mask_ref, rank)
    up = jnp.concatenate([ref[share:] for ref in factors], axis=0)
    total = mxu(up, gq_ref[...], NN)
    out_ref[rank:] = select(total, mask_ref, rank)
    sent_ref[...] = out_ref[...].astype(jnp.bfloat16)


def relayed(peers):
    return [distance for distance in distances(peers)[1:] if distance % 2 and distance > 1]


def product_kernel(peers, local_slots, parts, mask_ref, *refs):
    lows, (x_ref, gq_ref), outs = refs[:parts], refs[parts : parts + 2], refs[parts + 2 :]
    low = lows[0][...]
    for ref in lows[1:]:
        low = low + ref[...].astype(jnp.float32)
    rank = low.shape[0] // 2
    share = rank * local_slots
    low = low.astype(jnp.bfloat16).astype(jnp.float32)
    wide_in, wide_grad = spread(low[:rank], mask_ref), spread(low[rank:], mask_ref)
    up = mxu(wide_in, gq_ref[...], NT) * ADAPTER_SCALE
    down = mxu(wide_grad, x_ref[...], NN) * ADAPTER_SCALE
    place = {distance: index for index, distance in enumerate(distances(peers))}
    rows = {
        distance: slice(index * share, (index + 1) * share) for distance, index in place.items()
    }
    own_ref, near_ref, low_ref, relay_ref, kept_ref, *far_refs = outs
    own_ref[:share], own_ref[share:] = down[rows[0]], up[rows[0]]
    near_ref[:share] = down[rows[1]].astype(jnp.bfloat16)
    near_ref[share:] = up[rows[1]].astype(jnp.bfloat16)
    low_ref[...] = low[rank:].astype(jnp.bfloat16)
    for index, distance in enumerate(relayed(peers)):
        part = slice(index * share, (index + 1) * share)
        relay_ref[part] = up[rows[distance]].astype(jnp.bfloat16)
        kept_ref[part] = up[rows[distance ^ 1]]
    for distance, ref in zip(distances(peers)[1:-1], far_refs):
        ref[...] = down[rows[distance]].astype(jnp.bfloat16)


def input_kernel(peers, local_slots, mask_ref, low_ref, *refs):
    factors, out_ref = refs[:peers], refs[peers]
    rank = low_ref.shape[0]
    wide = spread(low_ref[...].astype(jnp.float32), mask_ref)
    down = jnp.concatenate([ref[: rank * local_slots] for ref in factors], axis=0)
    out_ref[...] = (mxu(wide, down, TN) * ADAPTER_SCALE).astype(jnp.bfloat16)


def call(kernel, arrays, out_shape, flops, name):
    return pl.pallas_call(
        kernel,
        in_specs=[pl.BlockSpec(memory_space=pltpu.VMEM)] * len(arrays),
        out_specs=jax.tree.map(lambda _: pl.BlockSpec(memory_space=pltpu.VMEM), out_shape),
        out_shape=out_shape,
        compiler_params=pltpu.CompilerParams(vmem_limit_bytes=VMEM_BYTES),
        cost_estimate=pl.CostEstimate(flops=flops, bytes_accessed=4 * 2**20, transcendentals=0),
        name=name,
    )(*arrays)


def swap(array, axis, distance):
    size = lax.axis_size(axis)
    return lax.ppermute(array, axis, [(i, i ^ distance) for i in range(size)])


def local(
    normed_input,
    rotated_queries,
    rotated_keys,
    value_rows,
    output_gradient,
    document_length,
    document_adapter,
    adapter_in_slot,
    down_weight,
    up_weight,
):
    row_count, width = normed_input.shape
    local_slots, rank, _ = down_weight.shape
    share = local_slots * rank
    peers, parts = lax.axis_size("dp"), lax.axis_size("tensor")
    own, bias, mask = pack(
        row_count,
        peers,
        document_length,
        document_adapter,
        adapter_in_slot,
        down_weight.reshape(share, width),
        up_weight.reshape(share, width),
    )
    factors = [own] + [swap(own, "dp", distance) for distance in distances(peers)[1:]]
    query_gradient, key_gradient, value_gradient, near = attention_backward(
        bias, rotated_queries, output_gradient, rotated_keys, value_rows
    )
    low, low_sent = call(
        functools.partial(low_kernel, peers, local_slots),
        (
            mask,
            normed_input,
            near,
            *factors,
        ),
        [
            jax.ShapeDtypeStruct((2 * rank, row_count), dtype)
            for dtype in (jnp.float32, jnp.bfloat16)
        ],
        10**9,
        "low",
    )
    lows = [low] + [swap(low_sent, "tensor", distance) for distance in distances(parts)[1:]]
    relays = relayed(peers)
    far = distances(peers)[1:-1]
    own_terms, near_terms, low_grads, relay, kept, *far_terms = call(
        functools.partial(product_kernel, peers, local_slots, parts),
        (mask, *lows, normed_input, query_gradient),
        [
            jax.ShapeDtypeStruct((2 * share, width), jnp.float32),
            jax.ShapeDtypeStruct((2 * share, width), jnp.bfloat16),
            jax.ShapeDtypeStruct((rank, row_count), jnp.bfloat16),
            jax.ShapeDtypeStruct((len(relays) * share, width), jnp.bfloat16),
            jax.ShapeDtypeStruct((len(relays) * share, width), jnp.float32),
        ]
        + [jax.ShapeDtypeStruct((share, width), jnp.bfloat16)] * len(far),
        10**9,
        "product",
    )
    relay = swap(relay, "dp", 1)
    far_terms = [swap(part, "dp", distance) for distance, part in zip(far, far_terms)]
    far_terms[0], near_terms = lax.optimization_barrier((far_terms[0], near_terms))
    near_terms = swap(near_terms, "dp", 1)
    paired = (kept + relay.astype(jnp.float32)).astype(jnp.bfloat16)
    paired = [
        swap(paired[index * share : (index + 1) * share], "dp", distance ^ 1)
        for index, distance in enumerate(relays)
    ]
    input_gradient = call(
        functools.partial(input_kernel, peers, local_slots),
        (mask, low_grads, *factors),
        jax.ShapeDtypeStruct((row_count, width), jnp.bfloat16),
        10**9,
        "input_gradient",
    )
    down_gradient = own_terms[:share] + near_terms[:share].astype(jnp.float32)
    up_gradient = own_terms[share:] + near_terms[share:].astype(jnp.float32)
    for part in far_terms[::-1]:
        down_gradient = down_gradient + part.astype(jnp.float32)
    for part in paired:
        up_gradient = up_gradient + part.astype(jnp.float32)
    down_gradient = down_gradient.reshape(local_slots, rank, width)
    up_gradient = up_gradient.reshape(local_slots, rank, width)
    return (input_gradient, key_gradient, value_gradient, down_gradient, up_gradient)


def solution(mesh):
    return jax.shard_map(
        local,
        mesh=mesh,
        in_specs=(
            P(("groups", "dp"), "tensor"),
            P(("groups", "dp"), "tensor"),
            P(("groups", "dp"), "tensor"),
            P(("groups", "dp"), "tensor"),
            P(("groups", "dp"), "tensor"),
            P(("groups", "dp"), None),
            P(("groups", "dp"), None),
            P(),
            P(("groups", "dp"), None, "tensor"),
            P(("groups", "dp"), None, "tensor"),
        ),
        out_specs=(
            P(("groups", "dp"), "tensor"),
            P(("groups", "dp"), "tensor"),
            P(("groups", "dp"), "tensor"),
            P(("groups", "dp"), None, "tensor"),
            P(("groups", "dp"), None, "tensor"),
        ),
        check_vma=False,
    )
```

```python
import functools
import math

import jax
import jax.numpy as jnp
from jax import lax
from jax.experimental import pallas as pl
from jax.experimental.pallas import tpu as pltpu
from jax.sharding import PartitionSpec as P

QUERY_HEAD_COUNT = 64
KEY_VALUE_HEADS = 8
HEAD_SIZE = 128
GROUP_SHARE = QUERY_HEAD_COUNT // KEY_VALUE_HEADS
DOCUMENT_REACH = 256
BLOCK = 128
UNIT_HEADS = 2

MASKED = -1e30
ADAPTER_SCALE = 2.0
LOG2_E = 1.4426950408889634
ATTENTION_VMEM = 24 * 1024 * 1024
VMEM_BYTES = 16 * 1024 * 1024

NN = (((1,), (0,)), ((), ()))
NT = (((1,), (1,)), ((), ()))
TN = (((0,), (0,)), ((), ()))


def mxu(a, b, dims):
    return lax.dot_general(a, b, dims, preferred_element_type=jnp.float32)


def query_spans(row_count):
    return [
        (at, max(0, (at - (DOCUMENT_REACH - 1)) // BLOCK * BLOCK), at + BLOCK)
        for at in range(0, row_count, BLOCK)
    ]


def distances(size):
    return [0, *range(size - 1, 0, -1)]


def pack_kernel(
    row_count,
    peers,
    len_hbm,
    adapter_hbm,
    slot_hbm,
    down_hbm,
    up_hbm,
    own_ref,
    bias_ref,
    mask_ref,
    len_ref,
    adapter_ref,
    slot_ref,
    sems,
):
    share = down_hbm.shape[0]
    local_slots = slot_hbm.shape[0] // peers
    pairs = (
        (len_hbm, len_ref),
        (adapter_hbm, adapter_ref),
        (slot_hbm, slot_ref),
        (down_hbm, own_ref.at[:share]),
        (up_hbm, own_ref.at[share:]),
    )
    copies = [
        pltpu.make_async_copy(source, target, sems.at[index])
        for index, (source, target) in enumerate(pairs)
    ]
    for copy in copies:
        copy.start()
    for copy in copies[:3]:
        copy.wait()
    lengths = [len_ref[0, index] for index in range(len_ref.shape[1] - 1)]

    token = lax.broadcasted_iota(jnp.int32, (1, row_count), 1)
    adapter = jnp.full((1, row_count), adapter_ref[0, 0], jnp.int32)
    begin = jnp.zeros((1, row_count), jnp.int32)
    end = jnp.int32(0)
    for index, length in enumerate(lengths):
        end = end + length
        adapter = jnp.where(token >= end, adapter_ref[0, index + 1], adapter)
        begin = jnp.where(token >= end, end, begin)
    me = lax.axis_index("dp")
    for place, distance in enumerate(distances(peers)):
        for own in range(local_slots):
            row = place * local_slots + own
            held = slot_ref[(me ^ distance) * local_slots + own]
            mask_ref[row : row + 1, :] = jnp.where(adapter == held, 1.0, 0.0)
    at = 0
    for first, low, high in query_spans(row_count):
        width = high - low
        query = lax.broadcasted_iota(jnp.int32, (1, BLOCK), 1) + first
        start = begin[:, first : first + BLOCK]
        key = lax.broadcasted_iota(jnp.int32, (width, BLOCK), 0) + low
        bias_ref[at : at + width, :] = jnp.where((key >= start) & (key <= query), 0.0, MASKED)
        at += width
    for copy in copies[3:]:
        copy.wait()


def pack(row_count, peers, lengths, adapters, slots, down, up):
    pair_rows = sum(high - low for _, low, high in query_spans(row_count))
    arrays = [
        pltpu.with_memory_space_constraint(array, pltpu.HBM)
        for array in (lengths, adapters, slots, down, up)
    ]
    return pl.pallas_call(
        functools.partial(pack_kernel, row_count, peers),
        in_specs=[pl.BlockSpec(memory_space=pltpu.HBM)] * 5,
        out_specs=[pl.BlockSpec(memory_space=pltpu.VMEM)] * 3,
        out_shape=[
            jax.ShapeDtypeStruct((2 * down.shape[0], down.shape[1]), down.dtype),
            jax.ShapeDtypeStruct((pair_rows, BLOCK), jnp.float32),
            jax.ShapeDtypeStruct((slots.shape[0], row_count), jnp.float32),
        ],
        scratch_shapes=[
            pltpu.SMEM(lengths.shape, jnp.int32),
            pltpu.SMEM(adapters.shape, jnp.int32),
            pltpu.SMEM(slots.shape, jnp.int32),
            pltpu.SemaphoreType.DMA((5,)),
        ],
        compiler_params=pltpu.CompilerParams(vmem_limit_bytes=VMEM_BYTES),
        cost_estimate=pl.CostEstimate(flops=10**10, bytes_accessed=2**20, transcendentals=0),
        name="pack",
    )(*arrays)


def attention_kernel(
    bias_ref, q_ref, g_ref, k_ref, v_ref, gq_hbm, gk_ref, gv_ref, gq_ref, sems
):
    row_count = q_ref.shape[0]
    groups = k_ref.shape[1] // HEAD_SIZE
    scale = 1.0 / math.sqrt(HEAD_SIZE)
    spans = query_spans(row_count)

    units = []
    for group in range(groups):
        at = 0
        for block, (first, low, high) in enumerate(spans):
            for part in range(0, GROUP_SHARE, UNIT_HEADS):
                heads = [
                    slice(h * HEAD_SIZE, (h + 1) * HEAD_SIZE)
                    for h in range(
                        group * GROUP_SHARE + part, group * GROUP_SHARE + part + UNIT_HEADS
                    )
                ]
                units.append((group, block, heads, slice(first, first + BLOCK), low, high, at))
            at += high - low

    columns = [slice(group * HEAD_SIZE, (group + 1) * HEAD_SIZE) for group in range(groups)]
    key_t = [k_ref[:, column].T for column in columns]
    grad_key = [[None] * len(spans) for _ in range(groups)]
    grad_value = [[None] * len(spans) for _ in range(groups)]
    copies = []

    def products(unit):
        group, _, heads, rows, low, high, _ = unit
        query = jnp.concatenate([q_ref[rows, head] for head in heads], axis=0)
        grad = jnp.concatenate([g_ref[rows, head] for head in heads], axis=0)
        scores = mxu(k_ref[low:high, columns[group]], query, NT)
        grad_weights = mxu(v_ref[low:high, columns[group]], grad, NT)
        return query, grad, scores, grad_weights

    def softmax(unit, query, grad, all_scores, all_grad_weights):
        low, high, at = unit[4:]
        bias = bias_ref[at : at + high - low, :]
        rounded, grad_scores = [], []
        for h in range(UNIT_HEADS):
            part = slice(h * BLOCK, (h + 1) * BLOCK)
            scores = all_scores[:, part] * (scale * LOG2_E) + bias
            grad_weights = all_grad_weights[:, part]
            largest = jnp.max(scores, axis=0, keepdims=True)
            numerator = jnp.exp2(scores - largest)
            weights = numerator * (1.0 / jnp.sum(numerator, axis=0, keepdims=True))
            rounded.append(weights.astype(jnp.bfloat16))
            delta = jnp.sum(rounded[-1].astype(jnp.float32) * grad_weights, axis=0, keepdims=True)
            grad_scores.append((weights * (grad_weights - delta)).astype(jnp.bfloat16))
        return query, grad, jnp.concatenate(rounded, axis=1), jnp.concatenate(grad_scores, axis=1)

    def add(total, terms, low, high):
        for index in range(low // BLOCK, high // BLOCK):
            part = terms[index * BLOCK - low : (index + 1) * BLOCK - low]
            total[index] = part if total[index] is None else total[index] + part

    def gradients(unit, query, grad, rounded, grad_scores):
        group, block, heads, rows, low, high, _ = unit
        grad_query = (mxu(key_t[group][:, low:high], grad_scores, NN) * scale).astype(jnp.bfloat16)
        for h, head in enumerate(heads):
            gq_ref[head, rows] = grad_query[:, h * BLOCK : (h + 1) * BLOCK]
        add(grad_value[group], mxu(rounded, grad, NN), low, high)
        add(grad_key[group], mxu(grad_scores, query, NN), low, high)
        width = GROUP_SHARE * HEAD_SIZE
        if heads[-1].stop == (group + 1) * width:
            done = (slice(group * width, (group + 1) * width), rows)
            copies.append(
                pltpu.make_async_copy(gq_ref.at[done], gq_hbm.at[done], sems.at[len(copies)])
            )
            copies[-1].start()
            if block == len(spans) - 1:
                for index in range(len(spans)):
                    keys = slice(index * BLOCK, (index + 1) * BLOCK)
                    gk_ref[keys, columns[group]] = (grad_key[group][index] * scale).astype(
                        jnp.bfloat16
                    )
                    gv_ref[keys, columns[group]] = grad_value[group][index].astype(jnp.bfloat16)

    ahead, behind = products(units[0]), None
    for index, unit in enumerate(units):
        held = ahead
        if index + 1 < len(units):
            ahead = products(units[index + 1])
        held = softmax(unit, *held)
        if behind is not None:
            gradients(units[index - 1], *behind)
        behind = held
    gradients(units[-1], *behind)
    for copy in copies:
        copy.wait()


def attention_backward(bias, queries, output_gradient, keys, values):
    turned = (queries.shape[1], queries.shape[0])
    chunks = keys.shape[1] // HEAD_SIZE * (queries.shape[0] // BLOCK)
    vmem = pl.BlockSpec(memory_space=pltpu.VMEM)
    return pl.pallas_call(
        attention_kernel,
        in_specs=[vmem] * 5,
        out_specs=[pl.BlockSpec(memory_space=pltpu.HBM), vmem, vmem, vmem],
        out_shape=[
            pltpu.HBM(turned, jnp.bfloat16),
            jax.ShapeDtypeStruct(keys.shape, jnp.bfloat16),
            jax.ShapeDtypeStruct(values.shape, jnp.bfloat16),
            jax.ShapeDtypeStruct(turned, jnp.bfloat16),
        ],
        scratch_shapes=[
            pltpu.SemaphoreType.DMA((chunks,)),
        ],
        compiler_params=pltpu.CompilerParams(vmem_limit_bytes=ATTENTION_VMEM),
        cost_estimate=pl.CostEstimate(
            flops=8 * 10**9, bytes_accessed=8 * 2**20, transcendentals=0
        ),
        name="attention_backward",
    )(bias, queries, output_gradient, keys, values)


def select(wide, mask_ref, rank):
    total = None
    for slot in range(mask_ref.shape[0]):
        part = wide[slot * rank : (slot + 1) * rank] * mask_ref[slot : slot + 1, :]
        total = part if total is None else total + part
    return total


def spread(low, mask_ref):
    return jnp.concatenate(
        [low * mask_ref[slot : slot + 1, :] for slot in range(mask_ref.shape[0])], axis=0
    ).astype(jnp.bfloat16)


def low_kernel(peers, local_slots, mask_ref, x_ref, gq_ref, *refs):
    factors, (out_ref, sent_ref) = refs[:peers], refs[peers:]
    rank = factors[0].shape[0] // (2 * local_slots)
    share = rank * local_slots
    down = jnp.concatenate([ref[:share] for ref in factors], axis=0)
    out_ref[:rank] = select(mxu(down, x_ref[...], NT), mask_ref, rank)
    up = jnp.concatenate([ref[share:] for ref in factors], axis=0)
    total = mxu(up, gq_ref[...], NN)
    out_ref[rank:] = select(total, mask_ref, rank)
    sent_ref[...] = out_ref[...].astype(jnp.bfloat16)


def relayed(peers):
    return [distance for distance in distances(peers)[1:] if distance % 2 and distance > 1]


def product_kernel(peers, local_slots, parts, mask_ref, *refs):
    lows, (x_ref, gq_ref), outs = refs[:parts], refs[parts : parts + 2], refs[parts + 2 :]
    low = lows[0][...]
    for ref in lows[1:]:
        low = low + ref[...].astype(jnp.float32)
    rank = low.shape[0] // 2
    share = rank * local_slots
    low = low.astype(jnp.bfloat16).astype(jnp.float32)
    wide_in, wide_grad = spread(low[:rank], mask_ref), spread(low[rank:], mask_ref)
    up = mxu(wide_in, gq_ref[...], NT) * ADAPTER_SCALE
    down = mxu(wide_grad, x_ref[...], NN) * ADAPTER_SCALE
    place = {distance: index for index, distance in enumerate(distances(peers))}
    rows = {
        distance: slice(index * share, (index + 1) * share) for distance, index in place.items()
    }
    own_ref, near_ref, low_ref, relay_ref, kept_ref, *far_refs = outs
    own_ref[:share], own_ref[share:] = down[rows[0]], up[rows[0]]
    near_ref[:share] = down[rows[1]].astype(jnp.bfloat16)
    near_ref[share:] = up[rows[1]].astype(jnp.bfloat16)
    low_ref[...] = low[rank:].astype(jnp.bfloat16)
    for index, distance in enumerate(relayed(peers)):
        part = slice(index * share, (index + 1) * share)
        relay_ref[part] = up[rows[distance]].astype(jnp.bfloat16)
        kept_ref[part] = up[rows[distance ^ 1]]
    for distance, ref in zip(distances(peers)[1:-1], far_refs):
        ref[...] = down[rows[distance]].astype(jnp.bfloat16)


def input_kernel(peers, local_slots, mask_ref, low_ref, *refs):
    factors, out_ref = refs[:peers], refs[peers]
    rank = low_ref.shape[0]
    wide = spread(low_ref[...].astype(jnp.float32), mask_ref)
    down = jnp.concatenate([ref[: rank * local_slots] for ref in factors], axis=0)
    out_ref[...] = (mxu(wide, down, TN) * ADAPTER_SCALE).astype(jnp.bfloat16)


def call(kernel, arrays, out_shape, flops, name):
    return pl.pallas_call(
        kernel,
        in_specs=[pl.BlockSpec(memory_space=pltpu.VMEM)] * len(arrays),
        out_specs=jax.tree.map(lambda _: pl.BlockSpec(memory_space=pltpu.VMEM), out_shape),
        out_shape=out_shape,
        compiler_params=pltpu.CompilerParams(vmem_limit_bytes=VMEM_BYTES),
        cost_estimate=pl.CostEstimate(flops=flops, bytes_accessed=4 * 2**20, transcendentals=0),
        name=name,
    )(*arrays)


def swap(array, axis, distance):
    size = lax.axis_size(axis)
    return lax.ppermute(array, axis, [(i, i ^ distance) for i in range(size)])


def local(
    normed_input,
    rotated_queries,
    rotated_keys,
    value_rows,
    output_gradient,
    document_length,
    document_adapter,
    adapter_in_slot,
    down_weight,
    up_weight,
):
    row_count, width = normed_input.shape
    local_slots, rank, _ = down_weight.shape
    share = local_slots * rank
    peers, parts = lax.axis_size("dp"), lax.axis_size("tensor")
    own, bias, mask = pack(
        row_count,
        peers,
        document_length,
        document_adapter,
        adapter_in_slot,
        down_weight.reshape(share, width),
        up_weight.reshape(share, width),
    )
    factors = [own] + [swap(own, "dp", distance) for distance in distances(peers)[1:]]
    query_gradient, key_gradient, value_gradient, near = attention_backward(
        bias, rotated_queries, output_gradient, rotated_keys, value_rows
    )
    low, low_sent = call(
        functools.partial(low_kernel, peers, local_slots),
        (
            mask,
            normed_input,
            near,
            *factors,
        ),
        [
            jax.ShapeDtypeStruct((2 * rank, row_count), dtype)
            for dtype in (jnp.float32, jnp.bfloat16)
        ],
        10**9,
        "low",
    )
    lows = [low] + [swap(low_sent, "tensor", distance) for distance in distances(parts)[1:]]
    relays = relayed(peers)
    far = distances(peers)[1:-1]
    own_terms, near_terms, low_grads, relay, kept, *far_terms = call(
        functools.partial(product_kernel, peers, local_slots, parts),
        (mask, *lows, normed_input, query_gradient),
        [
            jax.ShapeDtypeStruct((2 * share, width), jnp.float32),
            jax.ShapeDtypeStruct((2 * share, width), jnp.bfloat16),
            jax.ShapeDtypeStruct((rank, row_count), jnp.bfloat16),
            jax.ShapeDtypeStruct((len(relays) * share, width), jnp.bfloat16),
            jax.ShapeDtypeStruct((len(relays) * share, width), jnp.float32),
        ]
        + [jax.ShapeDtypeStruct((share, width), jnp.bfloat16)] * len(far),
        10**9,
        "product",
    )
    relay = swap(relay, "dp", 1)
    far_terms = [swap(part, "dp", distance) for distance, part in zip(far, far_terms)]
    relay, near_terms = lax.optimization_barrier((relay, near_terms))
    near_terms = swap(near_terms, "dp", 1)
    paired = (kept + relay.astype(jnp.float32)).astype(jnp.bfloat16)
    paired = [
        swap(paired[index * share : (index + 1) * share], "dp", distance ^ 1)
        for index, distance in enumerate(relays)
    ]
    input_gradient = call(
        functools.partial(input_kernel, peers, local_slots),
        (mask, low_grads, *factors),
        jax.ShapeDtypeStruct((row_count, width), jnp.bfloat16),
        10**9,
        "input_gradient",
    )
    down_gradient = own_terms[:share] + near_terms[:share].astype(jnp.float32)
    up_gradient = own_terms[share:] + near_terms[share:].astype(jnp.float32)
    for part in far_terms:
        down_gradient = down_gradient + part.astype(jnp.float32)
    for part in paired:
        up_gradient = up_gradient + part.astype(jnp.float32)
    down_gradient = down_gradient.reshape(local_slots, rank, width)
    up_gradient = up_gradient.reshape(local_slots, rank, width)
    return (input_gradient, key_gradient, value_gradient, down_gradient, up_gradient)


def solution(mesh):
    return jax.shard_map(
        local,
        mesh=mesh,
        in_specs=(
            P(("groups", "dp"), "tensor"),
            P(("groups", "dp"), "tensor"),
            P(("groups", "dp"), "tensor"),
            P(("groups", "dp"), "tensor"),
            P(("groups", "dp"), "tensor"),
            P(("groups", "dp"), None),
            P(("groups", "dp"), None),
            P(),
            P(("groups", "dp"), None, "tensor"),
            P(("groups", "dp"), None, "tensor"),
        ),
        out_specs=(
            P(("groups", "dp"), "tensor"),
            P(("groups", "dp"), "tensor"),
            P(("groups", "dp"), "tensor"),
            P(("groups", "dp"), None, "tensor"),
            P(("groups", "dp"), None, "tensor"),
        ),
        check_vma=False,
    )
```
